32 devices in a mesh: dp: 8 (over y, x, core), expert: 4 (over z).
Axes of the slice: x: 2, y: 2, z: 4, core: 2. Of those that a mesh axis runs over, the one named last changes fastest.
Arguments:
- tokens: bfloat16 [2, 8192, 1536], P(None, ('dp', 'expert')), may hold values from -6 to 6
- out_grad: bfloat16 [2, 8192, 1536], P(None, ('dp', 'expert')), may hold values from -6 to 6
- routes: int32 [2, 8192, 8], P(None, ('dp', 'expert')), may hold values from 0 to 39, all different within a row; in each aligned block of 256 rows (0 to 255, 256 to 511, ..., all dimensions but the last counted through in order) at most 64 rows name the same one
- attn_gain: bfloat16 [1536], P('dp'), may hold values from 0.5 to 1.5
- w_query: bfloat16 [1536, 1536], P('dp'), may hold values from -0.21875 to 0.21875
- w_key: bfloat16 [1536, 512], P('dp'), may hold values from -0.21875 to 0.21875
- w_value: bfloat16 [1536, 512], P('dp'), may hold values from -0.15625 to 0.15625
- w_out: bfloat16 [1536, 1536], P('dp'), may hold values from -1.25 to 1.25
- moe_gain: bfloat16 [1536], P('dp'), may hold values from 0.5 to 1.5
- w_router: bfloat16 [1536, 40], P('dp'), may hold values from -0.078125 to 0.078125
- w_gate: bfloat16 [40, 1536, 512], P('expert'), may hold values from -0.15625 to 0.15625
- w_up: bfloat16 [40, 1536, 512], P('expert'), may hold values from -0.15625 to 0.15625
- w_down: bfloat16 [40, 512, 1536], P('expert'), may hold values from -1 to 1
Outputs:
- mixed: bfloat16 [2, 8192, 1536], P(None, ('dp', 'expert'))
- grad_tokens: float32 [2, 8192, 1536], P(None, ('dp', 'expert'))
- grad_attn_gain: float32 [1536], P('dp')
- grad_query: float32 [1536, 1536], P('dp')
- grad_key: float32 [1536, 512], P('dp')
- grad_value: float32 [1536, 512], P('dp')
- grad_out: float32 [1536, 1536], P('dp')
- grad_moe_gain: float32 [1536], P('dp')
- grad_router: float32 [1536, 40], P('dp')
- grad_gate: float32 [40, 1536, 512], P('expert', 'dp')
- grad_up: float32 [40, 1536, 512], P('expert', 'dp')
- grad_down: float32 [40, 512, 1536], P('expert', 'dp')
The draws below stay inside these ranges and needn't reach their ends.
Inputs may be any that keep to these rules, and one draw needn't show every extreme that they name: `routes`: each row names 8 different experts; in each aligned block of 256 rows (one device's tokens of one micro-batch) no expert is named by more than 64 rows, a bound that some block reaches.
All inputs are finite; a program needn't handle non-finite values.
Results may differ from the reference program's by a relative error of at most 0.024.
Values may be sent and summed in bfloat16 or wider, within the bound.
No kernel may reach another device: no remote copies, remote signals or barrier semaphores. Data moves between devices by JAX's collectives and lax.ppermute only.
A program may use at most 576 MiB of HBM per device.

```python
import math
import jax
import jax.numpy as jnp
import numpy as np
from jax import lax

D = 1536
HEADS = 24
KV_HEADS = 8
HEAD = 64
FF = 512
EXPERTS = 40
TOP = 8
BLOCK = 256
SEQ = 1024
CAP = 64
MICRO = 2
QD = 1536
KD = 512
TOKENS_MB = 8192


def shard_levels(rng, dims, shards, low, top_value):
    def one(dim, parts):
        heights = jax.random.uniform(jax.random.fold_in(jax.random.fold_in(rng, 6), dim), (parts,), jnp.float32, low / len(shards), top_value / len(shards))
        return jnp.repeat(jnp.exp(heights), dims[dim] // parts).reshape((-1,) + (1,) * (len(dims) - dim - 1))

    factor_of = one(*shards[0])
    for cut in shards[1:]:
        factor_of = factor_of * one(*cut)
    return factor_of


def shared_out(key, own, number, rows, count, top, reach, skew):
    sequence = jax.random.permutation(key, count)
    crowded, common = portions_of(count, rows * top, reach, skew, True), portions_of(count, rows * top, reach, skew, False)
    places = jnp.arange(count)

    def named(lengths, rotation):
        used = int((lengths > 0).sum())
        fixed = max(1, used // 4)
        shifted = fixed + (places - fixed + rotation * (used - fixed)) % max(1, count - fixed)
        return jnp.zeros((count,), jnp.int32).at[sequence[jnp.where(places < fixed, places, shifted)]].set(jnp.asarray(lengths, jnp.int32))

    lengths = jnp.where(number % 4 == 0, named(crowded, number // 4), named(common, number - number // 4 - 1))
    mixed = jax.random.permutation(jax.random.fold_in(own, 3), count)
    giver, taker = mixed[0:count // 2 * 2:2], mixed[1:count // 2 * 2:2]
    slack = jnp.minimum(lengths[giver] - 1, reach - lengths[taker]) // 2
    slack = jnp.where((giver == sequence[0]) | (taker == sequence[0]) | (lengths[taker] == 0), 0, jnp.maximum(slack, 0))
    shifted = jax.random.randint(jax.random.fold_in(own, 4), (count // 2,), 0, 1 << 20) % (slack + 1)
    lengths = lengths.at[giver].add(-shifted).at[taker].add(shifted)
    members = jnp.searchsorted(jnp.cumsum(lengths), jnp.arange(rows * top), side="right").astype(jnp.int32)
    grid = members.reshape(top, rows).T
    grid = grid[jax.random.permutation(jax.random.fold_in(own, 1), rows)]
    rotation = jax.random.randint(jax.random.fold_in(own, 2), (rows, 1), 0, top)
    return jnp.take_along_axis(grid, (jnp.arange(top)[None, :] + rotation) % top, axis=1)


def portions_of(count, total, limit, slope, full):
    weights = [(1 << 20) // math.isqrt(grade ** slope) + 1 for grade in range(1, count + 1)]
    largest = limit if full else min(limit, max(-(-total // count), total * weights[0] // sum(weights)))
    least = 1 if total - largest >= count - 1 else 0
    counts, spare = [largest] + [least] * (count - 1), total - largest - least * (count - 1)
    while spare > 0:
        candidates = [i for i in range(1, count) if counts[i] < largest] or [i for i in range(1, count) if counts[i] < limit]
        pool, budget = sum([weights[i] for i in candidates]), spare
        for i in candidates:
            more = min(limit - counts[i], max(1, budget * weights[i] // pool), spare)
            counts[i] = counts[i] + more
            spare = spare - more
    return np.array(counts)


def noise(own_key, extent, width, reach, split=(), kind=jnp.bfloat16):
    values = jax.random.normal(own_key, extent, jnp.float32) * width
    if len(split) > 0:
        values = shard_levels(own_key, extent, split, -0.22, 0.18) * values
    return jnp.clip(values, min=-reach, max=reach).astype(kind)


def setup_inputs(seed: int = 0) -> dict:
    key_of = jax.random.split(jax.random.key(seed), 14)
    tokens = noise(key_of[0], (MICRO, TOKENS_MB, D), 1.0, 6.0, ((1, 32),))
    out_grad = noise(key_of[1], (MICRO, TOKENS_MB, D), 1.0, 6.0, ((1, 32),))
    routes_keys = jax.random.split(jax.random.fold_in(key_of[2], 1), MICRO * TOKENS_MB // BLOCK)
    routes_turns = jax.random.permutation(jax.random.fold_in(key_of[2], 3), MICRO * TOKENS_MB // BLOCK)
    routes = jax.vmap(lambda own, number: shared_out(jax.random.fold_in(key_of[2], 2), own, number, BLOCK, EXPERTS, TOP, CAP, 1))(routes_keys, routes_turns).reshape((MICRO, TOKENS_MB, TOP))
    attn_gain = jnp.clip(1.0 + 0.1 * jax.random.normal(key_of[3], (D,), jnp.float32), 0.5, 1.5).astype(jnp.bfloat16)
    w_query = noise(key_of[4], (D, QD), (D // 2) ** -0.5, 0.21875, ((0, 8),))
    w_key = noise(key_of[5], (D, KD), (D // 2) ** -0.5, 0.21875, ((0, 8),))
    w_value = noise(key_of[6], (D, KD), D ** -0.5, 0.15625, ((0, 8),))
    w_out = noise(key_of[7], (QD, D), (max(QD // 64, 1)) ** -0.5, 1.25, ((0, 8),))
    moe_gain = jnp.clip(1.0 + 0.1 * jax.random.normal(key_of[8], (D,), jnp.float32), 0.5, 1.5).astype(jnp.bfloat16)
    w_router = noise(key_of[9], (D, EXPERTS), (4 * D) ** -0.5, 0.078125, ((0, 8),))
    w_gate = noise(key_of[10], (EXPERTS, D, FF), D ** -0.5, 0.15625, ((0, 4),))
    w_up = noise(key_of[11], (EXPERTS, D, FF), D ** -0.5, 0.15625, ((0, 4),))
    w_down = noise(key_of[12], (EXPERTS, FF, D), (max(FF // 16, 1)) ** -0.5, 1.0, ((0, 4),))
    return {"tokens": tokens, "out_grad": out_grad, "routes": routes, "attn_gain": attn_gain, "w_query": w_query, "w_key": w_key, "w_value": w_value, "w_out": w_out, "moe_gain": moe_gain, "w_router": w_router, "w_gate": w_gate, "w_up": w_up, "w_down": w_down}


EPSILON = 1e-06
ROPE_BASE = 10000.0
NEGATIVE = -1e+30

@jax.custom_vjp
def low(v):
    return lax.optimization_barrier(v.astype(jnp.bfloat16)).astype(jnp.float32)

@jax.custom_vjp
def low_back(v):
    return v

def low_keep(v):
    return (low(v), None)

def low_pass(kept, grad):
    return (grad,)

def back_keep(v):
    return (v, None)

def back_low(kept, grad):
    return (low(grad),)
low.defvjp(low_keep, low_pass)
low_back.defvjp(back_keep, back_low)

def matmul(left, right):
    return jnp.dot(left, right, precision=lax.Precision.HIGHEST, preferred_element_type=jnp.float32)

def rotary(length):
    half_size = HEAD // 2
    frequency = ROPE_BASE ** (-jnp.arange(half_size, dtype=jnp.float32) / half_size)
    angle = jnp.arange(length, dtype=jnp.float32)[:, None] * frequency[None, :]
    return (jnp.cos(angle)[:, None, :], jnp.sin(angle)[:, None, :])

def rotate(values, cosine, sine):
    half_size = values.shape[-1] // 2
    first, second = (values[..., :half_size], values[..., half_size:])
    return jnp.concatenate([first * cosine - second * sine, second * cosine + first * sine], axis=-1)

def reference(tokens, out_grad, routes, attn_gain, w_query, w_key, w_value, w_out, moe_gain, w_router, w_gate, w_up, w_down):
    route_flat = routes.reshape(-1, TOP).astype(jnp.int32)
    total_rows = route_flat.shape[0]
    blocks = total_rows // BLOCK
    pair_routes = route_flat.reshape(blocks, BLOCK * TOP)
    onehot = (pair_routes[:, :, None] == jnp.arange(EXPERTS, dtype=jnp.int32)[None, None, :]).astype(jnp.int32)
    earlier = jnp.cumsum(onehot, axis=1) - onehot
    slot_index = lax.optimization_barrier(jnp.sum(earlier * onehot, axis=2)).reshape(total_rows, TOP)
    block_of = jnp.arange(total_rows, dtype=jnp.int32) // BLOCK
    slot_place = block_of[:, None] * CAP + slot_index
    capacity = blocks * CAP
    cosine, sine = rotary(SEQ)
    query_block = jnp.arange(SEQ, dtype=jnp.int32) // BLOCK
    visible = query_block[:, None] >= query_block[None, :]
    repeat = HEADS // KV_HEADS
    score_scale = HEAD ** (-0.5)

    def forward(x_rows, gain_one, query_w, key_w, value_w, out_w, gain_two, router_w, gate_w, up_w, down_w):

        def group_attention(packed):
            query_rows, key_rows, value_rows = packed
            scores = low_back(jnp.einsum('qrd,kd->rqk', query_rows, key_rows, precision=lax.Precision.HIGHEST) * score_scale)
            scores = jnp.where(visible[None], scores, NEGATIVE)
            row_max = lax.optimization_barrier(jnp.max(scores, axis=-1, keepdims=True))
            weights = jnp.exp(scores - row_max)
            row_sum = lax.optimization_barrier(jnp.sum(weights, axis=-1))
            merged = jnp.einsum('rqk,kd->qrd', low(weights), value_rows, precision=lax.Precision.HIGHEST)
            return merged / jnp.transpose(row_sum)[:, :, None]

        def sequence_branch(sequence_rows):
            inverse_rms = lax.rsqrt(lax.optimization_barrier(jnp.mean(sequence_rows * sequence_rows, axis=-1, keepdims=True)) + EPSILON)
            normed = low(sequence_rows * inverse_rms * gain_one)
            query_rows = low_back(matmul(normed, query_w)).reshape(SEQ, HEADS, HEAD)
            key_rows = low_back(matmul(normed, key_w)).reshape(SEQ, KV_HEADS, HEAD)
            value_rows = low(low_back(matmul(normed, value_w))).reshape(SEQ, KV_HEADS, HEAD)
            query_rows = low(rotate(query_rows, cosine, sine)).reshape(SEQ, KV_HEADS, repeat, HEAD)
            key_rows = low(rotate(key_rows, cosine, sine))
            head_out = lax.map(jax.checkpoint(group_attention), (jnp.transpose(query_rows, (1, 0, 2, 3)), jnp.transpose(key_rows, (1, 0, 2)), jnp.transpose(value_rows, (1, 0, 2))))
            merged = jnp.transpose(head_out, (1, 0, 2, 3)).reshape(SEQ, QD)
            merged = low(low_back(merged))
            return low_back(matmul(merged, out_w))
        branch = lax.map(jax.checkpoint(sequence_branch), x_rows.reshape(-1, SEQ, D))
        flat = (x_rows + branch.reshape(x_rows.shape)).reshape(-1, D)
        inverse_two = lax.rsqrt(lax.optimization_barrier(jnp.mean(flat * flat, axis=-1, keepdims=True)) + EPSILON)
        normed_two = low(flat * inverse_two * gain_two)
        logits = low_back(matmul(normed_two, router_w))
        chosen = jnp.take_along_axis(logits, route_flat, axis=1)
        gate_weights = jax.nn.softmax(chosen, axis=-1)

        def expert(running, packed):
            expert_index, gate_matrix, up_matrix, down_matrix = packed
            picked = route_flat == expert_index
            present = jnp.any(picked, axis=1)
            where_to = jnp.where(present, lax.optimization_barrier(jnp.sum(jnp.where(picked, slot_place, 0), axis=1)), capacity)
            gate_share = lax.optimization_barrier(jnp.sum(jnp.where(picked, gate_weights, 0.0), axis=1))
            inbound = low_back(jnp.zeros((capacity, D), jnp.float32).at[where_to].set(normed_two, mode='drop'))
            gate_pre = low_back(matmul(inbound, gate_matrix))
            up_pre = low_back(matmul(inbound, up_matrix))
            active = low(jax.nn.silu(gate_pre) * up_pre)
            result = low(low_back(matmul(active, down_matrix)))
            returned = jnp.take(result, jnp.minimum(where_to, capacity - 1), axis=0)
            return (running + gate_share[:, None] * returned, None)
        mixture, unused = lax.scan(jax.checkpoint(expert), jnp.zeros_like(flat), (jnp.arange(EXPERTS, dtype=jnp.int32), gate_w, up_w, down_w))
        return (flat + mixture).reshape(x_rows.shape)
    primal = (tokens, attn_gain, w_query, w_key, w_value, w_out, moe_gain, w_router, w_gate, w_up, w_down)
    floats = tuple((argument.astype(jnp.float32) for argument in primal))
    result, pullback = jax.vjp(forward, *floats)
    gradients = pullback(out_grad.astype(jnp.float32))
    return (result.astype(jnp.bfloat16), gradients[0], gradients[1], gradients[2], gradients[3], gradients[4], gradients[5], gradients[6], gradients[7], gradients[8], gradients[9], gradients[10])
```

```python
from functools import partial

import jax
import jax.numpy as jnp
from jax import lax
from jax.experimental import pallas as pl
from jax.experimental.pallas import tpu as pltpu
from jax.sharding import PartitionSpec as P

HEADS = 24
KV_HEADS = 8
HEAD = 64
FF = 512
EXPERTS = 40
TOP = 8
BLOCK = 256
SEQ = 1024
CAP = 64
QD = 1536
KD = 512

EPSILON = 1e-06
ROPE_BASE = 10000.0
NEGATIVE = -1e30
LANES = 128
COLUMNS = 256
VMEM_LIMIT = 56 * 2**20

BF = jnp.bfloat16
F32 = jnp.float32


def dense_dot(left, right):
    return jnp.dot(left, right, preferred_element_type=F32)


def left_dot(left, right):
    return lax.dot_general(left, right, (((0,), (0,)), ((), ())), preferred_element_type=F32)


def right_dot(left, right):
    return lax.dot_general(left, right, (((1,), (1,)), ((), ())), preferred_element_type=F32)


def rotary_tables(positions):
    half_size = HEAD // 2
    frequency = ROPE_BASE ** (-jnp.arange(half_size, dtype=F32) / half_size)
    angle = positions.astype(F32)[:, None] * frequency[None, :]
    return (jnp.cos(angle)[:, None, :], jnp.sin(angle)[:, None, :])


def rotate(values, cosine, sine):
    half_size = values.shape[-1] // 2
    first, second = (values[..., :half_size], values[..., half_size:])
    return jnp.concatenate(
        [first * cosine - second * sine, second * cosine + first * sine], axis=-1
    )


def unrotate(grads, cosine, sine):
    half_size = grads.shape[-1] // 2
    first, second = (grads[..., :half_size], grads[..., half_size:])
    return jnp.concatenate(
        [first * cosine + second * sine, second * cosine - first * sine], axis=-1
    )


def params(limit=VMEM_LIMIT):
    return pltpu.CompilerParams(vmem_limit_bytes=limit)


def picks(slot_rows):
    slots = lax.broadcasted_iota(jnp.int32, (CAP, BLOCK), 0).astype(F32)
    one, zero = jnp.float32(1), jnp.float32(0)
    return [jnp.where(slots == slot_rows[e : e + 1, :], one, zero) for e in range(slot_rows.shape[0])]


def dispatch_kernel(slot_ref, rows_ref, out_ref):
    experts = slot_ref.shape[0]
    chosen = jnp.concatenate([p.astype(BF) for p in picks(slot_ref[...])], axis=0)
    for start in range(0, out_ref.shape[2], COLUMNS):
        rows = dense_dot(chosen, rows_ref[:, start : start + COLUMNS])
        out_ref[:, :, start : start + COLUMNS] = rows.astype(BF).reshape(experts, CAP, COLUMNS)


def dispatch(slot_rows, rows, features):
    experts, total = slot_rows.shape
    blocks = total // BLOCK
    return pl.pallas_call(
        dispatch_kernel,
        grid=(blocks,),
        in_specs=[
            pl.BlockSpec((experts, BLOCK), lambda b: (0, b)),
            pl.BlockSpec((BLOCK, features), lambda b: (b, 0)),
        ],
        out_specs=pl.BlockSpec((experts, CAP, features), lambda b: (0, b, 0)),
        out_shape=jax.ShapeDtypeStruct((experts, blocks * CAP, features), BF),
        compiler_params=params(),
        cost_estimate=pl.CostEstimate(
            flops=2 * experts * CAP * total * features,
            bytes_accessed=2 * features * (total + experts * blocks * CAP),
            transcendentals=0,
        ),
        name="dispatch",
    )(slot_rows, rows)


def combine_kernel(slot_ref, slots_ref, *rest):
    out_ref = rest[-1]
    experts, features = slots_ref.shape[0], slots_ref.shape[2]
    chosen = jnp.concatenate([p.astype(BF) for p in picks(slot_ref[...])], axis=0)
    for start in range(0, features, COLUMNS):
        held = slots_ref[:, :, start : start + COLUMNS].reshape(experts * CAP, COLUMNS)
        out_ref[:, start : start + COLUMNS] = left_dot(chosen, held).astype(BF)
    if len(rest) > 1:
        out_ref[:, features:] = rest[0][...]


def combine(slot_rows, slots, extra=None):
    experts, total = slot_rows.shape
    blocks = total // BLOCK
    features = slots.shape[2]
    extras = [] if extra is None else [extra]
    width = features + sum(a.shape[1] for a in extras)
    return pl.pallas_call(
        combine_kernel,
        grid=(blocks,),
        in_specs=[
            pl.BlockSpec((experts, BLOCK), lambda b: (0, b)),
            pl.BlockSpec((experts, CAP, features), lambda b: (0, b, 0)),
            *[pl.BlockSpec((BLOCK, a.shape[1]), lambda b: (b, 0)) for a in extras],
        ],
        out_specs=pl.BlockSpec((BLOCK, width), lambda b: (b, 0)),
        out_shape=jax.ShapeDtypeStruct((total, width), BF),
        compiler_params=params(),
        cost_estimate=pl.CostEstimate(
            flops=2 * experts * CAP * total * features,
            bytes_accessed=2 * features * (total + experts * blocks * CAP),
            transcendentals=0,
        ),
        name="combine",
    )(slot_rows, slots, *extras)


def expert_kernel(
    slot_ref, gate_ref, x_ref, dy_ref, wg_ref, wu_ref, wd_ref,
    ys_ref, dx_ref, gdy_ref, act_ref, dg_ref, du_ref, dgates_ref,
):
    rows = x_ref[0]
    blocks = rows.shape[0] // CAP
    pre = dense_dot(rows, wg_ref[0])
    up = dense_dot(rows, wu_ref[0])
    sigma = 1.0 / (1.0 + jnp.exp(-pre))
    silu = pre * sigma
    active = (silu * up).astype(BF)
    act_ref[0] = active
    chosen = []
    shares = []
    for b in range(blocks):
        where = slice(b * BLOCK, (b + 1) * BLOCK)
        one_hot = picks(slot_ref[0][:, where])[0]
        chosen.append(one_hot)
        shares.append(jnp.sum(one_hot * gate_ref[0][:, where], axis=1, keepdims=True))
    share = jnp.concatenate(shares, axis=0)
    result = dense_dot(active, wd_ref[0])
    grads = dy_ref[0].astype(F32)
    dots = jnp.sum(result * grads, axis=1, keepdims=True)
    ys_ref[0] = (result * share).astype(BF)
    gated = (grads * share).astype(BF)
    gdy_ref[0] = gated
    for b in range(blocks):
        dgates_ref[0, :, b * BLOCK : (b + 1) * BLOCK] = jnp.sum(
            chosen[b] * dots[b * CAP : (b + 1) * CAP], axis=0, keepdims=True
        )
    dact = right_dot(gated, wd_ref[0])
    dpre = (dact * up * sigma * (1.0 + pre * (1.0 - sigma))).astype(BF)
    dup = (dact * silu).astype(BF)
    dg_ref[0] = dpre
    du_ref[0] = dup
    dx_ref[0] = (right_dot(dpre, wg_ref[0]) + right_dot(dup, wu_ref[0])).astype(BF)


def expert_pass(slot_rows, gate_rows, x_slots, dy_slots, w_gate, w_up, w_down):
    experts, total = slot_rows.shape
    _, rows, features = x_slots.shape
    hidden = w_gate.shape[2]
    one = lambda e: (e, 0, 0)
    line = pl.BlockSpec((1, 1, total), one)
    wide = pl.BlockSpec((1, rows, features), one)
    narrow = pl.BlockSpec((1, rows, hidden), one)
    wide_shape = jax.ShapeDtypeStruct((experts, rows, features), BF)
    narrow_shape = jax.ShapeDtypeStruct((experts, rows, hidden), BF)
    outs = pl.pallas_call(
        expert_kernel,
        grid=(experts,),
        in_specs=[
            line, line, wide, wide,
            pl.BlockSpec((1, features, hidden), one),
            pl.BlockSpec((1, features, hidden), one),
            pl.BlockSpec((1, hidden, features), one),
        ],
        out_specs=[wide, wide, wide, narrow, narrow, narrow, line],
        out_shape=[
            wide_shape, wide_shape, wide_shape, narrow_shape, narrow_shape, narrow_shape,
            jax.ShapeDtypeStruct((experts, 1, total), F32),
        ],
        compiler_params=params(),
        cost_estimate=pl.CostEstimate(
            flops=12 * experts * rows * features * hidden,
            bytes_accessed=6 * experts * features * hidden + 10 * experts * rows * features,
            transcendentals=experts * rows * hidden,
        ),
        name="experts",
    )(slot_rows[:, None, :], gate_rows[:, None, :], x_slots, dy_slots, w_gate, w_up, w_down)
    return outs[:-1], outs[-1][:, 0, :]


def weight_kernel(*refs):
    count = (len(refs) - 3) // 5
    ins, (gate_ref, up_ref, down_ref) = refs[: 5 * count], refs[5 * count :]
    xs, gdys, acts, dgs, dus = [ins[i::5] for i in range(5)]
    total = lambda lefts, rights: sum(
        left_dot(left[0], right[0]) for left, right in zip(lefts, rights)
    )
    gate_ref[0] = total(xs, dgs).astype(BF)
    up_ref[0] = total(xs, dus).astype(BF)
    down_ref[0] = total(acts, gdys).astype(BF)


def weight_pass(parts):
    experts, rows, features = parts[0][0].shape
    hidden = parts[0][2].shape[2]
    one = lambda e: (e, 0, 0)
    count = len(parts)
    return pl.pallas_call(
        weight_kernel,
        grid=(experts,),
        in_specs=[
            pl.BlockSpec((1, rows, a.shape[2]), one) for part in parts for a in part
        ],
        out_specs=[
            pl.BlockSpec((1, features, hidden), one),
            pl.BlockSpec((1, features, hidden), one),
            pl.BlockSpec((1, hidden, features), one),
        ],
        out_shape=[
            jax.ShapeDtypeStruct((experts, features, hidden), BF),
            jax.ShapeDtypeStruct((experts, features, hidden), BF),
            jax.ShapeDtypeStruct((experts, hidden, features), BF),
        ],
        compiler_params=params(),
        cost_estimate=pl.CostEstimate(
            flops=6 * count * experts * rows * features * hidden,
            bytes_accessed=6 * experts * features * hidden + 4 * count * experts * rows * (features + hidden),
            transcendentals=0,
        ),
        name="expert_weights",
    )(*[a for part in parts for a in part])


def online_step(carried, query_rows, key_rows, value_rows, score_scale):
    running_max, running_sum, running_out = carried
    scores = (
        jnp.einsum("qgrd,kgd->grqk", query_rows, key_rows, preferred_element_type=F32)
        * score_scale
    )
    new_max = jnp.maximum(running_max, jnp.max(scores, axis=-1))
    factor = jnp.exp(running_max - new_max)
    weights = jnp.exp(scores - new_max[..., None])
    running_sum = running_sum * factor + jnp.sum(weights, axis=-1)
    running_out = running_out * factor[..., None] + jnp.einsum(
        "grqk,kgd->grqd", weights.astype(BF), value_rows, preferred_element_type=F32
    )
    return (new_max, running_sum, running_out)


def keep_state(carried):
    return carried


def attend(query_b, keys, values, first_block, own_rank, score_scale):
    repeat = HEADS // KV_HEADS
    state = (
        jnp.full((KV_HEADS, repeat, BLOCK), NEGATIVE, F32),
        jnp.zeros((KV_HEADS, repeat, BLOCK), F32),
        jnp.zeros((KV_HEADS, repeat, BLOCK, HEAD), F32),
    )
    for index in range(keys.shape[0] // BLOCK):
        rows = slice(index * BLOCK, (index + 1) * BLOCK)
        update = partial(
            online_step,
            query_rows=query_b,
            key_rows=keys[rows].reshape(BLOCK, KV_HEADS, HEAD),
            value_rows=values[rows].reshape(BLOCK, KV_HEADS, HEAD),
            score_scale=score_scale,
        )
        seen = jnp.logical_and(index >= first_block, index <= own_rank)
        state = lax.cond(seen, update, keep_state, state)
    running_max, running_sum, running_out = state
    return running_out / running_sum[..., None], running_max + jnp.log(running_sum)


def attend_back(query_b, grad_attn, row_delta, log_total, keys, values, first_block, own_rank, score_scale):
    repeat = HEADS // KV_HEADS
    count = keys.shape[0] // BLOCK

    def back_block(grad_query, block_index):
        key_rows = lax.dynamic_slice_in_dim(keys, block_index * BLOCK, BLOCK, 0).reshape(BLOCK, KV_HEADS, HEAD)
        value_rows = lax.dynamic_slice_in_dim(values, block_index * BLOCK, BLOCK, 0).reshape(BLOCK, KV_HEADS, HEAD)

        def visible_block(grad_query):
            scores = (
                jnp.einsum("qgrd,kgd->grqk", query_b, key_rows, preferred_element_type=F32)
                * score_scale
            )
            probabilities = jnp.exp(scores - log_total[..., None])
            grad_probs = jnp.einsum("qgrd,kgd->grqk", grad_attn, value_rows, preferred_element_type=F32)
            grad_scores = (probabilities * (grad_probs - row_delta[..., None])).astype(BF)
            grad_query = grad_query + score_scale * jnp.einsum(
                "grqk,kgd->qgrd", grad_scores, key_rows, preferred_element_type=F32
            )
            grad_keys = score_scale * jnp.einsum(
                "grqk,qgrd->kgd", grad_scores, query_b, preferred_element_type=F32
            )
            grad_values = jnp.einsum(
                "grqk,qgrd->kgd", probabilities.astype(BF), grad_attn, preferred_element_type=F32
            )
            return (grad_query, grad_keys.reshape(BLOCK, KD), grad_values.reshape(BLOCK, KD))

        def skipped_block(grad_query):
            zero_rows = jnp.zeros((BLOCK, KD), F32)
            return (grad_query, zero_rows, zero_rows)

        seen = jnp.logical_and(block_index >= first_block, block_index <= own_rank)
        grad_query, grad_keys, grad_values = lax.cond(seen, visible_block, skipped_block, grad_query)
        return (grad_query, (grad_keys, grad_values))

    grad_query, (key_parts, value_parts) = lax.scan(
        back_block,
        jnp.zeros((BLOCK, KV_HEADS, repeat, HEAD), F32),
        jnp.arange(count, dtype=jnp.int32),
    )
    return grad_query, key_parts.reshape(count * BLOCK, KD), value_parts.reshape(count * BLOCK, KD)


def local(
    tokens, out_grad, routes, attn_gain, w_query, w_key, w_value, w_out, moe_gain, w_router,
    w_gate, w_up, w_down,
):
    micros, _, features = tokens.shape
    expert_count = lax.axis_size("expert")
    own_rank = lax.axis_index("expert")
    exp_dev = w_gate.shape[0]
    repeat = HEADS // KV_HEADS
    score_scale = HEAD ** (-0.5)
    seq_blocks = SEQ // BLOCK
    place_in_seq = own_rank % seq_blocks
    first_block = own_rank - place_in_seq
    cosine, sine = rotary_tables(place_in_seq * BLOCK + jnp.arange(BLOCK, dtype=jnp.int32))
    every = lambda a, axis: lax.all_gather(a, axis, axis=0, tiled=True)

    qkv_w = every(jnp.concatenate([w_query, w_key, w_value], axis=1), "dp")
    out_w = every(w_out, "dp")
    router_w = every(w_router, "dp")
    gains = lax.all_gather(jnp.stack([attn_gain, moe_gain]), "dp", axis=1, tiled=True).astype(F32)
    gain_one, gain_two = gains[0:1], gains[1:2]

    route_columns = jnp.pad(routes.astype(BF), ((0, 0), (0, 0), (0, LANES - TOP)))
    dy_sent = jnp.concatenate([out_grad, route_columns], axis=2)
    dy_all = [every(dy_sent[m], "expert") for m in range(micros)]
    experts_row = jnp.arange(EXPERTS, dtype=jnp.int32)
    before = jnp.tril(jnp.ones((BLOCK, BLOCK), F32), -1).astype(BF)

    x_rows = [tokens[m].astype(F32) for m in range(micros)]
    inverse_one = [lax.rsqrt(jnp.mean(x * x, axis=-1, keepdims=True) + EPSILON) for x in x_rows]
    normed = [(x * r * gain_one).astype(BF) for x, r in zip(x_rows, inverse_one)]
    normed_whole = jnp.concatenate(normed, axis=0)
    qkv = dense_dot(normed_whole, qkv_w)

    outputs, grads_x = [], []
    kept = []
    for m in range(micros):
        own = qkv[m * BLOCK : (m + 1) * BLOCK]
        query_b = (
            rotate(own[:, :QD].reshape(BLOCK, HEADS, HEAD), cosine, sine)
            .astype(BF)
            .reshape(BLOCK, KV_HEADS, repeat, HEAD)
        )
        key_b = rotate(own[:, QD : QD + KD].reshape(BLOCK, KV_HEADS, HEAD), cosine, sine).astype(BF)
        kv = jnp.concatenate([key_b.reshape(BLOCK, KD), own[:, QD + KD :].astype(BF)], axis=1)
        kv_all = every(kv, "expert")
        keys, values = kv_all[:, :KD], kv_all[:, KD:]
        out_four, log_total = attend(query_b, keys, values, first_block, own_rank, score_scale)
        out_b = jnp.transpose(out_four, (2, 0, 1, 3)).reshape(BLOCK, QD).astype(BF)
        mid = x_rows[m] + dense_dot(out_b, out_w)
        inverse_two = lax.rsqrt(jnp.mean(mid * mid, axis=-1, keepdims=True) + EPSILON)
        normed_two = (mid * inverse_two * gain_two).astype(BF)
        normed_all = every(normed_two, "expert")
        kept.append((query_b, keys, values, out_four, log_total, out_b, mid, inverse_two, normed_two, normed_all))

    def gate_table(rows, members):
        logits = jnp.where(members, dense_dot(rows, router_w), NEGATIVE)
        weights = jnp.exp(logits - jnp.max(logits, axis=-1, keepdims=True))
        return weights / jnp.sum(weights, axis=-1, keepdims=True)

    def membership(route_rows):
        return jnp.any(route_rows[:, :, None] == experts_row[None, None, :], axis=1)

    expert_parts = []
    sent = []
    for m in range(micros):
        normed_all = kept[m][-1]
        all_routes = dy_all[m][:, features : features + TOP].astype(jnp.int32)
        members = membership(all_routes)
        blocks = members.reshape(expert_count, BLOCK, EXPERTS)
        slots = jnp.einsum("ts,bse->bte", before, blocks.astype(BF), preferred_element_type=F32)
        slots = jnp.where(blocks, slots, -1.0).reshape(-1, EXPERTS)
        mine = lambda table: lax.dynamic_slice_in_dim(table, own_rank * exp_dev, exp_dev, 1).T
        slot_rows = mine(slots)
        gate_rows = mine(gate_table(normed_all, members))
        dy_slots = dispatch(slot_rows, dy_all[m], features)
        x_slots = dispatch(slot_rows, normed_all, features)
        (ys, dx, gdy, act, dg, du), dgates = expert_pass(
            slot_rows, gate_rows, x_slots, dy_slots, w_gate, w_up, w_down
        )
        expert_parts.append((x_slots, gdy, act, dg, du))
        table = lax.dynamic_update_slice_in_dim(
            jnp.zeros((EXPERTS, dgates.shape[1]), F32), dgates, own_rank * exp_dev, 0
        ).T
        high = table.astype(BF)
        low = (table - high.astype(F32)).astype(BF)
        extra = jnp.concatenate(
            [high, low, jnp.zeros((table.shape[0], LANES - 2 * EXPERTS), BF)], axis=1
        )
        scatter = lambda a: lax.psum_scatter(a, "expert", scatter_dimension=0, tiled=True)
        dx_home = scatter(combine(slot_rows, dx, extra))
        mixture = scatter(combine(slot_rows, ys))
        sent.append((dx_home, mixture))

    new_gate, new_up, new_down = weight_pass(expert_parts)
    scatter_dp = lambda a, axis: lax.psum_scatter(a, "dp", scatter_dimension=axis, tiled=True)
    out_gate = scatter_dp(new_gate, 1).astype(F32)
    out_up = scatter_dp(new_up, 1).astype(F32)
    out_down = scatter_dp(new_down, 1).astype(F32)

    router_grads, gain_two_grads, gain_one_grads = [], [], []
    branches, grad_qkvs = [], []
    for m in range(micros):
        query_b, keys, values, out_four, log_total, out_b, mid, inverse_two, normed_two, _ = kept[m]
        dx_home, mixture = sent[m]
        outputs.append((mid + mixture.astype(F32)).astype(BF))
        grad_y = out_grad[m].astype(F32)
        members = membership(routes[m])
        gates = gate_table(normed_two, members)
        high = dx_home[:, features : features + EXPERTS].astype(F32)
        low = dx_home[:, features + EXPERTS : features + 2 * EXPERTS].astype(F32)
        dgates = high + low
        grad_chosen = gates * (dgates - jnp.sum(gates * dgates, axis=-1, keepdims=True))
        grad_logits = jnp.where(members, grad_chosen, 0.0).astype(BF)
        router_grads.append(left_dot(normed_two, grad_logits))
        grad_normed_two = dx_home[:, :features].astype(F32) + right_dot(grad_logits, router_w)
        gain_two_grads.append(jnp.sum(grad_normed_two * mid * inverse_two, axis=0))
        scaled_two = grad_normed_two * gain_two
        grad_mid = (
            grad_y
            + inverse_two * scaled_two
            - mid * inverse_two**3 * jnp.mean(scaled_two * mid, axis=-1, keepdims=True)
        )
        grad_branch = grad_mid.astype(BF)
        branches.append(grad_branch)
        grad_attn = right_dot(grad_branch, out_w).astype(BF).reshape(BLOCK, KV_HEADS, repeat, HEAD)
        row_delta = jnp.sum(jnp.transpose(grad_attn, (1, 2, 0, 3)) * out_four, axis=-1)
        grad_query, key_parts, value_parts = attend_back(
            query_b, grad_attn, row_delta, log_total, keys, values, first_block, own_rank, score_scale
        )
        own_kv = lax.psum_scatter(
            jnp.concatenate([key_parts, value_parts], axis=1).astype(BF),
            "expert", scatter_dimension=0, tiled=True,
        )
        grad_key_b = (
            unrotate(own_kv[:, :KD].astype(F32).reshape(BLOCK, KV_HEADS, HEAD), cosine, sine)
            .astype(BF)
            .reshape(BLOCK, KD)
        )
        grad_query_b = (
            unrotate(grad_query.reshape(BLOCK, HEADS, HEAD), cosine, sine).astype(BF).reshape(BLOCK, QD)
        )
        grad_qkv = jnp.concatenate([grad_query_b, grad_key_b, own_kv[:, KD:]], axis=1)
        grad_qkvs.append(grad_qkv)
        grad_normed = right_dot(grad_qkv, qkv_w)
        gain_one_grads.append(jnp.sum(grad_normed * x_rows[m] * inverse_one[m], axis=0))
        scaled_one = grad_normed * gain_one
        grads_x.append(
            grad_mid
            + inverse_one[m] * scaled_one
            - x_rows[m] * inverse_one[m] ** 3 * jnp.mean(scaled_one * x_rows[m], axis=-1, keepdims=True)
        )

    total = lambda a: lax.psum(a, "expert").astype(F32)
    new_out = left_dot(
        jnp.concatenate([k[5] for k in kept], axis=0), jnp.concatenate(branches, axis=0)
    )
    grad_out = total(scatter_dp(new_out.astype(BF), 0))
    new_qkv = left_dot(normed_whole, jnp.concatenate(grad_qkvs, axis=0))
    qkv_sum = total(scatter_dp(new_qkv.astype(BF), 0))
    small = jnp.concatenate(
        [sum(router_grads), sum(gain_one_grads)[:, None], sum(gain_two_grads)[:, None]], axis=1
    )
    small_sum = total(scatter_dp(small.astype(BF), 0))
    return (
        jnp.stack(outputs),
        jnp.stack(grads_x),
        small_sum[:, EXPERTS],
        qkv_sum[:, :QD],
        qkv_sum[:, QD : QD + KD],
        qkv_sum[:, QD + KD :],
        grad_out,
        small_sum[:, EXPERTS + 1],
        small_sum[:, :EXPERTS],
        out_gate,
        out_up,
        out_down,
    )


def solution(mesh):
    rows = P(None, ("dp", "expert"), None)
    return jax.shard_map(
        local,
        mesh=mesh,
        in_specs=(
            rows, rows, rows, P("dp"), P("dp", None), P("dp", None), P("dp", None), P("dp", None),
            P("dp"), P("dp", None),
            P("expert", None, None), P("expert", None, None), P("expert", None, None),
        ),
        out_specs=(
            rows, rows, P("dp"), P("dp", None), P("dp", None), P("dp", None), P("dp", None),
            P("dp"), P("dp", None),
            P("expert", "dp", None), P("expert", "dp", None), P("expert", "dp", None),
        ),
        check_vma=False,
    )
```

```python
from functools import partial

import jax
import jax.numpy as jnp
from jax import lax
from jax.experimental import pallas as pl
from jax.experimental.pallas import tpu as pltpu
from jax.sharding import PartitionSpec as P

HEADS = 24
KV_HEADS = 8
HEAD = 64
FF = 512
EXPERTS = 40
TOP = 8
BLOCK = 256
SEQ = 1024
CAP = 64
QD = 1536
KD = 512

EPSILON = 1e-06
ROPE_BASE = 10000.0
NEGATIVE = -1e30
LANES = 128
COLUMNS = 256
VMEM_LIMIT = 56 * 2**20

BF = jnp.bfloat16
F32 = jnp.float32


def dense_dot(left, right):
    return jnp.dot(left, right, preferred_element_type=F32)


def left_dot(left, right):
    return lax.dot_general(left, right, (((0,), (0,)), ((), ())), preferred_element_type=F32)


def right_dot(left, right):
    return lax.dot_general(left, right, (((1,), (1,)), ((), ())), preferred_element_type=F32)


def rotary_tables(positions):
    half_size = HEAD // 2
    frequency = ROPE_BASE ** (-jnp.arange(half_size, dtype=F32) / half_size)
    angle = positions.astype(F32)[:, None] * frequency[None, :]
    cosine, sine = jnp.cos(angle), jnp.sin(angle)
    tiles = LANES // HEAD
    return (
        jnp.concatenate([cosine, cosine] * tiles, axis=1),
        jnp.concatenate([-sine, sine] * tiles, axis=1),
    )


def params(limit=VMEM_LIMIT):
    return pltpu.CompilerParams(vmem_limit_bytes=limit)


def swap_halves(values):
    lane = lax.broadcasted_iota(jnp.int32, values.shape, 1)
    half = HEAD // 2
    return jnp.where(
        lane % HEAD < half,
        pltpu.roll(values, LANES - half, 1),
        pltpu.roll(values, half, 1),
    )


def turn(values, cosine, sine):
    return values * cosine + swap_halves(values) * sine


def norm_kernel(x_ref, gain_ref, normed_ref, scale_ref):
    rows = x_ref[...].astype(F32)
    scale = lax.rsqrt(jnp.mean(rows * rows, axis=1, keepdims=True) + EPSILON)
    scale_ref[...] = scale
    normed_ref[...] = (rows * scale * gain_ref[...]).astype(BF)


def norm_rows(x, gain):
    total, features = x.shape
    return pl.pallas_call(
        norm_kernel,
        grid=(total // BLOCK,),
        in_specs=[
            pl.BlockSpec((BLOCK, features), lambda i: (i, 0)),
            pl.BlockSpec((1, features), lambda i: (0, 0)),
        ],
        out_specs=[
            pl.BlockSpec((BLOCK, features), lambda i: (i, 0)),
            pl.BlockSpec((BLOCK, 1), lambda i: (i, 0)),
        ],
        out_shape=[
            jax.ShapeDtypeStruct((total, features), BF),
            jax.ShapeDtypeStruct((total, 1), F32),
        ],
        compiler_params=params(),
        cost_estimate=pl.CostEstimate(flops=5 * total * features, bytes_accessed=4 * total * features, transcendentals=0),
        name="norm",
    )(x, gain)


def project_kernel(turned, normed_ref, w_ref, cosine_ref, sine_ref, *outs):
    tile = w_ref.shape[1]
    rows = dense_dot(normed_ref[...], w_ref[...])

    def write(turning):
        for start in range(0, tile, LANES):
            for m, out_ref in enumerate(outs):
                part = rows[m * BLOCK : (m + 1) * BLOCK, start : start + LANES]
                if turning:
                    part = turn(part, cosine_ref[...], sine_ref[...])
                out_ref[:, start : start + LANES] = part.astype(BF)

    pl.when(pl.program_id(0) < turned)(lambda: write(True))
    pl.when(pl.program_id(0) >= turned)(lambda: write(False))


def project(normed, weight, columns, turned_columns, cosine, sine):
    total, features = normed.shape
    tile = 2 * COLUMNS
    micros = total // BLOCK
    return pl.pallas_call(
        partial(project_kernel, turned_columns // tile),
        grid=(columns // tile,),
        in_specs=[
            pl.BlockSpec((total, features), lambda j: (0, 0)),
            pl.BlockSpec((features, tile), lambda j: (0, j)),
            pl.BlockSpec((BLOCK, LANES), lambda j: (0, 0)),
            pl.BlockSpec((BLOCK, LANES), lambda j: (0, 0)),
        ],
        out_specs=[pl.BlockSpec((BLOCK, tile), lambda j: (0, j))] * micros,
        out_shape=[jax.ShapeDtypeStruct((BLOCK, columns), BF)] * micros,
        compiler_params=params(),
        cost_estimate=pl.CostEstimate(
            flops=2 * total * features * columns,
            bytes_accessed=2 * (features * columns + total * (features + columns)),
            transcendentals=0,
        ),
        name="project",
    )(normed, weight, cosine, sine)


def outward_kernel(ob_ref, w_ref, x_ref, gain_ref, router_ref, routes_ref, mid_ref, sent_ref, scale_ref, gates_ref):
    j = pl.program_id(0)
    tile = w_ref.shape[1]
    features = mid_ref.shape[1]
    where = pl.ds(pl.multiple_of(j * tile, tile), tile)
    mid_ref[:, where] = x_ref[:, where].astype(F32) + dense_dot(ob_ref[...], w_ref[...])

    @pl.when(j == pl.num_programs(0) - 1)
    def _():
        mid = mid_ref[...]
        scale = lax.rsqrt(jnp.mean(mid * mid, axis=1, keepdims=True) + EPSILON)
        scale_ref[...] = scale
        normed = (mid * scale * gain_ref[...]).astype(BF)
        sent_ref[:, :features] = normed
        lane = lax.broadcasted_iota(jnp.int32, (BLOCK, LANES), 1)
        routes = routes_ref[...]
        member = lane == routes[:, 0:1]
        for k in range(1, TOP):
            member = jnp.logical_or(member, lane == routes[:, k : k + 1])
        logits = jnp.where(member, dense_dot(normed, router_ref[...]), NEGATIVE)
        weights = jnp.exp(logits - jnp.max(logits, axis=1, keepdims=True))
        weights = jnp.where(member, weights, 0.0)
        gates = weights / jnp.sum(weights, axis=1, keepdims=True)
        gates_ref[...] = gates
        high = gates.astype(BF).astype(F32)
        sent_ref[:, features:] = (high + pltpu.roll(gates - high, EXPERTS, 1)).astype(BF)


def outward(ob, w_qo, x, gain, router, routes):
    features = x.shape[1]
    tile = 2 * COLUMNS
    whole = lambda a: pl.BlockSpec(a.shape, lambda j: (0, 0))
    fixed = lambda *shape: pl.BlockSpec(shape, lambda j: (0, 0))
    return pl.pallas_call(
        outward_kernel,
        grid=(features // tile,),
        in_specs=[
            whole(ob),
            pl.BlockSpec((QD, tile), lambda j: (0, QD // tile + j)),
            whole(x), whole(gain), whole(router), whole(routes),
        ],
        out_specs=[fixed(BLOCK, features), fixed(BLOCK, features + LANES), fixed(BLOCK, 1), fixed(BLOCK, LANES)],
        out_shape=[
            jax.ShapeDtypeStruct((BLOCK, features), F32),
            jax.ShapeDtypeStruct((BLOCK, features + LANES), BF),
            jax.ShapeDtypeStruct((BLOCK, 1), F32),
            jax.ShapeDtypeStruct((BLOCK, LANES), F32),
        ],
        compiler_params=params(),
        cost_estimate=pl.CostEstimate(
            flops=2 * BLOCK * features * QD, bytes_accessed=2 * features * QD + 14 * BLOCK * features, transcendentals=0
        ),
        name="outward",
    )(ob, w_qo, x, gain, router, routes)


def home_kernel(
    dx_ref, gates_ref, mid_ref, scale_ref, dy_ref, router_ref, gain_ref, w_ref,
    dmid_ref, da_ref, dob_ref, dlog_ref, dgain_ref,
):
    j = pl.program_id(0)
    features = mid_ref.shape[1]
    tile = w_ref.shape[0]

    @pl.when(j == 0)
    def _():
        table = dx_ref[:, features:].astype(F32)
        dgates = table + pltpu.roll(table, LANES - EXPERTS, 1)
        gates = gates_ref[...]
        dc = gates * (dgates - jnp.sum(gates * dgates, axis=1, keepdims=True))
        dlog = dc.astype(BF)
        dlog_ref[...] = dlog
        dnormed = dx_ref[:, :features].astype(F32) + right_dot(dlog, router_ref[...])
        mid = mid_ref[...]
        scale = scale_ref[...]
        dgain_ref[...] = jnp.sum(dnormed * mid * scale, axis=0, keepdims=True)
        scaled = dnormed * gain_ref[...]
        mean = jnp.mean(scaled * mid, axis=1, keepdims=True)
        dmid = dy_ref[...].astype(F32) + scale * scaled - mid * (scale * scale * scale * mean)
        dmid_ref[...] = dmid
        da_ref[...] = dmid.astype(BF)

    where = pl.ds(pl.multiple_of(j * tile, tile), tile)
    dob_ref[:, where] = right_dot(da_ref[...], w_ref[...]).astype(BF)


def home_back(dx, gates, mid, scale, dy, router, gain, w_qo):
    features = mid.shape[1]
    tile = 2 * COLUMNS
    whole = lambda a: pl.BlockSpec(a.shape, lambda j: (0, 0))
    fixed = lambda *shape: pl.BlockSpec(shape, lambda j: (0, 0))
    return pl.pallas_call(
        home_kernel,
        grid=(QD // tile,),
        in_specs=[
            whole(dx), whole(gates), whole(mid), whole(scale), whole(dy), whole(router), whole(gain),
            pl.BlockSpec((tile, features), lambda j: (j, 1)),
        ],
        out_specs=[
            fixed(BLOCK, features), fixed(BLOCK, features), fixed(BLOCK, QD), fixed(BLOCK, LANES), fixed(1, features),
        ],
        out_shape=[
            jax.ShapeDtypeStruct((BLOCK, features), F32),
            jax.ShapeDtypeStruct((BLOCK, features), BF),
            jax.ShapeDtypeStruct((BLOCK, QD), BF),
            jax.ShapeDtypeStruct((BLOCK, LANES), BF),
            jax.ShapeDtypeStruct((1, features), F32),
        ],
        compiler_params=params(),
        cost_estimate=pl.CostEstimate(
            flops=2 * BLOCK * features * QD, bytes_accessed=2 * features * QD + 18 * BLOCK * features, transcendentals=0
        ),
        name="home_back",
    )(dx, gates, mid, scale, dy, router, gain, w_qo)


def last_kernel(
    dq_ref, dkv_ref, cosine_ref, sine_ref, wq_ref, wkv_ref, x_ref, scale_ref, gain_ref, dmid_ref,
    dx_ref, dkvb_ref, dgain_ref,
):
    j = pl.program_id(0)
    tile = wq_ref.shape[0]

    @pl.when(j == 0)
    def _():
        for start in range(0, KD, LANES):
            part = dkv_ref[0, :, start : start + LANES].astype(F32)
            dkvb_ref[:, start : start + LANES] = turn(part, cosine_ref[...], -sine_ref[...]).astype(BF)
        dkvb_ref[:, KD:] = dkv_ref[1]

    where = pl.ds(pl.multiple_of(j * tile, tile), tile)
    dx_ref[:, where] = right_dot(dq_ref[...], wq_ref[...]) + right_dot(dkvb_ref[...], wkv_ref[...])

    @pl.when(j == pl.num_programs(0) - 1)
    def _():
        dnormed = dx_ref[...]
        rows = x_ref[...].astype(F32)
        scale = scale_ref[...]
        dgain_ref[...] = jnp.sum(dnormed * rows * scale, axis=0, keepdims=True)
        scaled = dnormed * gain_ref[...]
        mean = jnp.mean(scaled * rows, axis=1, keepdims=True)
        dx_ref[...] = dmid_ref[...] + scale * scaled - rows * (scale * scale * scale * mean)


def last_back(dq, dkv, cosine, sine, w_q, w_kv, x, scale, gain, dmid):
    features = x.shape[1]
    tile = 2 * COLUMNS
    whole = lambda a: pl.BlockSpec(a.shape, lambda j: (0,) * a.ndim)
    fixed = lambda *shape: pl.BlockSpec(shape, lambda j: (0, 0))
    return pl.pallas_call(
        last_kernel,
        grid=(features // tile,),
        in_specs=[
            whole(dq), whole(dkv), whole(cosine), whole(sine),
            pl.BlockSpec((tile, QD), lambda j: (j, 0)),
            pl.BlockSpec((tile, 2 * KD), lambda j: (j, 0)),
            whole(x), whole(scale), whole(gain), whole(dmid),
        ],
        out_specs=[fixed(BLOCK, features), fixed(BLOCK, 2 * KD), fixed(1, features)],
        out_shape=[
            jax.ShapeDtypeStruct((BLOCK, features), F32),
            jax.ShapeDtypeStruct((BLOCK, 2 * KD), BF),
            jax.ShapeDtypeStruct((1, features), F32),
        ],
        compiler_params=params(),
        cost_estimate=pl.CostEstimate(
            flops=2 * BLOCK * features * (QD + 2 * KD),
            bytes_accessed=2 * features * (QD + 2 * KD) + 16 * BLOCK * features,
            transcendentals=0,
        ),
        name="last_back",
    )(dq, dkv, cosine, sine, w_q, w_kv, x, scale, gain, dmid)


def halves(core_ref, held_ref, step, keep_ref, send_ref):
    core = core_ref[0]
    for q in range(held_ref.shape[0] // (2 * step)):
        mine = pl.multiple_of((2 * q + core) * step, step)
        other = pl.multiple_of((2 * q + 1 - core) * step, step)
        keep_ref[q * step : (q + 1) * step, :] = held_ref[pl.ds(mine, step), :]
        send_ref[q * step : (q + 1) * step, :] = held_ref[pl.ds(other, step), :]


def dense_kernel(micros, step, core_ref, *refs):
    ins, (gains_ref, keep_ref, send_ref, held_ref) = refs[: 7 * micros], refs[7 * micros :]
    normed, dq, dkv, sent, dlog, ob, da = (ins[i * micros : (i + 1) * micros] for i in range(7))

    def total(lefts, rights):
        return sum(left_dot(left[...], right[...]) for left, right in zip(lefts, rights))

    start = 0
    for lefts, rights in ((normed, dq), (normed, dkv), (sent, dlog), (ob, da)):
        width = rights[0].shape[1]
        part = total(lefts, rights)
        if rights is dlog:
            part = part + gains_ref[...]
        held_ref[:, start : start + width] = part.astype(BF)
        start += width
    halves(core_ref, held_ref, step, keep_ref, send_ref)


def dense_grads(core, step, normed, dq, dkv, sent, dlog, ob, da, gains):
    groups = (normed, dq, dkv, sent, dlog, ob, da)
    micros = len(dq)
    tile = max(3 * LANES, 2 * step)
    lefts = (True, False, False, True, False, True, False)
    width = sum(group[0].shape[1] for group, left in zip(groups, lefts) if not left)
    specs = []
    for group, left in zip(groups, lefts):
        for m, a in enumerate(group):
            if left:
                block = m if a.shape[0] > BLOCK else 0
                specs.append(pl.BlockSpec((BLOCK, tile), lambda j, s, block=block: (block, j)))
            else:
                specs.append(pl.BlockSpec(a.shape, lambda j, s: (0, 0)))
    half = jax.ShapeDtypeStruct((QD // 2, width), BF)
    return pl.pallas_call(
        partial(dense_kernel, micros, step),
        grid_spec=pltpu.PrefetchScalarGridSpec(
            num_scalar_prefetch=1,
            grid=(QD // tile,),
            in_specs=[*specs, pl.BlockSpec((tile, gains.shape[1]), lambda j, s: (j, 0))],
            out_specs=[pl.BlockSpec((tile // 2, width), lambda j, s: (j, 0))] * 2,
            scratch_shapes=[pltpu.VMEM((tile, width), BF)],
        ),
        out_shape=[half, half],
        compiler_params=params(),
        cost_estimate=pl.CostEstimate(
            flops=2 * micros * BLOCK * QD * width,
            bytes_accessed=2 * QD * width + 4 * micros * BLOCK * (QD + width),
            transcendentals=0,
        ),
        name="dense_grads",
    )(core, *[a for group in groups for a in group], gains)


PAIR = 2 * HEAD
GROUP = HEADS // KV_HEADS * PAIR


def spread(values):
    lane = lax.broadcasted_iota(jnp.int32, (BLOCK, LANES), 1)
    first = lane < HEAD
    zero = jnp.zeros((BLOCK, LANES), F32)
    one, two, three = (values[:, i * LANES : (i + 1) * LANES] for i in range(3))
    return jnp.concatenate(
        [
            jnp.where(first, one, zero),
            jnp.where(first, pltpu.roll(one, HEAD, 1), zero),
            jnp.where(first, two, zero),
            jnp.where(first, zero, two),
            jnp.where(first, zero, pltpu.roll(three, HEAD, 1)),
            jnp.where(first, zero, three),
        ],
        axis=0,
    )


def gather_heads(rows):
    lane = lax.broadcasted_iota(jnp.int32, (BLOCK, LANES), 1)
    first = lane < HEAD
    part = [rows[i * BLOCK : (i + 1) * BLOCK] for i in range(6)]
    return (
        jnp.where(first, part[0], pltpu.roll(part[1], HEAD, 1)),
        jnp.where(first, part[2], part[3]),
        jnp.where(first, pltpu.roll(part[4], HEAD, 1), part[5]),
    )


def attend_kernel(place_ref, q_ref, *refs):
    blocks = SEQ // BLOCK
    keys, values = refs[:blocks], refs[blocks : 2 * blocks]
    o_ref, ob_ref, lse_ref, max_ref, sum_ref, acc_ref = refs[2 * blocks :]
    query = spread(q_ref[...].astype(F32) * HEAD ** (-0.5)).astype(BF)
    for r in range(blocks):

        @pl.when(place_ref[0] >= r)
        def _():
            scores = right_dot(keys[r][...], query)
            top = jnp.max(scores, axis=0, keepdims=True)
            if r > 0:
                before = max_ref[...]
                top = jnp.maximum(top, before)
            weights = jnp.exp(scores - top)
            total = jnp.sum(weights, axis=0, keepdims=True)
            out = left_dot(values[r][...], weights.astype(BF))
            if r > 0:
                factor = jnp.exp(before - top)
                total = total + sum_ref[...] * factor
                out = out + acc_ref[...] * factor
            max_ref[...] = top
            sum_ref[...] = total
            acc_ref[...] = out

    lse_ref[0] = max_ref[...] + jnp.log(sum_ref[...])
    rows = jnp.transpose(acc_ref[...] / sum_ref[...])
    for i, part in enumerate(gather_heads(rows)):
        o_ref[:, i * LANES : (i + 1) * LANES] = part
        ob_ref[:, i * LANES : (i + 1) * LANES] = part.astype(BF)


def attend(place, query, kvs):
    pairs = KV_HEADS // 2
    rows = 6 * BLOCK
    return pl.pallas_call(
        attend_kernel,
        grid_spec=pltpu.PrefetchScalarGridSpec(
            num_scalar_prefetch=1,
            grid=(pairs,),
            in_specs=[
                pl.BlockSpec((BLOCK, GROUP), lambda p, s: (0, p)),
                *[pl.BlockSpec((BLOCK, PAIR), lambda p, s: (0, p)) for _ in kvs],
                *[pl.BlockSpec((BLOCK, PAIR), lambda p, s: (0, KV_HEADS // 2 + p)) for _ in kvs],
            ],
            out_specs=[
                pl.BlockSpec((BLOCK, GROUP), lambda p, s: (0, p)),
                pl.BlockSpec((BLOCK, GROUP), lambda p, s: (0, p)),
                pl.BlockSpec((1, 1, rows), lambda p, s: (p, 0, 0)),
            ],
            scratch_shapes=[
                pltpu.VMEM((1, rows), F32),
                pltpu.VMEM((1, rows), F32),
                pltpu.VMEM((PAIR, rows), F32),
            ],
        ),
        out_shape=[
            jax.ShapeDtypeStruct((BLOCK, QD), F32),
            jax.ShapeDtypeStruct((BLOCK, QD), BF),
            jax.ShapeDtypeStruct((pairs, 1, rows), F32),
        ],
        compiler_params=params(),
        cost_estimate=pl.CostEstimate(
            flops=8 * SEQ * BLOCK * HEADS * PAIR, bytes_accessed=10 * BLOCK * QD, transcendentals=SEQ * BLOCK * HEADS
        ),
        name="attend",
    )(place, query, *kvs, *kvs)


def attend_back_kernel(place_ref, q_ref, dob_ref, o_ref, lse_ref, cosine_ref, sine_ref, *refs):
    blocks = SEQ // BLOCK
    keys, values = refs[:blocks], refs[blocks : 2 * blocks]
    dq_ref, outs, acc_ref = refs[2 * blocks], refs[2 * blocks + 1 : 3 * blocks + 1], refs[-1]
    query = spread(q_ref[...].astype(F32) * HEAD ** (-0.5)).astype(BF)
    grads = spread(dob_ref[...].astype(F32))
    delta = jnp.sum(jnp.transpose(grads * spread(o_ref[...])), axis=0, keepdims=True)
    grads = grads.astype(BF)
    for r in range(blocks):

        @pl.when(place_ref[0] >= r)
        def _():
            key = keys[r][...]
            weights = jnp.exp(right_dot(key, query) - lse_ref[0])
            dscores = (weights * (right_dot(values[r][...], grads) - delta)).astype(BF)
            outs[r][0] = dense_dot(dscores, query).astype(BF)
            outs[r][1] = dense_dot(weights.astype(BF), grads).astype(BF)
            part = left_dot(key, dscores)
            acc_ref[...] = part if r == 0 else acc_ref[...] + part

        @pl.when(place_ref[0] < r)
        def _():
            outs[r][...] = jnp.zeros(outs[r].shape, BF)

    rows = jnp.transpose(acc_ref[...]) * HEAD ** (-0.5)
    for i, part in enumerate(gather_heads(rows)):
        dq_ref[:, i * LANES : (i + 1) * LANES] = turn(part, cosine_ref[...], -sine_ref[...]).astype(BF)


def attend_back(place, query, dob, o, lse, cosine, sine, kvs):
    pairs = KV_HEADS // 2
    rows = 6 * BLOCK
    heads = pl.BlockSpec((BLOCK, GROUP), lambda p, s: (0, p))
    table = pl.BlockSpec((BLOCK, LANES), lambda p, s: (0, 0))
    return pl.pallas_call(
        attend_back_kernel,
        grid_spec=pltpu.PrefetchScalarGridSpec(
            num_scalar_prefetch=1,
            grid=(pairs,),
            in_specs=[
                heads, heads, heads,
                pl.BlockSpec((1, 1, rows), lambda p, s: (p, 0, 0)),
                table, table,
                *[pl.BlockSpec((BLOCK, PAIR), lambda p, s: (0, p)) for _ in kvs],
                *[pl.BlockSpec((BLOCK, PAIR), lambda p, s: (0, KV_HEADS // 2 + p)) for _ in kvs],
            ],
            out_specs=[heads, *[pl.BlockSpec((2, BLOCK, PAIR), lambda p, s: (0, 0, p)) for _ in kvs]],
            scratch_shapes=[pltpu.VMEM((PAIR, rows), F32)],
        ),
        out_shape=[
            jax.ShapeDtypeStruct((BLOCK, QD), BF),
            *[jax.ShapeDtypeStruct((2, BLOCK, KD), BF) for _ in kvs],
        ],
        compiler_params=params(),
        cost_estimate=pl.CostEstimate(
            flops=20 * SEQ * BLOCK * HEADS * PAIR, bytes_accessed=14 * BLOCK * QD, transcendentals=SEQ * BLOCK * HEADS
        ),
        name="attend_back",
    )(place, query, dob, o, lse, cosine, sine, *kvs, *kvs)


def picks(slot_rows):
    slots = lax.broadcasted_iota(jnp.int32, (CAP, BLOCK), 0).astype(F32)
    one, zero = jnp.float32(1), jnp.float32(0)
    return [jnp.where(slots == slot_rows[e : e + 1, :], one, zero) for e in range(slot_rows.shape[0])]


def dispatch_kernel(slot_ref, rows_ref, out_ref):
    experts = slot_ref.shape[0]
    chosen = jnp.concatenate([p.astype(BF) for p in picks(slot_ref[...])], axis=0)
    width = out_ref.shape[2]
    for start in range(0, width, COLUMNS):
        size = min(COLUMNS, width - start)
        rows = dense_dot(chosen, rows_ref[:, start : start + size])
        out_ref[:, :, start : start + size] = rows.astype(BF).reshape(experts, CAP, size)


def dispatch(slot_rows, rows, features):
    experts, total = slot_rows.shape
    blocks = total // BLOCK
    return pl.pallas_call(
        dispatch_kernel,
        grid=(blocks,),
        in_specs=[
            pl.BlockSpec((experts, BLOCK), lambda b: (0, b)),
            pl.BlockSpec((BLOCK, features), lambda b: (b, 0)),
        ],
        out_specs=pl.BlockSpec((experts, CAP, features), lambda b: (0, b, 0)),
        out_shape=jax.ShapeDtypeStruct((experts, blocks * CAP, features), BF),
        compiler_params=params(),
        cost_estimate=pl.CostEstimate(
            flops=2 * experts * CAP * total * features,
            bytes_accessed=2 * features * (total + experts * blocks * CAP),
            transcendentals=0,
        ),
        name="dispatch",
    )(slot_rows, rows)


def combine_kernel(slot_ref, slots_ref, out_ref):
    experts, features = slots_ref.shape[0], slots_ref.shape[2]
    chosen = jnp.concatenate([p.astype(BF) for p in picks(slot_ref[...])], axis=0)
    for start in range(0, features, COLUMNS):
        size = min(COLUMNS, features - start)
        held = slots_ref[:, :, start : start + size].reshape(experts * CAP, size)
        out_ref[:, start : start + size] = left_dot(chosen, held).astype(BF)


def combine(slot_rows, slots):
    experts, total = slot_rows.shape
    blocks = total // BLOCK
    features = slots.shape[2]
    return pl.pallas_call(
        combine_kernel,
        grid=(blocks,),
        in_specs=[
            pl.BlockSpec((experts, BLOCK), lambda b: (0, b)),
            pl.BlockSpec((experts, CAP, features), lambda b: (0, b, 0)),
        ],
        out_specs=pl.BlockSpec((BLOCK, features), lambda b: (b, 0)),
        out_shape=jax.ShapeDtypeStruct((total, features), BF),
        compiler_params=params(),
        cost_estimate=pl.CostEstimate(
            flops=2 * experts * CAP * total * features,
            bytes_accessed=2 * features * (total + experts * blocks * CAP),
            transcendentals=0,
        ),
        name="combine",
    )(slot_rows, slots)


def expert_kernel(
    rank_ref, x_ref, dy_ref, wg_ref, wu_ref, wd_ref, ys_ref, dx_ref, gdy_ref, act_ref, dg_ref, du_ref
):
    features = dy_ref.shape[2]
    rows = x_ref[0, :, :features]
    pre = dense_dot(rows, wg_ref[0])
    up = dense_dot(rows, wu_ref[0])
    sigma = 1.0 / (1.0 + jnp.exp(-pre))
    silu = pre * sigma
    active = (silu * up).astype(BF)
    act_ref[0] = active
    column = rank_ref[0] * pl.num_programs(0) + pl.program_id(0)
    lane = lax.broadcasted_iota(jnp.int32, (rows.shape[0], LANES), 1)
    is_high, is_low = lane == column, lane == column + EXPERTS
    table = jnp.where(jnp.logical_or(is_high, is_low), x_ref[0, :, features:].astype(F32), 0.0)
    share = jnp.sum(table, axis=1, keepdims=True)
    result = dense_dot(active, wd_ref[0])
    grads = dy_ref[0].astype(F32)
    dots = jnp.sum(result * grads, axis=1, keepdims=True)
    high = dots.astype(BF).astype(F32)
    dx_ref[0, :, features:] = jnp.where(is_high, high, jnp.where(is_low, dots - high, 0.0)).astype(BF)
    ys_ref[0] = (result * share).astype(BF)
    gated = (grads * share).astype(BF)
    gdy_ref[0] = gated
    dact = right_dot(gated, wd_ref[0])
    dpre = (dact * up * sigma * (1.0 + pre * (1.0 - sigma))).astype(BF)
    dup = (dact * silu).astype(BF)
    dg_ref[0] = dpre
    du_ref[0] = dup
    dx_ref[0, :, :features] = (right_dot(dpre, wg_ref[0]) + right_dot(dup, wu_ref[0])).astype(BF)


def expert_pass(rank, x_slots, dy_slots, w_gate, w_up, w_down):
    experts, rows, features = dy_slots.shape
    hidden = w_gate.shape[2]
    one = lambda e, r: (e, 0, 0)
    longer = pl.BlockSpec((1, rows, features + LANES), one)
    wide = pl.BlockSpec((1, rows, features), one)
    narrow = pl.BlockSpec((1, rows, hidden), one)
    shape = lambda width: jax.ShapeDtypeStruct((experts, rows, width), BF)
    return pl.pallas_call(
        expert_kernel,
        grid_spec=pltpu.PrefetchScalarGridSpec(
            num_scalar_prefetch=1,
            grid=(experts,),
            in_specs=[
                longer, wide,
                pl.BlockSpec((1, features, hidden), one),
                pl.BlockSpec((1, features, hidden), one),
                pl.BlockSpec((1, hidden, features), one),
            ],
            out_specs=[wide, longer, wide, narrow, narrow, narrow],
        ),
        out_shape=[
            shape(features), shape(features + LANES), shape(features), shape(hidden), shape(hidden), shape(hidden)
        ],
        compiler_params=params(),
        cost_estimate=pl.CostEstimate(
            flops=12 * experts * rows * features * hidden,
            bytes_accessed=6 * experts * features * hidden + 10 * experts * rows * features,
            transcendentals=experts * rows * hidden,
        ),
        name="experts",
    )(rank, x_slots, dy_slots, w_gate, w_up, w_down)


def weight_kernel(count, products, step, core_ref, *refs):
    lefts, rights = refs[:count], refs[count : count * (1 + products)]
    outs, held_ref = refs[count * (1 + products) : -1], refs[-1]
    for i in range(products):
        total = sum(left_dot(lefts[m][0], rights[i * count + m][0]) for m in range(count))
        held_ref[...] = total.astype(BF)
        halves(core_ref, held_ref, step, outs[2 * i].at[0], outs[2 * i + 1].at[0])


def weight_pass(core, step, depth, lefts, *rights):
    experts, rows, width = rights[0][0].shape
    one = lambda e, s: (e, 0, 0)
    count, products = len(lefts), len(rights)
    half = jax.ShapeDtypeStruct((experts, depth // 2, width), BF)
    return pl.pallas_call(
        partial(weight_kernel, count, products, step),
        grid_spec=pltpu.PrefetchScalarGridSpec(
            num_scalar_prefetch=1,
            grid=(experts,),
            in_specs=[
                *[pl.BlockSpec((1, rows, depth), one) for _ in lefts],
                *[pl.BlockSpec((1, rows, width), one) for right in rights for _ in right],
            ],
            out_specs=[pl.BlockSpec((1, depth // 2, width), one)] * (2 * products),
            scratch_shapes=[pltpu.VMEM((depth, width), BF)],
        ),
        out_shape=[half] * (2 * products),
        compiler_params=params(),
        cost_estimate=pl.CostEstimate(
            flops=2 * count * products * experts * rows * depth * width,
            bytes_accessed=2 * experts * (products * depth * width + count * rows * (depth + products * width)),
            transcendentals=0,
        ),
        name="expert_weights",
    )(core, *lefts, *[a for right in rights for a in right])


def after(value, *marks):
    return lax.optimization_barrier((value, *marks))[0]


def together(*values):
    return lax.optimization_barrier(values)


def local(
    tokens, out_grad, routes, attn_gain, w_query, w_key, w_value, w_out, moe_gain, w_router,
    w_gate, w_up, w_down,
):
    micros, _, features = tokens.shape
    count = lax.axis_size("expert")
    rank = lax.axis_index("expert")
    exp_dev = w_gate.shape[0]
    dp = lax.axis_size("dp")
    core = (lax.axis_index("dp") % 2).astype(jnp.int32)[None]
    seq_blocks = SEQ // BLOCK
    place = rank % seq_blocks
    cosine, sine = rotary_tables(place * BLOCK + jnp.arange(BLOCK, dtype=jnp.int32))
    place = place.astype(jnp.int32)[None]
    around = [(i, (i + 1) % count) for i in range(count)]
    upward = [(i, i + 1) for i in range(count - 1) if (i + 1) % seq_blocks]
    downward = [(b, a) for a, b in upward]
    ring = lambda a: lax.ppermute(a, "expert", around)
    later = lambda a: lax.ppermute(a, "expert", upward)
    earlier = lambda a: lax.ppermute(a, "expert", downward)
    add = lambda a, b: (a.astype(F32) + b.astype(F32)).astype(BF)
    every = lambda a, axis: lax.all_gather(a, axis, axis=0, tiled=True)
    swap = lambda a: lax.ppermute(a, "dp", [(i, i ^ 1) for i in range(dp)])
    same_core = [list(range(c, dp, 2)) for c in range(2)]
    share = lambda a, dim: lax.psum_scatter(
        a, "dp", scatter_dimension=dim, axis_index_groups=same_core, tiled=True
    )

    beside = jnp.zeros((w_router.shape[0], LANES - EXPERTS - 2), BF)
    kv_w = every(
        jnp.concatenate([w_key, w_value, w_router, attn_gain[:, None], moe_gain[:, None], beside], axis=1), "dp"
    )
    qo_w = every(after(jnp.concatenate([w_query, w_out], axis=1), kv_w), "dp")
    router_w = kv_w[:, 2 * KD :]
    gains = router_w[:, EXPERTS : EXPERTS + 2].T.astype(F32)
    gain_one, gain_two = gains[0:1], gains[1:2]

    members = jnp.any(routes[:, :, :, None] == jnp.arange(EXPERTS, dtype=jnp.int32), axis=2)
    before = jnp.tril(jnp.ones((BLOCK, BLOCK), F32), -1).astype(BF)
    slots = jnp.einsum("ts,mse->mte", before, members.astype(BF), preferred_element_type=F32)
    slots = jnp.where(members, slots, -1.0).astype(BF)
    dy_ring = [
        jnp.concatenate([out_grad, slots, jnp.zeros((micros, BLOCK, LANES - EXPERTS), BF)], axis=2)
    ]

    dy_ring.append(ring(dy_ring[0]))
    x_whole = tokens.reshape(micros * BLOCK, features)
    normed, scale_one = norm_rows(x_whole, gain_one)
    normed_one, dy_ring[1] = together(normed, dy_ring[1])
    kv_own = project(normed_one, kv_w, 2 * KD, KD, cosine, sine)
    dy_ring.append(ring(dy_ring[1]))
    kvs = [[kv_own[0]]]
    for _ in range(seq_blocks - 1):
        kvs[0].append(later(kvs[0][-1]))
    normed_two, dy_ring[2] = together(normed, dy_ring[2])
    queries = project(normed_two, qo_w, QD, QD, cosine, sine)
    while len(dy_ring) < count:
        dy_ring.append(ring(dy_ring[-1]))

    heads, mids, sent = [], [], []
    held = [after(kv_own[1], kvs[0][-1])]
    held.append(later(held[-1]))
    for m in range(micros):
        o, ob, lse = attend(place, queries[m], kvs[m])
        if m == 0:
            held[-1], o, ob, lse = together(held[-1], o, ob, lse)
            held.append(later(held[-1]))
            ob, dy_ring[-1] = together(ob, dy_ring[-1])
        heads.append((o, ob, lse))
        mid, out, scale_two, gates = outward(ob, qo_w, tokens[m], gain_two, router_w, routes[m])
        mids.append((mid, out, scale_two, gates))
        sent.append(every(out, "expert"))
        if m == 0:
            held[-1], out = together(held[-1], out)
            while len(held) < seq_blocks:
                held.append(later(held[-1]))
            kvs.append(held)

    def in_order(m):
        whole = jnp.zeros((count * BLOCK, features + LANES), BF)
        for step, block in enumerate(dy_ring):
            whole = lax.dynamic_update_slice_in_dim(whole, block[m], (rank - step) % count * BLOCK, 0)
        return whole

    parts, slot_rows, scaled, dx_sums, dx_home = [], [], [], [], []
    for m in range(micros):
        dy_all = in_order(m)
        table = lax.dynamic_slice_in_dim(dy_all, features + rank * exp_dev, exp_dev, 1)
        slot_rows.append(table.astype(F32).T)
        dy_slots = dispatch(slot_rows[m], dy_all, features)
        x_slots = dispatch(slot_rows[m], sent[m], features + LANES)
        if m > 0:
            x_slots, dx_sums[-1] = together(x_slots, dx_sums[-1])
        ys, dx, *rest = expert_pass(rank.astype(jnp.int32)[None], x_slots, dy_slots, w_gate, w_up, w_down)
        parts.append((x_slots, *rest))
        scaled.append(ys)
        dx_sums.append(combine(slot_rows[m], dx))
    for a in dx_sums:
        dx_home.append(lax.psum_scatter(a, "expert", scatter_dimension=0, tiled=True))

    xs, gdys, acts, dgs, dus = zip(*parts)
    hidden = w_down.shape[1]
    first_act, dx_home[0], _ = together(acts[0], dx_home[0], dx_sums[-1])
    keep_down, send_down = weight_pass(core, hidden // dp, hidden, (first_act, *acts[1:]), gdys)
    got_down = swap(send_down)
    dgs = after(dgs[0], keep_down), *dgs[1:]
    ups = weight_pass(core, features // dp, features, xs, dgs, dus)
    got_down, *ups = together(got_down, *ups)
    down_half = add(keep_down, got_down)
    down_grad = share(down_half, 1)
    got_gate, got_up = swap(ups[1]), swap(ups[3])

    def back_home(m, dx):
        mid, _, scale_two, gates = mids[m]
        return home_back(dx, gates, mid, scale_two, out_grad[m], router_w, gain_two, qo_w)

    def back_heads(m, dob):
        o, _, lse = heads[m]
        dq, *pieces = attend_back(place, queries[m], dob, o, lse, cosine, sine, kvs[m])
        return dq, pieces[::-1]

    first = list(back_home(0, after(dx_home[0], down_half)))
    dq_one, far_one = back_heads(0, first[2])
    got_gate, got_up, dq_one = together(got_gate, got_up, dq_one)
    gate_half = add(ups[0], got_gate)
    up_half = add(ups[2], got_up)
    gate_grad = share(gate_half, 1)
    up_grad = share(up_half, 1)
    back_one = earlier(far_one[0])
    second = list(back_home(1, after(dx_home[1], gate_half, up_half)))
    back_one, second[2] = together(back_one, second[2])
    back_one = earlier(add(back_one, far_one[1]))
    dq_two, far_two = back_heads(1, second[2])
    back_one, dq_two, far_two[0] = together(back_one, dq_two, far_two[0])
    for piece in far_one[2:-1]:
        back_one = earlier(add(back_one, piece))
    back_two = earlier(far_two[0])
    back_one = add(back_one, far_one[-1])

    def back_last(m, dq, dkv, dmid):
        return last_back(
            dq, dkv, cosine, sine, qo_w, kv_w, tokens[m], scale_one[m * BLOCK : (m + 1) * BLOCK], gain_one, dmid
        )

    back_two, back_one = together(back_two, back_one)
    back_two = earlier(add(back_two, far_two[1]))
    grad_x_one, dkv_one, dgain_one = back_last(0, dq_one, back_one, first[0])
    back_two, dkv_one = together(back_two, dkv_one)
    for piece in far_two[2:-1]:
        back_two = earlier(add(back_two, piece))
    back_two = add(back_two, far_two[-1])
    grad_x_two, dkv_two, dgain_two = back_last(1, dq_two, back_two, second[0])

    gain_rows = jnp.concatenate([dgain_one + dgain_two, first[4] + second[4]], axis=0)
    gain_columns = jnp.pad(gain_rows.T, ((0, 0), (EXPERTS, LANES - EXPERTS - 2)))
    gain_columns = after(gain_columns, down_grad, gate_grad)
    keep, send = dense_grads(
        core, features // dp, [normed] * micros, [dq_one, dq_two], [dkv_one, dkv_two], [k[1] for k in mids],
        [first[3], second[3]], [h[1] for h in heads], [first[1], second[1]], gain_columns,
    )
    dense_sum = share(add(keep, swap(send)), 0)
    dense = lax.psum(dense_sum, "expert").astype(F32)
    columns = lambda start, width: dense[:, start : start + width]
    small = QD + 2 * KD

    mixed = []
    for m in range(micros):
        sums = combine(slot_rows[m], after(scaled[m], keep))
        block = lambda j: lax.dynamic_slice_in_dim(sums, (rank - 1 - j) % count * BLOCK, BLOCK, 0)
        held = block(0)
        for step in range(1, count):
            held = add(ring(held), block(step))
        mixed.append((mids[m][0] + held.astype(F32)).astype(BF))
    return (
        jnp.stack(mixed),
        jnp.stack([grad_x_one, grad_x_two]),
        dense[:, small + EXPERTS],
        columns(0, QD),
        columns(QD, KD),
        columns(QD + KD, KD),
        columns(small + LANES, features),
        dense[:, small + EXPERTS + 1],
        columns(small, EXPERTS),
        gate_grad.astype(F32),
        up_grad.astype(F32),
        down_grad.astype(F32),
    )


def solution(mesh):
    rows = P(None, ("dp", "expert"), None)
    return jax.shard_map(
        local,
        mesh=mesh,
        in_specs=(
            rows, rows, rows, P("dp"), P("dp", None), P("dp", None), P("dp", None), P("dp", None),
            P("dp"), P("dp", None),
            P("expert", None, None), P("expert", None, None), P("expert", None, None),
        ),
        out_specs=(
            rows, rows, P("dp"), P("dp", None), P("dp", None), P("dp", None), P("dp", None),
            P("dp"), P("dp", None),
            P("expert", "dp", None), P("expert", "dp", None), P("expert", "dp", None),
        ),
        check_vma=False,
    )
```

```python
from functools import partial

import jax
import jax.numpy as jnp
from jax import lax
from jax.experimental import pallas as pl
from jax.experimental.pallas import tpu as pltpu
from jax.sharding import PartitionSpec as P

HEADS = 24
KV_HEADS = 8
HEAD = 64
FF = 512
EXPERTS = 40
TOP = 8
BLOCK = 256
SEQ = 1024
CAP = 64
QD = 1536
KD = 512

EPSILON = 1e-06
ROPE_BASE = 10000.0
NEGATIVE = -1e30
LANES = 128
COLUMNS = 256
VMEM_LIMIT = 56 * 2**20
COST_SCALE = 0.1

BF = jnp.bfloat16
F32 = jnp.float32


def dense_dot(left, right):
    return jnp.dot(left, right, preferred_element_type=F32)


def left_dot(left, right):
    return lax.dot_general(left, right, (((0,), (0,)), ((), ())), preferred_element_type=F32)


def right_dot(left, right):
    return lax.dot_general(left, right, (((1,), (1,)), ((), ())), preferred_element_type=F32)


def rotary_tables(positions):
    half_size = HEAD // 2
    frequency = ROPE_BASE ** (-jnp.arange(half_size, dtype=F32) / half_size)
    angle = positions.astype(F32)[:, None] * frequency[None, :]
    cosine, sine = jnp.cos(angle), jnp.sin(angle)
    tiles = LANES // HEAD
    return (
        jnp.concatenate([cosine, cosine] * tiles, axis=1),
        jnp.concatenate([-sine, sine] * tiles, axis=1),
    )


def cost(flops, bytes_accessed, transcendentals):
    scale = lambda n: int(n * COST_SCALE)
    return pl.CostEstimate(
        flops=scale(flops), bytes_accessed=scale(bytes_accessed), transcendentals=scale(transcendentals)
    )


def params(limit=VMEM_LIMIT):
    return pltpu.CompilerParams(vmem_limit_bytes=limit)


def swap_halves(values):
    lane = lax.broadcasted_iota(jnp.int32, values.shape, 1)
    half = HEAD // 2
    return jnp.where(
        lane % HEAD < half,
        pltpu.roll(values, LANES - half, 1),
        pltpu.roll(values, half, 1),
    )


def turn(values, cosine, sine):
    return values * cosine + swap_halves(values) * sine


def norm_kernel(x_ref, gain_ref, normed_ref, scale_ref):
    rows = x_ref[...].astype(F32)
    scale = lax.rsqrt(jnp.mean(rows * rows, axis=1, keepdims=True) + EPSILON)
    scale_ref[...] = scale
    normed_ref[...] = (rows * scale * gain_ref[...]).astype(BF)


def norm_rows(x, gain):
    total, features = x.shape
    return pl.pallas_call(
        norm_kernel,
        grid=(total // BLOCK,),
        in_specs=[
            pl.BlockSpec((BLOCK, features), lambda i: (i, 0)),
            pl.BlockSpec((1, features), lambda i: (0, 0)),
        ],
        out_specs=[
            pl.BlockSpec((BLOCK, features), lambda i: (i, 0)),
            pl.BlockSpec((BLOCK, 1), lambda i: (i, 0)),
        ],
        out_shape=[
            jax.ShapeDtypeStruct((total, features), BF),
            jax.ShapeDtypeStruct((total, 1), F32),
        ],
        compiler_params=params(),
        cost_estimate=cost(flops=5 * total * features, bytes_accessed=4 * total * features, transcendentals=0),
        name="norm",
    )(x, gain)


def project_kernel(turned, normed_ref, w_ref, cosine_ref, sine_ref, *outs):
    tile = w_ref.shape[1]
    rows = dense_dot(normed_ref[...], w_ref[...])

    def write(turning):
        for start in range(0, tile, LANES):
            for m, out_ref in enumerate(outs):
                part = rows[m * BLOCK : (m + 1) * BLOCK, start : start + LANES]
                if turning:
                    part = turn(part, cosine_ref[...], sine_ref[...])
                out_ref[:, start : start + LANES] = part.astype(BF)

    pl.when(pl.program_id(0) < turned)(lambda: write(True))
    pl.when(pl.program_id(0) >= turned)(lambda: write(False))


def project(normed, weight, start, columns, turned_columns, cosine, sine):
    total, features = normed.shape
    tile = 2 * COLUMNS
    micros = total // BLOCK
    return pl.pallas_call(
        partial(project_kernel, turned_columns // tile),
        grid=(columns // tile,),
        in_specs=[
            pl.BlockSpec((total, features), lambda j: (0, 0)),
            pl.BlockSpec((features, tile), lambda j: (0, start // tile + j)),
            pl.BlockSpec((BLOCK, LANES), lambda j: (0, 0)),
            pl.BlockSpec((BLOCK, LANES), lambda j: (0, 0)),
        ],
        out_specs=[pl.BlockSpec((BLOCK, tile), lambda j: (0, j))] * micros,
        out_shape=[jax.ShapeDtypeStruct((BLOCK, columns), BF)] * micros,
        compiler_params=params(),
        cost_estimate=cost(
            flops=2 * total * features * columns,
            bytes_accessed=2 * (features * columns + total * (features + columns)),
            transcendentals=0,
        ),
        name="project",
    )(normed, weight, cosine, sine)


def outward_kernel(ob_ref, w_ref, x_ref, gain_ref, router_ref, routes_ref, mid_ref, sent_ref, scale_ref, gates_ref):
    j = pl.program_id(0)
    tile = w_ref.shape[1]
    features = mid_ref.shape[1]
    where = pl.ds(pl.multiple_of(j * tile, tile), tile)
    mid_ref[:, where] = x_ref[:, where].astype(F32) + dense_dot(ob_ref[...], w_ref[...])

    @pl.when(j == pl.num_programs(0) - 1)
    def _():
        mid = mid_ref[...]
        scale = lax.rsqrt(jnp.mean(mid * mid, axis=1, keepdims=True) + EPSILON)
        scale_ref[...] = scale
        normed = (mid * scale * gain_ref[...]).astype(BF)
        sent_ref[:, :features] = normed
        lane = lax.broadcasted_iota(jnp.int32, (BLOCK, LANES), 1)
        routes = routes_ref[...]
        member = lane == routes[:, 0:1]
        for k in range(1, TOP):
            member = jnp.logical_or(member, lane == routes[:, k : k + 1])
        logits = jnp.where(member, dense_dot(normed, router_ref[...]), NEGATIVE)
        weights = jnp.exp(logits - jnp.max(logits, axis=1, keepdims=True))
        weights = jnp.where(member, weights, 0.0)
        gates = weights / jnp.sum(weights, axis=1, keepdims=True)
        gates_ref[...] = gates
        high = gates.astype(BF).astype(F32)
        sent_ref[:, features:] = (high + pltpu.roll(gates - high, EXPERTS, 1)).astype(BF)


def outward(ob, w_qo, x, gain, router, routes):
    features = x.shape[1]
    tile = 2 * COLUMNS
    whole = lambda a: pl.BlockSpec(a.shape, lambda j: (0, 0))
    fixed = lambda *shape: pl.BlockSpec(shape, lambda j: (0, 0))
    return pl.pallas_call(
        outward_kernel,
        grid=(features // tile,),
        in_specs=[
            whole(ob),
            pl.BlockSpec((QD, tile), lambda j: (0, QD // tile + j)),
            whole(x), whole(gain), whole(router), whole(routes),
        ],
        out_specs=[fixed(BLOCK, features), fixed(BLOCK, features + LANES), fixed(BLOCK, 1), fixed(BLOCK, LANES)],
        out_shape=[
            jax.ShapeDtypeStruct((BLOCK, features), F32),
            jax.ShapeDtypeStruct((BLOCK, features + LANES), BF),
            jax.ShapeDtypeStruct((BLOCK, 1), F32),
            jax.ShapeDtypeStruct((BLOCK, LANES), F32),
        ],
        compiler_params=params(),
        cost_estimate=cost(
            flops=2 * BLOCK * features * QD, bytes_accessed=2 * features * QD + 14 * BLOCK * features, transcendentals=0
        ),
        name="outward",
    )(ob, w_qo, x, gain, router, routes)


def home_kernel(
    dx_ref, gates_ref, mid_ref, scale_ref, dy_ref, router_ref, gain_ref, w_ref,
    dmid_ref, da_ref, dob_ref, dlog_ref, dgain_ref,
):
    j = pl.program_id(0)
    features = mid_ref.shape[1]
    tile = w_ref.shape[0]

    @pl.when(j == 0)
    def _():
        table = dx_ref[:, features:].astype(F32)
        dgates = table + pltpu.roll(table, LANES - EXPERTS, 1)
        gates = gates_ref[...]
        dc = gates * (dgates - jnp.sum(gates * dgates, axis=1, keepdims=True))
        dlog = dc.astype(BF)
        dlog_ref[...] = dlog
        dnormed = dx_ref[:, :features].astype(F32) + right_dot(dlog, router_ref[...])
        mid = mid_ref[...]
        scale = scale_ref[...]
        dgain_ref[...] = jnp.sum(dnormed * mid * scale, axis=0, keepdims=True)
        scaled = dnormed * gain_ref[...]
        mean = jnp.mean(scaled * mid, axis=1, keepdims=True)
        dmid = dy_ref[...].astype(F32) + scale * scaled - mid * (scale * scale * scale * mean)
        dmid_ref[...] = dmid
        da_ref[...] = dmid.astype(BF)

    where = pl.ds(pl.multiple_of(j * tile, tile), tile)
    dob_ref[:, where] = right_dot(da_ref[...], w_ref[...]).astype(BF)


def home_back(dx, gates, mid, scale, dy, router, gain, w_qo):
    features = mid.shape[1]
    tile = 2 * COLUMNS
    whole = lambda a: pl.BlockSpec(a.shape, lambda j: (0, 0))
    fixed = lambda *shape: pl.BlockSpec(shape, lambda j: (0, 0))
    return pl.pallas_call(
        home_kernel,
        grid=(QD // tile,),
        in_specs=[
            whole(dx), whole(gates), whole(mid), whole(scale), whole(dy), whole(router), whole(gain),
            pl.BlockSpec((tile, features), lambda j: (j, 1)),
        ],
        out_specs=[
            fixed(BLOCK, features), fixed(BLOCK, features), fixed(BLOCK, QD), fixed(BLOCK, LANES), fixed(1, features),
        ],
        out_shape=[
            jax.ShapeDtypeStruct((BLOCK, features), F32),
            jax.ShapeDtypeStruct((BLOCK, features), BF),
            jax.ShapeDtypeStruct((BLOCK, QD), BF),
            jax.ShapeDtypeStruct((BLOCK, LANES), BF),
            jax.ShapeDtypeStruct((1, features), F32),
        ],
        compiler_params=params(),
        cost_estimate=cost(
            flops=2 * BLOCK * features * QD, bytes_accessed=2 * features * QD + 18 * BLOCK * features, transcendentals=0
        ),
        name="home_back",
    )(dx, gates, mid, scale, dy, router, gain, w_qo)


def last_kernel(
    dq_ref, dkv_ref, cosine_ref, sine_ref, wq_ref, wkv_ref, x_ref, scale_ref, gain_ref, dmid_ref,
    dx_ref, dkvb_ref, dgain_ref,
):
    j = pl.program_id(0)
    tile = wq_ref.shape[0]

    @pl.when(j == 0)
    def _():
        for start in range(0, KD, LANES):
            part = dkv_ref[0, :, start : start + LANES].astype(F32)
            dkvb_ref[:, start : start + LANES] = turn(part, cosine_ref[...], -sine_ref[...]).astype(BF)
        dkvb_ref[:, KD:] = dkv_ref[1]

    where = pl.ds(pl.multiple_of(j * tile, tile), tile)
    dx_ref[:, where] = right_dot(dq_ref[...], wq_ref[...]) + right_dot(dkvb_ref[...], wkv_ref[...])

    @pl.when(j == pl.num_programs(0) - 1)
    def _():
        dnormed = dx_ref[...]
        rows = x_ref[...].astype(F32)
        scale = scale_ref[...]
        dgain_ref[...] = jnp.sum(dnormed * rows * scale, axis=0, keepdims=True)
        scaled = dnormed * gain_ref[...]
        mean = jnp.mean(scaled * rows, axis=1, keepdims=True)
        dx_ref[...] = dmid_ref[...] + scale * scaled - rows * (scale * scale * scale * mean)


def last_back(dq, dkv, cosine, sine, w_q, w_kv, x, scale, gain, dmid):
    features = x.shape[1]
    tile = 2 * COLUMNS
    whole = lambda a: pl.BlockSpec(a.shape, lambda j: (0,) * a.ndim)
    fixed = lambda *shape: pl.BlockSpec(shape, lambda j: (0, 0))
    return pl.pallas_call(
        last_kernel,
        grid=(features // tile,),
        in_specs=[
            whole(dq), whole(dkv), whole(cosine), whole(sine),
            pl.BlockSpec((tile, QD), lambda j: (j, 0)),
            pl.BlockSpec((tile, 2 * KD), lambda j: (j, QD // KD)),
            whole(x), whole(scale), whole(gain), whole(dmid),
        ],
        out_specs=[fixed(BLOCK, features), fixed(BLOCK, 2 * KD), fixed(1, features)],
        out_shape=[
            jax.ShapeDtypeStruct((BLOCK, features), F32),
            jax.ShapeDtypeStruct((BLOCK, 2 * KD), BF),
            jax.ShapeDtypeStruct((1, features), F32),
        ],
        compiler_params=params(),
        cost_estimate=cost(
            flops=2 * BLOCK * features * (QD + 2 * KD),
            bytes_accessed=2 * features * (QD + 2 * KD) + 16 * BLOCK * features,
            transcendentals=0,
        ),
        name="last_back",
    )(dq, dkv, cosine, sine, w_q, w_kv, x, scale, gain, dmid)


def halves(core_ref, held_ref, step, keep_ref, send_ref):
    core = core_ref[0]
    for q in range(held_ref.shape[0] // (2 * step)):
        mine = pl.multiple_of((2 * q + core) * step, step)
        other = pl.multiple_of((2 * q + 1 - core) * step, step)
        keep_ref[q * step : (q + 1) * step, :] = held_ref[pl.ds(mine, step), :]
        send_ref[q * step : (q + 1) * step, :] = held_ref[pl.ds(other, step), :]


def dense_kernel(micros, step, core_ref, *refs):
    ins, (gains_ref, keep_ref, send_ref, held_ref) = refs[: 7 * micros], refs[7 * micros :]
    normed, dq, dkv, sent, dlog, ob, da = (ins[i * micros : (i + 1) * micros] for i in range(7))

    def total(lefts, rights):
        return sum(left_dot(left[...], right[...]) for left, right in zip(lefts, rights))

    start = 0
    for lefts, rights in ((normed, dq), (normed, dkv), (sent, dlog), (ob, da)):
        width = rights[0].shape[1]
        part = total(lefts, rights)
        if rights is dlog:
            part = part + gains_ref[...]
        held_ref[:, start : start + width] = part.astype(BF)
        start += width
    halves(core_ref, held_ref, step, keep_ref, send_ref)


def dense_grads(core, step, normed, dq, dkv, sent, dlog, ob, da, gains):
    groups = (normed, dq, dkv, sent, dlog, ob, da)
    micros = len(dq)
    tile = max(3 * LANES, 2 * step)
    lefts = (True, False, False, True, False, True, False)
    width = sum(group[0].shape[1] for group, left in zip(groups, lefts) if not left)
    specs = []
    for group, left in zip(groups, lefts):
        for m, a in enumerate(group):
            if left:
                block = m if a.shape[0] > BLOCK else 0
                specs.append(pl.BlockSpec((BLOCK, tile), lambda j, s, block=block: (block, j)))
            else:
                specs.append(pl.BlockSpec(a.shape, lambda j, s: (0, 0)))
    half = jax.ShapeDtypeStruct((QD // 2, width), BF)
    return pl.pallas_call(
        partial(dense_kernel, micros, step),
        grid_spec=pltpu.PrefetchScalarGridSpec(
            num_scalar_prefetch=1,
            grid=(QD // tile,),
            in_specs=[*specs, pl.BlockSpec((tile, gains.shape[1]), lambda j, s: (j, 0))],
            out_specs=[pl.BlockSpec((tile // 2, width), lambda j, s: (j, 0))] * 2,
            scratch_shapes=[pltpu.VMEM((tile, width), BF)],
        ),
        out_shape=[half, half],
        compiler_params=params(),
        cost_estimate=cost(
            flops=2 * micros * BLOCK * QD * width,
            bytes_accessed=2 * QD * width + 4 * micros * BLOCK * (QD + width),
            transcendentals=0,
        ),
        name="dense_grads",
    )(core, *[a for group in groups for a in group], gains)


PAIR = 2 * HEAD
GROUP = HEADS // KV_HEADS * PAIR


def spread(values):
    lane = lax.broadcasted_iota(jnp.int32, (BLOCK, LANES), 1)
    first = lane < HEAD
    zero = jnp.zeros((BLOCK, LANES), F32)
    one, two, three = (values[:, i * LANES : (i + 1) * LANES] for i in range(3))
    return jnp.concatenate(
        [
            jnp.where(first, one, zero),
            jnp.where(first, pltpu.roll(one, HEAD, 1), zero),
            jnp.where(first, two, zero),
            jnp.where(first, zero, two),
            jnp.where(first, zero, pltpu.roll(three, HEAD, 1)),
            jnp.where(first, zero, three),
        ],
        axis=0,
    )


def gather_heads(rows):
    lane = lax.broadcasted_iota(jnp.int32, (BLOCK, LANES), 1)
    first = lane < HEAD
    part = [rows[i * BLOCK : (i + 1) * BLOCK] for i in range(6)]
    return (
        jnp.where(first, part[0], pltpu.roll(part[1], HEAD, 1)),
        jnp.where(first, part[2], part[3]),
        jnp.where(first, pltpu.roll(part[4], HEAD, 1), part[5]),
    )


def attend_kernel(place_ref, q_ref, *refs):
    blocks = SEQ // BLOCK
    keys, values = refs[:blocks], refs[blocks : 2 * blocks]
    o_ref, ob_ref, lse_ref, max_ref, sum_ref, acc_ref = refs[2 * blocks :]
    query = spread(q_ref[...].astype(F32) * HEAD ** (-0.5)).astype(BF)
    for r in range(blocks):

        @pl.when(place_ref[0] >= r)
        def _():
            scores = right_dot(keys[r][...], query)
            top = jnp.max(scores, axis=0, keepdims=True)
            if r > 0:
                before = max_ref[...]
                top = jnp.maximum(top, before)
            weights = jnp.exp(scores - top)
            total = jnp.sum(weights, axis=0, keepdims=True)
            out = left_dot(values[r][...], weights.astype(BF))
            if r > 0:
                factor = jnp.exp(before - top)
                total = total + sum_ref[...] * factor
                out = out + acc_ref[...] * factor
            max_ref[...] = top
            sum_ref[...] = total
            acc_ref[...] = out

    lse_ref[0] = max_ref[...] + jnp.log(sum_ref[...])
    rows = jnp.transpose(acc_ref[...] / sum_ref[...])
    for i, part in enumerate(gather_heads(rows)):
        o_ref[:, i * LANES : (i + 1) * LANES] = part
        ob_ref[:, i * LANES : (i + 1) * LANES] = part.astype(BF)


def attend(place, query, kvs):
    pairs = KV_HEADS // 2
    rows = 6 * BLOCK
    return pl.pallas_call(
        attend_kernel,
        grid_spec=pltpu.PrefetchScalarGridSpec(
            num_scalar_prefetch=1,
            grid=(pairs,),
            in_specs=[
                pl.BlockSpec((BLOCK, GROUP), lambda p, s: (0, p)),
                *[pl.BlockSpec((BLOCK, PAIR), lambda p, s: (0, p)) for _ in kvs],
                *[pl.BlockSpec((BLOCK, PAIR), lambda p, s: (0, KV_HEADS // 2 + p)) for _ in kvs],
            ],
            out_specs=[
                pl.BlockSpec((BLOCK, GROUP), lambda p, s: (0, p)),
                pl.BlockSpec((BLOCK, GROUP), lambda p, s: (0, p)),
                pl.BlockSpec((1, 1, rows), lambda p, s: (p, 0, 0)),
            ],
            scratch_shapes=[
                pltpu.VMEM((1, rows), F32),
                pltpu.VMEM((1, rows), F32),
                pltpu.VMEM((PAIR, rows), F32),
            ],
        ),
        out_shape=[
            jax.ShapeDtypeStruct((BLOCK, QD), F32),
            jax.ShapeDtypeStruct((BLOCK, QD), BF),
            jax.ShapeDtypeStruct((pairs, 1, rows), F32),
        ],
        compiler_params=params(),
        cost_estimate=cost(
            flops=8 * SEQ * BLOCK * HEADS * PAIR, bytes_accessed=10 * BLOCK * QD, transcendentals=SEQ * BLOCK * HEADS
        ),
        name="attend",
    )(place, query, *kvs, *kvs)


def attend_back_kernel(place_ref, q_ref, dob_ref, o_ref, lse_ref, cosine_ref, sine_ref, *refs):
    blocks = SEQ // BLOCK
    keys, values = refs[:blocks], refs[blocks : 2 * blocks]
    dq_ref, outs, acc_ref = refs[2 * blocks], refs[2 * blocks + 1 : 3 * blocks + 1], refs[-1]
    query = spread(q_ref[...].astype(F32) * HEAD ** (-0.5)).astype(BF)
    grads = spread(dob_ref[...].astype(F32))
    delta = jnp.sum(jnp.transpose(grads * spread(o_ref[...])), axis=0, keepdims=True)
    grads = grads.astype(BF)
    for r in range(blocks):

        @pl.when(place_ref[0] >= r)
        def _():
            key = keys[r][...]
            weights = jnp.exp(right_dot(key, query) - lse_ref[0])
            dscores = (weights * (right_dot(values[r][...], grads) - delta)).astype(BF)
            outs[r][0] = dense_dot(dscores, query).astype(BF)
            outs[r][1] = dense_dot(weights.astype(BF), grads).astype(BF)
            part = left_dot(key, dscores)
            acc_ref[...] = part if r == 0 else acc_ref[...] + part

        @pl.when(place_ref[0] < r)
        def _():
            outs[r][...] = jnp.zeros(outs[r].shape, BF)

    rows = jnp.transpose(acc_ref[...]) * HEAD ** (-0.5)
    for i, part in enumerate(gather_heads(rows)):
        dq_ref[:, i * LANES : (i + 1) * LANES] = turn(part, cosine_ref[...], -sine_ref[...]).astype(BF)


def attend_back(place, query, dob, o, lse, cosine, sine, kvs):
    pairs = KV_HEADS // 2
    rows = 6 * BLOCK
    heads = pl.BlockSpec((BLOCK, GROUP), lambda p, s: (0, p))
    table = pl.BlockSpec((BLOCK, LANES), lambda p, s: (0, 0))
    return pl.pallas_call(
        attend_back_kernel,
        grid_spec=pltpu.PrefetchScalarGridSpec(
            num_scalar_prefetch=1,
            grid=(pairs,),
            in_specs=[
                heads, heads, heads,
                pl.BlockSpec((1, 1, rows), lambda p, s: (p, 0, 0)),
                table, table,
                *[pl.BlockSpec((BLOCK, PAIR), lambda p, s: (0, p)) for _ in kvs],
                *[pl.BlockSpec((BLOCK, PAIR), lambda p, s: (0, KV_HEADS // 2 + p)) for _ in kvs],
            ],
            out_specs=[heads, *[pl.BlockSpec((2, BLOCK, PAIR), lambda p, s: (0, 0, p)) for _ in kvs]],
            scratch_shapes=[pltpu.VMEM((PAIR, rows), F32)],
        ),
        out_shape=[
            jax.ShapeDtypeStruct((BLOCK, QD), BF),
            *[jax.ShapeDtypeStruct((2, BLOCK, KD), BF) for _ in kvs],
        ],
        compiler_params=params(),
        cost_estimate=cost(
            flops=20 * SEQ * BLOCK * HEADS * PAIR, bytes_accessed=14 * BLOCK * QD, transcendentals=SEQ * BLOCK * HEADS
        ),
        name="attend_back",
    )(place, query, dob, o, lse, cosine, sine, *kvs, *kvs)


def picks(slot_rows):
    slots = lax.broadcasted_iota(jnp.int32, (CAP, BLOCK), 0).astype(F32)
    one, zero = jnp.float32(1), jnp.float32(0)
    return [jnp.where(slots == slot_rows[e : e + 1, :], one, zero) for e in range(slot_rows.shape[0])]


def dispatch_kernel(slot_ref, rows_ref, out_ref):
    experts = slot_ref.shape[0]
    chosen = jnp.concatenate([p.astype(BF) for p in picks(slot_ref[...])], axis=0)
    width = out_ref.shape[2]
    for start in range(0, width, COLUMNS):
        size = min(COLUMNS, width - start)
        rows = dense_dot(chosen, rows_ref[:, start : start + size])
        out_ref[:, :, start : start + size] = rows.astype(BF).reshape(experts, CAP, size)


def dispatch(slot_rows, rows, features):
    experts, total = slot_rows.shape
    blocks = total // BLOCK
    return pl.pallas_call(
        dispatch_kernel,
        grid=(blocks,),
        in_specs=[
            pl.BlockSpec((experts, BLOCK), lambda b: (0, b)),
            pl.BlockSpec((BLOCK, features), lambda b: (b, 0)),
        ],
        out_specs=pl.BlockSpec((experts, CAP, features), lambda b: (0, b, 0)),
        out_shape=jax.ShapeDtypeStruct((experts, blocks * CAP, features), BF),
        compiler_params=params(),
        cost_estimate=cost(
            flops=2 * experts * CAP * total * features,
            bytes_accessed=2 * features * (total + experts * blocks * CAP),
            transcendentals=0,
        ),
        name="dispatch",
    )(slot_rows, rows)


def combine_kernel(slot_ref, slots_ref, out_ref):
    experts, features = slots_ref.shape[0], slots_ref.shape[2]
    chosen = jnp.concatenate([p.astype(BF) for p in picks(slot_ref[...])], axis=0)
    for start in range(0, features, COLUMNS):
        size = min(COLUMNS, features - start)
        held = slots_ref[:, :, start : start + size].reshape(experts * CAP, size)
        out_ref[:, start : start + size] = left_dot(chosen, held).astype(BF)


def combine(slot_rows, slots):
    experts, total = slot_rows.shape
    blocks = total // BLOCK
    features = slots.shape[2]
    return pl.pallas_call(
        combine_kernel,
        grid=(blocks,),
        in_specs=[
            pl.BlockSpec((experts, BLOCK), lambda b: (0, b)),
            pl.BlockSpec((experts, CAP, features), lambda b: (0, b, 0)),
        ],
        out_specs=pl.BlockSpec((BLOCK, features), lambda b: (b, 0)),
        out_shape=jax.ShapeDtypeStruct((total, features), BF),
        compiler_params=params(),
        cost_estimate=cost(
            flops=2 * experts * CAP * total * features,
            bytes_accessed=2 * features * (total + experts * blocks * CAP),
            transcendentals=0,
        ),
        name="combine",
    )(slot_rows, slots)


def expert_kernel(
    rank_ref, x_ref, dy_ref, wg_ref, wu_ref, wd_ref, ys_ref, dx_ref, gdy_ref, act_ref, dg_ref, du_ref
):
    features = dy_ref.shape[2]
    rows = x_ref[0, :, :features]
    pre = dense_dot(rows, wg_ref[0])
    up = dense_dot(rows, wu_ref[0])
    sigma = 1.0 / (1.0 + jnp.exp(-pre))
    silu = pre * sigma
    active = (silu * up).astype(BF)
    act_ref[0] = active
    column = rank_ref[0] * pl.num_programs(0) + pl.program_id(0)
    lane = lax.broadcasted_iota(jnp.int32, (rows.shape[0], LANES), 1)
    is_high, is_low = lane == column, lane == column + EXPERTS
    table = jnp.where(jnp.logical_or(is_high, is_low), x_ref[0, :, features:].astype(F32), 0.0)
    share = jnp.sum(table, axis=1, keepdims=True)
    result = dense_dot(active, wd_ref[0])
    grads = dy_ref[0].astype(F32)
    dots = jnp.sum(result * grads, axis=1, keepdims=True)
    high = dots.astype(BF).astype(F32)
    dx_ref[0, :, features:] = jnp.where(is_high, high, jnp.where(is_low, dots - high, 0.0)).astype(BF)
    ys_ref[0] = (result * share).astype(BF)
    gated = (grads * share).astype(BF)
    gdy_ref[0] = gated
    dact = right_dot(gated, wd_ref[0])
    dpre = (dact * up * sigma * (1.0 + pre * (1.0 - sigma))).astype(BF)
    dup = (dact * silu).astype(BF)
    dg_ref[0] = dpre
    du_ref[0] = dup
    dx_ref[0, :, :features] = (right_dot(dpre, wg_ref[0]) + right_dot(dup, wu_ref[0])).astype(BF)


def expert_pass(rank, x_slots, dy_slots, w_gate, w_up, w_down):
    experts, rows, features = dy_slots.shape
    hidden = w_gate.shape[2]
    one = lambda e, r: (e, 0, 0)
    longer = pl.BlockSpec((1, rows, features + LANES), one)
    wide = pl.BlockSpec((1, rows, features), one)
    narrow = pl.BlockSpec((1, rows, hidden), one)
    shape = lambda width: jax.ShapeDtypeStruct((experts, rows, width), BF)
    return pl.pallas_call(
        expert_kernel,
        grid_spec=pltpu.PrefetchScalarGridSpec(
            num_scalar_prefetch=1,
            grid=(experts,),
            in_specs=[
                longer, wide,
                pl.BlockSpec((1, features, hidden), one),
                pl.BlockSpec((1, features, hidden), one),
                pl.BlockSpec((1, hidden, features), one),
            ],
            out_specs=[wide, longer, wide, narrow, narrow, narrow],
        ),
        out_shape=[
            shape(features), shape(features + LANES), shape(features), shape(hidden), shape(hidden), shape(hidden)
        ],
        compiler_params=params(),
        cost_estimate=cost(
            flops=12 * experts * rows * features * hidden,
            bytes_accessed=6 * experts * features * hidden + 10 * experts * rows * features,
            transcendentals=experts * rows * hidden,
        ),
        name="experts",
    )(rank, x_slots, dy_slots, w_gate, w_up, w_down)


def weight_kernel(count, products, step, core_ref, *refs):
    lefts, rights = refs[:count], refs[count : count * (1 + products)]
    outs, held_ref = refs[count * (1 + products) : -1], refs[-1]
    for i in range(products):
        total = sum(left_dot(lefts[m][0], rights[i * count + m][0]) for m in range(count))
        held_ref[...] = total.astype(BF)
        halves(core_ref, held_ref, step, outs[2 * i].at[0], outs[2 * i + 1].at[0])


def weight_pass(core, step, depth, lefts, *rights):
    experts, rows, width = rights[0][0].shape
    one = lambda e, s: (e, 0, 0)
    count, products = len(lefts), len(rights)
    half = jax.ShapeDtypeStruct((experts, depth // 2, width), BF)
    return pl.pallas_call(
        partial(weight_kernel, count, products, step),
        grid_spec=pltpu.PrefetchScalarGridSpec(
            num_scalar_prefetch=1,
            grid=(experts,),
            in_specs=[
                *[pl.BlockSpec((1, rows, depth), one) for _ in lefts],
                *[pl.BlockSpec((1, rows, width), one) for right in rights for _ in right],
            ],
            out_specs=[pl.BlockSpec((1, depth // 2, width), one)] * (2 * products),
            scratch_shapes=[pltpu.VMEM((depth, width), BF)],
        ),
        out_shape=[half] * (2 * products),
        compiler_params=params(),
        cost_estimate=cost(
            flops=2 * count * products * experts * rows * depth * width,
            bytes_accessed=2 * experts * (products * depth * width + count * rows * (depth + products * width)),
            transcendentals=0,
        ),
        name="expert_weights",
    )(core, *lefts, *[a for right in rights for a in right])


def fold_kernel(cut, step, place_ref, keep_ref, got_ref, *outs):
    x_place, y_place = place_ref[0], place_ref[1]

    def put(out_ref, slot, block):
        rows = pl.ds(pl.multiple_of(block * step, step), step)
        total = keep_ref[0, rows, :].astype(F32) + got_ref[0, rows, :].astype(F32)
        out_ref[0, slot * step : (slot + 1) * step, :] = total.astype(BF)

    first = pl.program_id(0) < cut

    @pl.when(first)
    def _():
        for y in range(2):
            put(outs[0], y, 2 * y + x_place)
            put(outs[1], y, 2 * y + 1 - x_place)

    @pl.when(jnp.logical_not(first))
    def _():
        for x in range(2):
            put(outs[2], x, 2 * y_place + x)
            put(outs[3], x, 2 * (1 - y_place) + x)


def fold(places, keep, got, tile=None):
    some, rows, width = keep.shape
    step = rows // 4
    count = some if tile is None else width // tile
    cut = (count + 1) // 2
    size = width if tile is None else tile
    place = (lambda i: (i, 0, 0)) if tile is None else (lambda i: (0, 0, i))
    block = lambda high, index: pl.BlockSpec((1, high, size), index)
    whole = block(rows, lambda i, s: place(i))
    one = block(2 * step, lambda i, s: place(jnp.minimum(i, cut - 1)))
    two = block(2 * step, lambda i, s: place(jnp.maximum(i - cut, 0)))
    shape = lambda n: jax.ShapeDtypeStruct(
        (n, 2 * step, width) if tile is None else (some, 2 * step, n * tile), BF
    )
    return pl.pallas_call(
        partial(fold_kernel, cut, step),
        grid_spec=pltpu.PrefetchScalarGridSpec(
            num_scalar_prefetch=1,
            grid=(count,),
            in_specs=[whole, whole],
            out_specs=[one, one, two, two],
        ),
        out_shape=[shape(cut), shape(cut), shape(count - cut), shape(count - cut)],
        compiler_params=params(),
        cost_estimate=cost(
            flops=some * rows * width, bytes_accessed=6 * some * rows * width, transcendentals=0
        ),
        name="fold",
    )(places, keep, got)


def fold_again_kernel(step, place_ref, keep_ref, got_ref, stay_ref, go_ref):
    for out_ref, half in ((stay_ref, place_ref[0]), (go_ref, 1 - place_ref[0])):
        rows = pl.ds(pl.multiple_of(half * step, step), step)
        total = keep_ref[0, rows, :].astype(F32) + got_ref[0, rows, :].astype(F32)
        out_ref[0] = total.astype(BF)


def fold_again(place, keep, got):
    some, rows, width = keep.shape
    step = rows // 2
    tile = width
    while tile * rows > 2**19 and tile % 2 == 0 and tile // 2 % LANES == 0:
        tile //= 2
    index = lambda i, j, s: (i, 0, j)
    return pl.pallas_call(
        partial(fold_again_kernel, step),
        grid_spec=pltpu.PrefetchScalarGridSpec(
            num_scalar_prefetch=1,
            grid=(some, width // tile),
            in_specs=[pl.BlockSpec((1, rows, tile), index)] * 2,
            out_specs=[pl.BlockSpec((1, step, tile), index)] * 2,
        ),
        out_shape=[jax.ShapeDtypeStruct((some, step, width), BF)] * 2,
        compiler_params=params(),
        cost_estimate=cost(
            flops=some * rows * width, bytes_accessed=6 * some * rows * width, transcendentals=0
        ),
        name="fold_again",
    )(place, keep, got)


def after(value, *marks):
    return lax.optimization_barrier((value, *marks))[0]


def together(*values):
    return lax.optimization_barrier(values)


def local(
    tokens, out_grad, routes, attn_gain, w_query, w_key, w_value, w_out, moe_gain, w_router,
    w_gate, w_up, w_down,
):
    micros, _, features = tokens.shape
    count = lax.axis_size("expert")
    rank = lax.axis_index("expert")
    exp_dev = w_gate.shape[0]
    dp = lax.axis_size("dp")
    core = (lax.axis_index("dp") % 2).astype(jnp.int32)[None]
    seq_blocks = SEQ // BLOCK
    place = rank % seq_blocks
    cosine, sine = rotary_tables(place * BLOCK + jnp.arange(BLOCK, dtype=jnp.int32))
    place = place.astype(jnp.int32)[None]
    around = [(i, (i + 1) % count) for i in range(count)]
    upward = [(i, i + 1) for i in range(count - 1) if (i + 1) % seq_blocks]
    downward = [(b, a) for a, b in upward]
    ring = lambda a: lax.ppermute(a, "expert", around)
    later = lambda a: lax.ppermute(a, "expert", upward)
    earlier = lambda a: lax.ppermute(a, "expert", downward)
    add = lambda a, b: (a.astype(F32) + b.astype(F32)).astype(BF)
    every = lambda a, axis: lax.all_gather(a, axis, axis=0, tiled=True)
    swap = lambda a: lax.ppermute(a, "dp", [(i, i ^ 1) for i in range(dp)])
    same_core = [list(range(c, dp, 2)) for c in range(2)]
    across = lambda a, bit: lax.ppermute(a, "dp", [(i, i ^ bit) for i in range(dp)])
    x_place, y_place = lax.axis_index("dp") // 2 % 2, lax.axis_index("dp") // 4
    square = dp == 8

    places = jnp.stack([x_place, y_place]).astype(jnp.int32)

    share = lambda a: lax.psum_scatter(a, "dp", scatter_dimension=1, axis_index_groups=same_core, tiled=True)

    def fold_first(keep, got, tile=None):
        return list(fold(places, keep, got, tile)) if square else [add(keep, got)]

    def send_first(parts):
        if not square:
            return parts
        one, one_sent, two, two_sent = parts
        return [one, across(one_sent, 2), two, across(two_sent, 4)]

    def halve_first(keep, got, tile=None):
        return send_first(fold_first(keep, got, tile))

    def halve_second(parts):
        if not square:
            return parts
        one, one_sent = fold_again(places[1:], *parts[:2])
        two, two_sent = fold_again(places[:1], *parts[2:])
        return [one, across(one_sent, 4), two, across(two_sent, 2)]

    def halve_last(parts, axis, dtype):
        if not square:
            return share(parts[0]).astype(dtype)
        total = lambda a, b: (a.astype(F32) + b.astype(F32)).astype(dtype)
        return jnp.concatenate([total(*parts[:2]), total(*parts[2:])], axis=axis)

    beside = jnp.zeros((w_router.shape[0], LANES - EXPERTS - 2), BF)
    weights = every(
        jnp.concatenate(
            [w_query, w_out, w_key, w_value, w_router, attn_gain[:, None], moe_gain[:, None], beside], axis=1
        ),
        "dp",
    )
    behind = QD + features + 2 * KD

    members = jnp.any(routes[:, :, :, None] == jnp.arange(EXPERTS, dtype=jnp.int32), axis=2)
    before = jnp.tril(jnp.ones((BLOCK, BLOCK), F32), -1).astype(BF)
    slots = jnp.einsum("ts,mse->mte", before, members.astype(BF), preferred_element_type=F32)
    slots = jnp.where(members, slots, -1.0).astype(BF)
    dy_sent = jnp.concatenate([out_grad, slots, jnp.zeros((micros, BLOCK, LANES - EXPERTS), BF)], axis=2)

    dy_ring = [dy_sent]
    for _ in range(count - 2):
        dy_ring.append(ring(dy_ring[-1]))
    router_w = weights[:, behind:]
    gains = router_w[:, EXPERTS : EXPERTS + 2].T.astype(F32)
    gain_one, gain_two = gains[0:1], gains[1:2]
    x_whole = tokens.reshape(micros * BLOCK, features)
    normed, scale_one = norm_rows(x_whole, gain_one)
    normed = after(normed, dy_ring[-1])
    kv_own = project(normed, weights, QD + features, 2 * KD, KD, cosine, sine)
    kv_one = [kv_own[0]]
    for _ in range(seq_blocks - 1):
        kv_one.append(later(kv_one[-1]))
    while len(dy_ring) < count:
        dy_ring.append(ring(dy_ring[-1]))
    kv_one[-1], dy_ring[-1] = together(kv_one[-1], dy_ring[-1])

    kv_two = [after(kv_own[1], kv_one[-1])]
    kv_two.append(later(kv_two[-1]))
    queries = list(project(after(normed, kv_one[-1]), weights, 0, QD, QD, cosine, sine))
    kv_two[-1], queries[0] = together(kv_two[-1], queries[0])
    kv_two.append(later(kv_two[-1]))
    o_one, ob_one, lse_one = attend(place, queries[0], kv_one)
    kv_two[-1], ob_one = together(kv_two[-1], ob_one)
    kv_two.append(later(kv_two[-1]))
    go_out = lambda m, ob: outward(ob, weights, tokens[m], gain_two, router_w, routes[m])
    mids = [list(go_out(0, ob_one))]
    sent = [every(mids[0][1], "expert")]
    kv_two[-1], mids[0][1] = together(kv_two[-1], mids[0][1])
    while len(kv_two) < seq_blocks:
        kv_two.append(later(kv_two[-1]))
    o_two, ob_two, lse_two = attend(place, queries[1], kv_two)
    mids.append(list(go_out(1, ob_two)))
    sent.append(every(mids[1][1], "expert"))
    kvs = (kv_one, kv_two)
    heads = ((o_one, ob_one, lse_one), (o_two, ob_two, lse_two))

    def in_order(m):
        whole = jnp.zeros((count * BLOCK, features + LANES), BF)
        for step, block in enumerate(dy_ring):
            whole = lax.dynamic_update_slice_in_dim(whole, block[m], (rank - step) % count * BLOCK, 0)
        return whole

    parts, slot_rows, scaled, dx_sums, dx_home = [], [], [], [], []
    for m in range(micros):
        dy_all = in_order(m)
        table = lax.dynamic_slice_in_dim(dy_all, features + rank * exp_dev, exp_dev, 1)
        slot_rows.append(table.astype(F32).T)
        dy_slots = dispatch(slot_rows[m], dy_all, features)
        if m > 0:
            mixture_sums = combine(slot_rows[0], after(scaled[0], dx_sums[0]))
            sent[m], dy_slots, dx_sums[-1], mixture_sums = together(sent[m], dy_slots, dx_sums[-1], mixture_sums)
        x_slots = dispatch(slot_rows[m], sent[m], features + LANES)
        ys, dx, *rest = expert_pass(rank.astype(jnp.int32)[None], x_slots, dy_slots, w_gate, w_up, w_down)
        parts.append((x_slots, *rest))
        scaled.append(ys)
        dx_sums.append(combine(slot_rows[m], dx))
    ring_block = lambda sums, j: lax.dynamic_slice_in_dim(sums, (rank - 1 - j) % count * BLOCK, BLOCK, 0)
    dx_home = [lax.psum_scatter(dx_sums[0], "expert", scatter_dimension=0, tiled=True)]

    xs, gdys, acts, dgs, dus = zip(*parts)
    hidden = w_down.shape[1]
    first_act, dx_home[0], dx_sums[1] = together(acts[0], dx_home[0], dx_sums[1])
    dx_held = ring(ring_block(dx_sums[1], 0))
    keep_down, send_down = weight_pass(core, hidden // dp, hidden, (first_act, *acts[1:]), gdys)
    dx_held, keep_down, send_down = together(dx_held, keep_down, send_down)
    got_down = swap(send_down)
    dx_held = ring(add(dx_held, ring_block(dx_sums[1], 1)))
    dgs = after(dgs[0], keep_down), *dgs[1:]
    ups = weight_pass(core, features // dp, features, xs, dgs, dus)
    held = ring(ring_block(after(mixture_sums, keep_down), 0))
    dx_held, got_down, *ups = together(dx_held, got_down, *ups)
    for step in range(2, count - 1):
        dx_held = ring(add(dx_held, ring_block(dx_sums[1], step)))
    down_half = add(keep_down, got_down)
    held, down_half = together(held, down_half)
    held = ring(add(held, ring_block(mixture_sums, 1)))
    down_grad = share(down_half)
    got_gate, got_up = swap(ups[1]), swap(ups[3])

    def back_home(m, dx):
        mid, _, scale_two, gates = mids[m]
        return home_back(dx, gates, mid, scale_two, out_grad[m], router_w, gain_two, weights)

    def back_heads(m, dob):
        o, _, lse = heads[m]
        dq, *pieces = attend_back(place, queries[m], dob, o, lse, cosine, sine, kvs[m])
        return dq, pieces[::-1]

    first = list(back_home(0, after(dx_home[0], down_half)))
    dq_one, far_one = back_heads(0, first[2])
    dx_held, held, got_gate, got_up, dq_one = together(dx_held, held, got_gate, got_up, dq_one)
    dx_home.append(add(dx_held, ring_block(dx_sums[1], count - 1)))
    for step in range(2, count - 1):
        held = ring(add(held, ring_block(mixture_sums, step)))
    up_half = add(ups[2], got_up)
    up_grad = share(up_half)
    back_one = earlier(far_one[0])
    second = list(back_home(1, after(dx_home[1], up_half, dq_one)))
    back_one, second[2] = together(back_one, second[2])
    back_one = earlier(add(back_one, far_one[1]))
    dq_two, far_two = back_heads(1, second[2])
    back_one, dq_two, far_two[0], held, down_grad = together(back_one, dq_two, far_two[0], held, down_grad)
    for piece in far_one[2:-1]:
        back_one = earlier(add(back_one, piece))
    back_two = earlier(far_two[0])
    mixtures = [add(held, ring_block(mixture_sums, count - 1))]
    gate_half = add(after(ups[0], dq_two), got_gate)
    gate_grad = share(gate_half)
    back_one = add(back_one, far_one[-1])

    def back_last(m, dq, dkv, dmid):
        return last_back(
            dq, dkv, cosine, sine, weights, weights, tokens[m], scale_one[m * BLOCK : (m + 1) * BLOCK], gain_one, dmid
        )

    back_two, back_one = together(back_two, back_one, gate_half)[:2]
    back_two = earlier(add(back_two, far_two[1]))
    grad_x_one, dkv_one, dgain_one = back_last(0, dq_one, back_one, first[0])
    back_two, dkv_one = together(back_two, dkv_one)
    for piece in far_two[2:-1]:
        back_two = earlier(add(back_two, piece))
    back_two = add(back_two, far_two[-1])
    grad_x_two, dkv_two, dgain_two = back_last(1, dq_two, back_two, second[0])
    gain_rows = jnp.concatenate([dgain_one + dgain_two, first[4] + second[4]], axis=0)
    gain_columns = jnp.pad(gain_rows.T, ((0, 0), (EXPERTS, LANES - EXPERTS - 2)))
    keep, send = dense_grads(
        core, features // dp, [normed] * micros, [dq_one, dq_two], [dkv_one, dkv_two], [k[1] for k in mids],
        [first[3], second[3]], [h[1] for h in heads], [first[1], second[1]], gain_columns,
    )
    got = swap(send)
    mixture_sums = combine(slot_rows[1], after(scaled[1], keep))
    got, mixture_sums = together(got, mixture_sums)
    dense_sums = halve_first(keep[None], got[None], 3 * LANES)
    held = ring(ring_block(after(mixture_sums, dense_sums[0]), 0))
    held = ring(add(held, ring_block(mixture_sums, 1)))
    held, *dense_sums = together(held, *dense_sums)
    dense_sums = halve_second(dense_sums)
    held = after(held, *dense_sums[::2])
    for step in range(2, count - 1):
        held = ring(add(held, ring_block(mixture_sums, step)))
    held, gate_grad, up_grad, *dense_sums = together(held, gate_grad, up_grad, *dense_sums)
    mixtures.append(add(held, ring_block(mixture_sums, count - 1)))
    dense_sum = halve_last(dense_sums, 2, BF)[0]
    gate_grad, up_grad, down_grad = gate_grad.astype(F32), up_grad.astype(F32), down_grad.astype(F32)
    dense = lax.psum(dense_sum, "expert").astype(F32)
    columns = lambda start, width: dense[:, start : start + width]
    small = QD + 2 * KD

    mixed = [(mids[m][0] + mixtures[m].astype(F32)).astype(BF) for m in range(micros)]
    return (
        jnp.stack(mixed),
        jnp.stack([grad_x_one, grad_x_two]),
        dense[:, small + EXPERTS],
        columns(0, QD),
        columns(QD, KD),
        columns(QD + KD, KD),
        columns(small + LANES, features),
        dense[:, small + EXPERTS + 1],
        columns(small, EXPERTS),
        gate_grad,
        up_grad,
        down_grad,
    )


def solution(mesh):
    rows = P(None, ("dp", "expert"), None)
    return jax.shard_map(
        local,
        mesh=mesh,
        in_specs=(
            rows, rows, rows, P("dp"), P("dp", None), P("dp", None), P("dp", None), P("dp", None),
            P("dp"), P("dp", None),
            P("expert", None, None), P("expert", None, None), P("expert", None, None),
        ),
        out_specs=(
            rows, rows, P("dp"), P("dp", None), P("dp", None), P("dp", None), P("dp", None),
            P("dp"), P("dp", None),
            P("expert", "dp", None), P("expert", "dp", None), P("expert", "dp", None),
        ),
        check_vma=False,
    )
```

```python
from functools import partial

import jax
import jax.numpy as jnp
from jax import lax
from jax.experimental import pallas as pl
from jax.experimental.pallas import tpu as pltpu
from jax.sharding import PartitionSpec as P

HEADS = 24
KV_HEADS = 8
HEAD = 64
FF = 512
EXPERTS = 40
TOP = 8
BLOCK = 256
SEQ = 1024
CAP = 64
QD = 1536
KD = 512

EPSILON = 1e-06
ROPE_BASE = 10000.0
NEGATIVE = -1e30
LANES = 128
COLUMNS = 256
VMEM_LIMIT = 56 * 2**20
COST_SCALE = 0.1

BF = jnp.bfloat16
F32 = jnp.float32


def dense_dot(left, right):
    return jnp.dot(left, right, preferred_element_type=F32)


def left_dot(left, right):
    return lax.dot_general(left, right, (((0,), (0,)), ((), ())), preferred_element_type=F32)


def right_dot(left, right):
    return lax.dot_general(left, right, (((1,), (1,)), ((), ())), preferred_element_type=F32)


def rotary_tables(positions):
    half_size = HEAD // 2
    frequency = ROPE_BASE ** (-jnp.arange(half_size, dtype=F32) / half_size)
    angle = positions.astype(F32)[:, None] * frequency[None, :]
    cosine, sine = jnp.cos(angle), jnp.sin(angle)
    tiles = LANES // HEAD
    return (
        jnp.concatenate([cosine, cosine] * tiles, axis=1),
        jnp.concatenate([-sine, sine] * tiles, axis=1),
    )


def cost(flops, bytes_accessed, transcendentals):
    scale = lambda n: int(n * COST_SCALE)
    return pl.CostEstimate(
        flops=scale(flops), bytes_accessed=scale(bytes_accessed), transcendentals=scale(transcendentals)
    )


def params(limit=VMEM_LIMIT):
    return pltpu.CompilerParams(vmem_limit_bytes=limit)


def swap_halves(values):
    lane = lax.broadcasted_iota(jnp.int32, values.shape, 1)
    half = HEAD // 2
    return jnp.where(
        lane % HEAD < half,
        pltpu.roll(values, LANES - half, 1),
        pltpu.roll(values, half, 1),
    )


def turn(values, cosine, sine):
    return values * cosine + swap_halves(values) * sine


def norm_kernel(x_ref, gain_ref, normed_ref, scale_ref):
    rows = x_ref[...].astype(F32)
    scale = lax.rsqrt(jnp.mean(rows * rows, axis=1, keepdims=True) + EPSILON)
    scale_ref[...] = scale
    normed_ref[...] = (rows * scale * gain_ref[...]).astype(BF)


def norm_rows(x, gain):
    total, features = x.shape
    return pl.pallas_call(
        norm_kernel,
        grid=(total // BLOCK,),
        in_specs=[
            pl.BlockSpec((BLOCK, features), lambda i: (i, 0)),
            pl.BlockSpec((1, features), lambda i: (0, 0)),
        ],
        out_specs=[
            pl.BlockSpec((BLOCK, features), lambda i: (i, 0)),
            pl.BlockSpec((BLOCK, 1), lambda i: (i, 0)),
        ],
        out_shape=[
            jax.ShapeDtypeStruct((total, features), BF),
            jax.ShapeDtypeStruct((total, 1), F32),
        ],
        compiler_params=params(),
        cost_estimate=cost(flops=5 * total * features, bytes_accessed=4 * total * features, transcendentals=0),
        name="norm",
    )(x, gain)


def project_kernel(turned, normed_ref, w_ref, cosine_ref, sine_ref, *outs):
    tile = w_ref.shape[1]
    rows = dense_dot(normed_ref[...], w_ref[...])

    def write(turning):
        for start in range(0, tile, LANES):
            for m, out_ref in enumerate(outs):
                part = rows[m * BLOCK : (m + 1) * BLOCK, start : start + LANES]
                if turning:
                    part = turn(part, cosine_ref[...], sine_ref[...])
                out_ref[:, start : start + LANES] = part.astype(BF)

    pl.when(pl.program_id(0) < turned)(lambda: write(True))
    pl.when(pl.program_id(0) >= turned)(lambda: write(False))


def project(normed, weight, start, columns, turned_columns, cosine, sine):
    total, features = normed.shape
    tile = 2 * COLUMNS
    micros = total // BLOCK
    return pl.pallas_call(
        partial(project_kernel, turned_columns // tile),
        grid=(columns // tile,),
        in_specs=[
            pl.BlockSpec((total, features), lambda j: (0, 0)),
            pl.BlockSpec((features, tile), lambda j: (0, start // tile + j)),
            pl.BlockSpec((BLOCK, LANES), lambda j: (0, 0)),
            pl.BlockSpec((BLOCK, LANES), lambda j: (0, 0)),
        ],
        out_specs=[pl.BlockSpec((BLOCK, tile), lambda j: (0, j))] * micros,
        out_shape=[jax.ShapeDtypeStruct((BLOCK, columns), BF)] * micros,
        compiler_params=params(),
        cost_estimate=cost(
            flops=2 * total * features * columns,
            bytes_accessed=2 * (features * columns + total * (features + columns)),
            transcendentals=0,
        ),
        name="project",
    )(normed, weight, cosine, sine)


def outward_kernel(ob_ref, w_ref, x_ref, gain_ref, router_ref, routes_ref, mid_ref, sent_ref, scale_ref, gates_ref):
    j = pl.program_id(0)
    tile = w_ref.shape[1]
    features = mid_ref.shape[1]
    where = pl.ds(pl.multiple_of(j * tile, tile), tile)
    mid_ref[:, where] = x_ref[:, where].astype(F32) + dense_dot(ob_ref[...], w_ref[...])

    @pl.when(j == pl.num_programs(0) - 1)
    def _():
        mid = mid_ref[...]
        scale = lax.rsqrt(jnp.mean(mid * mid, axis=1, keepdims=True) + EPSILON)
        scale_ref[...] = scale
        normed = (mid * scale * gain_ref[...]).astype(BF)
        sent_ref[:, :features] = normed
        lane = lax.broadcasted_iota(jnp.int32, (BLOCK, LANES), 1)
        routes = routes_ref[...]
        member = lane == routes[:, 0:1]
        for k in range(1, TOP):
            member = jnp.logical_or(member, lane == routes[:, k : k + 1])
        logits = jnp.where(member, dense_dot(normed, router_ref[...]), NEGATIVE)
        weights = jnp.exp(logits - jnp.max(logits, axis=1, keepdims=True))
        weights = jnp.where(member, weights, 0.0)
        gates = weights / jnp.sum(weights, axis=1, keepdims=True)
        gates_ref[...] = gates
        high = gates.astype(BF).astype(F32)
        sent_ref[:, features:] = (high + pltpu.roll(gates - high, EXPERTS, 1)).astype(BF)


def outward(ob, w_qo, x, gain, router, routes):
    features = x.shape[1]
    tile = 2 * COLUMNS
    whole = lambda a: pl.BlockSpec(a.shape, lambda j: (0, 0))
    fixed = lambda *shape: pl.BlockSpec(shape, lambda j: (0, 0))
    return pl.pallas_call(
        outward_kernel,
        grid=(features // tile,),
        in_specs=[
            whole(ob),
            pl.BlockSpec((QD, tile), lambda j: (0, QD // tile + j)),
            whole(x), whole(gain), whole(router), whole(routes),
        ],
        out_specs=[fixed(BLOCK, features), fixed(BLOCK, features + LANES), fixed(BLOCK, 1), fixed(BLOCK, LANES)],
        out_shape=[
            jax.ShapeDtypeStruct((BLOCK, features), F32),
            jax.ShapeDtypeStruct((BLOCK, features + LANES), BF),
            jax.ShapeDtypeStruct((BLOCK, 1), F32),
            jax.ShapeDtypeStruct((BLOCK, LANES), F32),
        ],
        compiler_params=params(),
        cost_estimate=cost(
            flops=2 * BLOCK * features * QD, bytes_accessed=2 * features * QD + 14 * BLOCK * features, transcendentals=0
        ),
        name="outward",
    )(ob, w_qo, x, gain, router, routes)


def home_kernel(
    dx_ref, gates_ref, mid_ref, scale_ref, dy_ref, router_ref, gain_ref, w_ref,
    dmid_ref, da_ref, dob_ref, dlog_ref, dgain_ref,
):
    j = pl.program_id(0)
    features = mid_ref.shape[1]
    tile = w_ref.shape[0]

    @pl.when(j == 0)
    def _():
        table = dx_ref[:, features:].astype(F32)
        dgates = table + pltpu.roll(table, LANES - EXPERTS, 1)
        gates = gates_ref[...]
        dc = gates * (dgates - jnp.sum(gates * dgates, axis=1, keepdims=True))
        dlog = dc.astype(BF)
        dlog_ref[...] = dlog
        dnormed = dx_ref[:, :features].astype(F32) + right_dot(dlog, router_ref[...])
        mid = mid_ref[...]
        scale = scale_ref[...]
        dgain_ref[...] = jnp.sum(dnormed * mid * scale, axis=0, keepdims=True)
        scaled = dnormed * gain_ref[...]
        mean = jnp.mean(scaled * mid, axis=1, keepdims=True)
        dmid = dy_ref[...].astype(F32) + scale * scaled - mid * (scale * scale * scale * mean)
        dmid_ref[...] = dmid
        da_ref[...] = dmid.astype(BF)

    where = pl.ds(pl.multiple_of(j * tile, tile), tile)
    dob_ref[:, where] = right_dot(da_ref[...], w_ref[...]).astype(BF)


def home_back(dx, gates, mid, scale, dy, router, gain, w_qo):
    features = mid.shape[1]
    tile = 2 * COLUMNS
    whole = lambda a: pl.BlockSpec(a.shape, lambda j: (0, 0))
    fixed = lambda *shape: pl.BlockSpec(shape, lambda j: (0, 0))
    return pl.pallas_call(
        home_kernel,
        grid=(QD // tile,),
        in_specs=[
            whole(dx), whole(gates), whole(mid), whole(scale), whole(dy), whole(router), whole(gain),
            pl.BlockSpec((tile, features), lambda j: (j, 1)),
        ],
        out_specs=[
            fixed(BLOCK, features), fixed(BLOCK, features), fixed(BLOCK, QD), fixed(BLOCK, LANES), fixed(1, features),
        ],
        out_shape=[
            jax.ShapeDtypeStruct((BLOCK, features), F32),
            jax.ShapeDtypeStruct((BLOCK, features), BF),
            jax.ShapeDtypeStruct((BLOCK, QD), BF),
            jax.ShapeDtypeStruct((BLOCK, LANES), BF),
            jax.ShapeDtypeStruct((1, features), F32),
        ],
        compiler_params=params(),
        cost_estimate=cost(
            flops=2 * BLOCK * features * QD, bytes_accessed=2 * features * QD + 18 * BLOCK * features, transcendentals=0
        ),
        name="home_back",
    )(dx, gates, mid, scale, dy, router, gain, w_qo)


def last_kernel(
    dq_ref, dkv_ref, cosine_ref, sine_ref, wq_ref, wkv_ref, x_ref, scale_ref, gain_ref, dmid_ref,
    dx_ref, dkvb_ref, dgain_ref,
):
    j = pl.program_id(0)
    tile = wq_ref.shape[0]

    @pl.when(j == 0)
    def _():
        for start in range(0, KD, LANES):
            part = dkv_ref[0, :, start : start + LANES].astype(F32)
            dkvb_ref[:, start : start + LANES] = turn(part, cosine_ref[...], -sine_ref[...]).astype(BF)
        dkvb_ref[:, KD:] = dkv_ref[1]

    where = pl.ds(pl.multiple_of(j * tile, tile), tile)
    dx_ref[:, where] = right_dot(dq_ref[...], wq_ref[...]) + right_dot(dkvb_ref[...], wkv_ref[...])

    @pl.when(j == pl.num_programs(0) - 1)
    def _():
        dnormed = dx_ref[...]
        rows = x_ref[...].astype(F32)
        scale = scale_ref[...]
        dgain_ref[...] = jnp.sum(dnormed * rows * scale, axis=0, keepdims=True)
        scaled = dnormed * gain_ref[...]
        mean = jnp.mean(scaled * rows, axis=1, keepdims=True)
        dx_ref[...] = dmid_ref[...] + scale * scaled - rows * (scale * scale * scale * mean)


def last_back(dq, dkv, cosine, sine, w_q, w_kv, x, scale, gain, dmid):
    features = x.shape[1]
    tile = 2 * COLUMNS
    whole = lambda a: pl.BlockSpec(a.shape, lambda j: (0,) * a.ndim)
    fixed = lambda *shape: pl.BlockSpec(shape, lambda j: (0, 0))
    return pl.pallas_call(
        last_kernel,
        grid=(features // tile,),
        in_specs=[
            whole(dq), whole(dkv), whole(cosine), whole(sine),
            pl.BlockSpec((tile, QD), lambda j: (j, 0)),
            pl.BlockSpec((tile, 2 * KD), lambda j: (j, QD // KD)),
            whole(x), whole(scale), whole(gain), whole(dmid),
        ],
        out_specs=[fixed(BLOCK, features), fixed(BLOCK, 2 * KD), fixed(1, features)],
        out_shape=[
            jax.ShapeDtypeStruct((BLOCK, features), F32),
            jax.ShapeDtypeStruct((BLOCK, 2 * KD), BF),
            jax.ShapeDtypeStruct((1, features), F32),
        ],
        compiler_params=params(),
        cost_estimate=cost(
            flops=2 * BLOCK * features * (QD + 2 * KD),
            bytes_accessed=2 * features * (QD + 2 * KD) + 16 * BLOCK * features,
            transcendentals=0,
        ),
        name="last_back",
    )(dq, dkv, cosine, sine, w_q, w_kv, x, scale, gain, dmid)


def halves(core_ref, held_ref, step, keep_ref, send_ref):
    core = core_ref[0]
    for q in range(held_ref.shape[0] // (2 * step)):
        mine = pl.multiple_of((2 * q + core) * step, step)
        other = pl.multiple_of((2 * q + 1 - core) * step, step)
        keep_ref[q * step : (q + 1) * step, :] = held_ref[pl.ds(mine, step), :]
        send_ref[q * step : (q + 1) * step, :] = held_ref[pl.ds(other, step), :]


def dense_kernel(micros, step, core_ref, *refs):
    ins, (gains_ref, keep_ref, send_ref, held_ref) = refs[: 7 * micros], refs[7 * micros :]
    normed, dq, dkv, sent, dlog, ob, da = (ins[i * micros : (i + 1) * micros] for i in range(7))

    def total(lefts, rights):
        return sum(left_dot(left[...], right[...]) for left, right in zip(lefts, rights))

    start = 0
    for lefts, rights in ((normed, dq), (normed, dkv), (sent, dlog), (ob, da)):
        width = rights[0].shape[1]
        part = total(lefts, rights)
        if rights is dlog:
            part = part + gains_ref[...]
        held_ref[:, start : start + width] = part.astype(BF)
        start += width
    halves(core_ref, held_ref, step, keep_ref, send_ref)


def dense_grads(core, step, normed, dq, dkv, sent, dlog, ob, da, gains):
    groups = (normed, dq, dkv, sent, dlog, ob, da)
    micros = len(dq)
    tile = max(3 * LANES, 2 * step)
    lefts = (True, False, False, True, False, True, False)
    width = sum(group[0].shape[1] for group, left in zip(groups, lefts) if not left)
    specs = []
    for group, left in zip(groups, lefts):
        for m, a in enumerate(group):
            if left:
                block = m if a.shape[0] > BLOCK else 0
                specs.append(pl.BlockSpec((BLOCK, tile), lambda j, s, block=block: (block, j)))
            else:
                specs.append(pl.BlockSpec(a.shape, lambda j, s: (0, 0)))
    half = jax.ShapeDtypeStruct((QD // 2, width), BF)
    return pl.pallas_call(
        partial(dense_kernel, micros, step),
        grid_spec=pltpu.PrefetchScalarGridSpec(
            num_scalar_prefetch=1,
            grid=(QD // tile,),
            in_specs=[*specs, pl.BlockSpec((tile, gains.shape[1]), lambda j, s: (j, 0))],
            out_specs=[pl.BlockSpec((tile // 2, width), lambda j, s: (j, 0))] * 2,
            scratch_shapes=[pltpu.VMEM((tile, width), BF)],
        ),
        out_shape=[half, half],
        compiler_params=params(),
        cost_estimate=cost(
            flops=2 * micros * BLOCK * QD * width,
            bytes_accessed=2 * QD * width + 4 * micros * BLOCK * (QD + width),
            transcendentals=0,
        ),
        name="dense_grads",
    )(core, *[a for group in groups for a in group], gains)


PAIR = 2 * HEAD
GROUP = HEADS // KV_HEADS * PAIR


def spread(values):
    lane = lax.broadcasted_iota(jnp.int32, (BLOCK, LANES), 1)
    first = lane < HEAD
    zero = jnp.zeros((BLOCK, LANES), F32)
    one, two, three = (values[:, i * LANES : (i + 1) * LANES] for i in range(3))
    return jnp.concatenate(
        [
            jnp.where(first, one, zero),
            jnp.where(first, pltpu.roll(one, HEAD, 1), zero),
            jnp.where(first, two, zero),
            jnp.where(first, zero, two),
            jnp.where(first, zero, pltpu.roll(three, HEAD, 1)),
            jnp.where(first, zero, three),
        ],
        axis=0,
    )


def gather_heads(rows):
    lane = lax.broadcasted_iota(jnp.int32, (BLOCK, LANES), 1)
    first = lane < HEAD
    part = [rows[i * BLOCK : (i + 1) * BLOCK] for i in range(6)]
    return (
        jnp.where(first, part[0], pltpu.roll(part[1], HEAD, 1)),
        jnp.where(first, part[2], part[3]),
        jnp.where(first, pltpu.roll(part[4], HEAD, 1), part[5]),
    )


def attend_kernel(place_ref, q_ref, *refs):
    blocks = SEQ // BLOCK
    keys, values = refs[:blocks], refs[blocks : 2 * blocks]
    o_ref, ob_ref, lse_ref, max_ref, sum_ref, acc_ref = refs[2 * blocks :]
    query = spread(q_ref[...].astype(F32) * HEAD ** (-0.5)).astype(BF)
    for r in range(blocks):

        @pl.when(place_ref[0] >= r)
        def _():
            scores = right_dot(keys[r][...], query)
            top = jnp.max(scores, axis=0, keepdims=True)
            if r > 0:
                before = max_ref[...]
                top = jnp.maximum(top, before)
            weights = jnp.exp(scores - top)
            total = jnp.sum(weights, axis=0, keepdims=True)
            out = left_dot(values[r][...], weights.astype(BF))
            if r > 0:
                factor = jnp.exp(before - top)
                total = total + sum_ref[...] * factor
                out = out + acc_ref[...] * factor
            max_ref[...] = top
            sum_ref[...] = total
            acc_ref[...] = out

    lse_ref[0] = max_ref[...] + jnp.log(sum_ref[...])
    rows = jnp.transpose(acc_ref[...] / sum_ref[...])
    for i, part in enumerate(gather_heads(rows)):
        o_ref[:, i * LANES : (i + 1) * LANES] = part
        ob_ref[:, i * LANES : (i + 1) * LANES] = part.astype(BF)


def attend(place, query, kvs):
    pairs = KV_HEADS // 2
    rows = 6 * BLOCK
    return pl.pallas_call(
        attend_kernel,
        grid_spec=pltpu.PrefetchScalarGridSpec(
            num_scalar_prefetch=1,
            grid=(pairs,),
            in_specs=[
                pl.BlockSpec((BLOCK, GROUP), lambda p, s: (0, p)),
                *[pl.BlockSpec((BLOCK, PAIR), lambda p, s: (0, p)) for _ in kvs],
                *[pl.BlockSpec((BLOCK, PAIR), lambda p, s: (0, KV_HEADS // 2 + p)) for _ in kvs],
            ],
            out_specs=[
                pl.BlockSpec((BLOCK, GROUP), lambda p, s: (0, p)),
                pl.BlockSpec((BLOCK, GROUP), lambda p, s: (0, p)),
                pl.BlockSpec((1, 1, rows), lambda p, s: (p, 0, 0)),
            ],
            scratch_shapes=[
                pltpu.VMEM((1, rows), F32),
                pltpu.VMEM((1, rows), F32),
                pltpu.VMEM((PAIR, rows), F32),
            ],
        ),
        out_shape=[
            jax.ShapeDtypeStruct((BLOCK, QD), F32),
            jax.ShapeDtypeStruct((BLOCK, QD), BF),
            jax.ShapeDtypeStruct((pairs, 1, rows), F32),
        ],
        compiler_params=params(),
        cost_estimate=cost(
            flops=8 * SEQ * BLOCK * HEADS * PAIR, bytes_accessed=10 * BLOCK * QD, transcendentals=SEQ * BLOCK * HEADS
        ),
        name="attend",
    )(place, query, *kvs, *kvs)


def attend_back_kernel(place_ref, q_ref, dob_ref, o_ref, lse_ref, cosine_ref, sine_ref, *refs):
    blocks = SEQ // BLOCK
    keys, values = refs[:blocks], refs[blocks : 2 * blocks]
    dq_ref, outs, acc_ref = refs[2 * blocks], refs[2 * blocks + 1 : 3 * blocks + 1], refs[-1]
    query = spread(q_ref[...].astype(F32) * HEAD ** (-0.5)).astype(BF)
    grads = spread(dob_ref[...].astype(F32))
    delta = jnp.sum(jnp.transpose(grads * spread(o_ref[...])), axis=0, keepdims=True)
    grads = grads.astype(BF)
    for r in range(blocks):

        @pl.when(place_ref[0] >= r)
        def _():
            key = keys[r][...]
            weights = jnp.exp(right_dot(key, query) - lse_ref[0])
            dscores = (weights * (right_dot(values[r][...], grads) - delta)).astype(BF)
            outs[r][0] = dense_dot(dscores, query).astype(BF)
            outs[r][1] = dense_dot(weights.astype(BF), grads).astype(BF)
            part = left_dot(key, dscores)
            acc_ref[...] = part if r == 0 else acc_ref[...] + part

        @pl.when(place_ref[0] < r)
        def _():
            outs[r][...] = jnp.zeros(outs[r].shape, BF)

    rows = jnp.transpose(acc_ref[...]) * HEAD ** (-0.5)
    for i, part in enumerate(gather_heads(rows)):
        dq_ref[:, i * LANES : (i + 1) * LANES] = turn(part, cosine_ref[...], -sine_ref[...]).astype(BF)


def attend_back(place, query, dob, o, lse, cosine, sine, kvs):
    pairs = KV_HEADS // 2
    rows = 6 * BLOCK
    heads = pl.BlockSpec((BLOCK, GROUP), lambda p, s: (0, p))
    table = pl.BlockSpec((BLOCK, LANES), lambda p, s: (0, 0))
    return pl.pallas_call(
        attend_back_kernel,
        grid_spec=pltpu.PrefetchScalarGridSpec(
            num_scalar_prefetch=1,
            grid=(pairs,),
            in_specs=[
                heads, heads, heads,
                pl.BlockSpec((1, 1, rows), lambda p, s: (p, 0, 0)),
                table, table,
                *[pl.BlockSpec((BLOCK, PAIR), lambda p, s: (0, p)) for _ in kvs],
                *[pl.BlockSpec((BLOCK, PAIR), lambda p, s: (0, KV_HEADS // 2 + p)) for _ in kvs],
            ],
            out_specs=[heads, *[pl.BlockSpec((2, BLOCK, PAIR), lambda p, s: (0, 0, p)) for _ in kvs]],
            scratch_shapes=[pltpu.VMEM((PAIR, rows), F32)],
        ),
        out_shape=[
            jax.ShapeDtypeStruct((BLOCK, QD), BF),
            *[jax.ShapeDtypeStruct((2, BLOCK, KD), BF) for _ in kvs],
        ],
        compiler_params=params(),
        cost_estimate=cost(
            flops=20 * SEQ * BLOCK * HEADS * PAIR, bytes_accessed=14 * BLOCK * QD, transcendentals=SEQ * BLOCK * HEADS
        ),
        name="attend_back",
    )(place, query, dob, o, lse, cosine, sine, *kvs, *kvs)


def picks(slot_rows):
    slots = lax.broadcasted_iota(jnp.int32, (CAP, BLOCK), 0).astype(F32)
    one, zero = jnp.float32(1), jnp.float32(0)
    return [jnp.where(slots == slot_rows[e : e + 1, :], one, zero) for e in range(slot_rows.shape[0])]


def dispatch_kernel(slot_ref, rows_ref, out_ref):
    experts = slot_ref.shape[0]
    chosen = jnp.concatenate([p.astype(BF) for p in picks(slot_ref[...])], axis=0)
    width = out_ref.shape[2]
    for start in range(0, width, COLUMNS):
        size = min(COLUMNS, width - start)
        rows = dense_dot(chosen, rows_ref[:, start : start + size])
        out_ref[:, :, start : start + size] = rows.astype(BF).reshape(experts, CAP, size)


def dispatch(slot_rows, rows, features):
    experts, total = slot_rows.shape
    blocks = total // BLOCK
    return pl.pallas_call(
        dispatch_kernel,
        grid=(blocks,),
        in_specs=[
            pl.BlockSpec((experts, BLOCK), lambda b: (0, b)),
            pl.BlockSpec((BLOCK, features), lambda b: (b, 0)),
        ],
        out_specs=pl.BlockSpec((experts, CAP, features), lambda b: (0, b, 0)),
        out_shape=jax.ShapeDtypeStruct((experts, blocks * CAP, features), BF),
        compiler_params=params(),
        cost_estimate=cost(
            flops=2 * experts * CAP * total * features,
            bytes_accessed=2 * features * (total + experts * blocks * CAP),
            transcendentals=0,
        ),
        name="dispatch",
    )(slot_rows, rows)


def combine_kernel(slot_ref, slots_ref, out_ref):
    experts, features = slots_ref.shape[0], slots_ref.shape[2]
    chosen = jnp.concatenate([p.astype(BF) for p in picks(slot_ref[...])], axis=0)
    for start in range(0, features, COLUMNS):
        size = min(COLUMNS, features - start)
        held = slots_ref[:, :, start : start + size].reshape(experts * CAP, size)
        out_ref[:, start : start + size] = left_dot(chosen, held).astype(BF)


def combine(slot_rows, slots):
    experts, total = slot_rows.shape
    blocks = total // BLOCK
    features = slots.shape[2]
    return pl.pallas_call(
        combine_kernel,
        grid=(blocks,),
        in_specs=[
            pl.BlockSpec((experts, BLOCK), lambda b: (0, b)),
            pl.BlockSpec((experts, CAP, features), lambda b: (0, b, 0)),
        ],
        out_specs=pl.BlockSpec((BLOCK, features), lambda b: (b, 0)),
        out_shape=jax.ShapeDtypeStruct((total, features), BF),
        compiler_params=params(),
        cost_estimate=cost(
            flops=2 * experts * CAP * total * features,
            bytes_accessed=2 * features * (total + experts * blocks * CAP),
            transcendentals=0,
        ),
        name="combine",
    )(slot_rows, slots)


def expert_kernel(
    rank_ref, x_ref, dy_ref, wg_ref, wu_ref, wd_ref, ys_ref, dx_ref, gdy_ref, act_ref, dg_ref, du_ref
):
    features = dy_ref.shape[2]
    rows = x_ref[0, :, :features]
    pre = dense_dot(rows, wg_ref[0])
    up = dense_dot(rows, wu_ref[0])
    sigma = 1.0 / (1.0 + jnp.exp(-pre))
    silu = pre * sigma
    active = (silu * up).astype(BF)
    act_ref[0] = active
    column = rank_ref[0] * pl.num_programs(0) + pl.program_id(0)
    lane = lax.broadcasted_iota(jnp.int32, (rows.shape[0], LANES), 1)
    is_high, is_low = lane == column, lane == column + EXPERTS
    table = jnp.where(jnp.logical_or(is_high, is_low), x_ref[0, :, features:].astype(F32), 0.0)
    share = jnp.sum(table, axis=1, keepdims=True)
    result = dense_dot(active, wd_ref[0])
    grads = dy_ref[0].astype(F32)
    dots = jnp.sum(result * grads, axis=1, keepdims=True)
    high = dots.astype(BF).astype(F32)
    dx_ref[0, :, features:] = jnp.where(is_high, high, jnp.where(is_low, dots - high, 0.0)).astype(BF)
    ys_ref[0] = (result * share).astype(BF)
    gated = (grads * share).astype(BF)
    gdy_ref[0] = gated
    dact = right_dot(gated, wd_ref[0])
    dpre = (dact * up * sigma * (1.0 + pre * (1.0 - sigma))).astype(BF)
    dup = (dact * silu).astype(BF)
    dg_ref[0] = dpre
    du_ref[0] = dup
    dx_ref[0, :, :features] = (right_dot(dpre, wg_ref[0]) + right_dot(dup, wu_ref[0])).astype(BF)


def expert_pass(rank, x_slots, dy_slots, w_gate, w_up, w_down):
    experts, rows, features = dy_slots.shape
    hidden = w_gate.shape[2]
    one = lambda e, r: (e, 0, 0)
    longer = pl.BlockSpec((1, rows, features + LANES), one)
    wide = pl.BlockSpec((1, rows, features), one)
    narrow = pl.BlockSpec((1, rows, hidden), one)
    shape = lambda width: jax.ShapeDtypeStruct((experts, rows, width), BF)
    return pl.pallas_call(
        expert_kernel,
        grid_spec=pltpu.PrefetchScalarGridSpec(
            num_scalar_prefetch=1,
            grid=(experts,),
            in_specs=[
                longer, wide,
                pl.BlockSpec((1, features, hidden), one),
                pl.BlockSpec((1, features, hidden), one),
                pl.BlockSpec((1, hidden, features), one),
            ],
            out_specs=[wide, longer, wide, narrow, narrow, narrow],
        ),
        out_shape=[
            shape(features), shape(features + LANES), shape(features), shape(hidden), shape(hidden), shape(hidden)
        ],
        compiler_params=params(),
        cost_estimate=cost(
            flops=12 * experts * rows * features * hidden,
            bytes_accessed=6 * experts * features * hidden + 10 * experts * rows * features,
            transcendentals=experts * rows * hidden,
        ),
        name="experts",
    )(rank, x_slots, dy_slots, w_gate, w_up, w_down)


def weight_kernel(count, products, step, core_ref, *refs):
    lefts, rights = refs[:count], refs[count : count * (1 + products)]
    outs, held_ref = refs[count * (1 + products) : -1], refs[-1]
    for i in range(products):
        total = sum(left_dot(lefts[m][0], rights[i * count + m][0]) for m in range(count))
        if step is None:
            outs[i][0] = total.astype(BF)
        else:
            held_ref[...] = total.astype(BF)
            halves(core_ref, held_ref, step, outs[2 * i].at[0], outs[2 * i + 1].at[0])


def weight_pass(core, step, depth, lefts, *rights):
    experts, rows, width = rights[0][0].shape
    one = lambda e, s: (e, 0, 0)
    count, products = len(lefts), len(rights)
    part = depth if step is None else depth // 2
    copies = products if step is None else 2 * products
    half = jax.ShapeDtypeStruct((experts, part, width), BF)
    return pl.pallas_call(
        partial(weight_kernel, count, products, step),
        grid_spec=pltpu.PrefetchScalarGridSpec(
            num_scalar_prefetch=1,
            grid=(experts,),
            in_specs=[
                *[pl.BlockSpec((1, rows, depth), one) for _ in lefts],
                *[pl.BlockSpec((1, rows, width), one) for right in rights for _ in right],
            ],
            out_specs=[pl.BlockSpec((1, part, width), one)] * copies,
            scratch_shapes=[pltpu.VMEM((depth, width), BF)],
        ),
        out_shape=[half] * copies,
        compiler_params=params(),
        cost_estimate=cost(
            flops=2 * count * products * experts * rows * depth * width,
            bytes_accessed=2 * experts * (products * depth * width + count * rows * (depth + products * width)),
            transcendentals=0,
        ),
        name="expert_weights",
    )(core, *lefts, *[a for right in rights for a in right])


def split_kernel(sums_ref, query_ref, key_ref, value_ref, router_ref, gains_ref, out_ref):
    part = lambda start, width: sums_ref[:, start : start + width].astype(F32)
    small = QD + 2 * KD
    query_ref[...] = part(0, QD)
    key_ref[...] = part(QD, KD)
    value_ref[...] = part(QD + KD, KD)
    table = part(small, LANES)
    router_ref[...] = table[:, :EXPERTS]
    gains_ref[...] = table[:, EXPERTS : EXPERTS + 2]
    out_ref[...] = part(small + LANES, out_ref.shape[1])


def split_dense(sums):
    rows, width = sums.shape
    shape = lambda n: jax.ShapeDtypeStruct((rows, n), F32)
    widths = (QD, KD, KD, EXPERTS, 2, width - QD - 2 * KD - LANES)
    return pl.pallas_call(
        split_kernel,
        out_shape=[shape(n) for n in widths],
        compiler_params=params(),
        cost_estimate=cost(flops=0, bytes_accessed=6 * rows * width, transcendentals=0),
        name="split_dense",
    )(sums)


def fold_kernel(cut, step, place_ref, keep_ref, got_ref, *outs):
    x_place, y_place = place_ref[0], place_ref[1]

    def put(out_ref, slot, block):
        rows = pl.ds(pl.multiple_of(block * step, step), step)
        total = keep_ref[0, rows, :].astype(F32) + got_ref[0, rows, :].astype(F32)
        out_ref[0, slot * step : (slot + 1) * step, :] = total.astype(BF)

    first = pl.program_id(0) < cut

    @pl.when(first)
    def _():
        for y in range(2):
            put(outs[0], y, 2 * y + x_place)
            put(outs[1], y, 2 * y + 1 - x_place)

    @pl.when(jnp.logical_not(first))
    def _():
        for x in range(2):
            put(outs[2], x, 2 * y_place + x)
            put(outs[3], x, 2 * (1 - y_place) + x)


def fold(places, keep, got, tile=None):
    some, rows, width = keep.shape
    step = rows // 4
    count = some if tile is None else width // tile
    cut = (count + 1) // 2
    size = width if tile is None else tile
    place = (lambda i: (i, 0, 0)) if tile is None else (lambda i: (0, 0, i))
    block = lambda high, index: pl.BlockSpec((1, high, size), index)
    whole = block(rows, lambda i, s: place(i))
    one = block(2 * step, lambda i, s: place(jnp.minimum(i, cut - 1)))
    two = block(2 * step, lambda i, s: place(jnp.maximum(i - cut, 0)))
    shape = lambda n: jax.ShapeDtypeStruct(
        (n, 2 * step, width) if tile is None else (some, 2 * step, n * tile), BF
    )
    return pl.pallas_call(
        partial(fold_kernel, cut, step),
        grid_spec=pltpu.PrefetchScalarGridSpec(
            num_scalar_prefetch=1,
            grid=(count,),
            in_specs=[whole, whole],
            out_specs=[one, one, two, two],
        ),
        out_shape=[shape(cut), shape(cut), shape(count - cut), shape(count - cut)],
        compiler_params=params(),
        cost_estimate=cost(
            flops=some * rows * width, bytes_accessed=6 * some * rows * width, transcendentals=0
        ),
        name="fold",
    )(places, keep, got)


def fold_again_kernel(step, place_ref, keep_ref, got_ref, stay_ref, go_ref):
    for out_ref, half in ((stay_ref, place_ref[0]), (go_ref, 1 - place_ref[0])):
        rows = pl.ds(pl.multiple_of(half * step, step), step)
        total = keep_ref[0, rows, :].astype(F32) + got_ref[0, rows, :].astype(F32)
        out_ref[0] = total.astype(BF)


def fold_again(place, keep, got):
    some, rows, width = keep.shape
    step = rows // 2
    tile = width
    while tile * rows > 2**19 and tile % 2 == 0 and tile // 2 % LANES == 0:
        tile //= 2
    index = lambda i, j, s: (i, 0, j)
    return pl.pallas_call(
        partial(fold_again_kernel, step),
        grid_spec=pltpu.PrefetchScalarGridSpec(
            num_scalar_prefetch=1,
            grid=(some, width // tile),
            in_specs=[pl.BlockSpec((1, rows, tile), index)] * 2,
            out_specs=[pl.BlockSpec((1, step, tile), index)] * 2,
        ),
        out_shape=[jax.ShapeDtypeStruct((some, step, width), BF)] * 2,
        compiler_params=params(),
        cost_estimate=cost(
            flops=some * rows * width, bytes_accessed=6 * some * rows * width, transcendentals=0
        ),
        name="fold_again",
    )(place, keep, got)


def after(value, *marks):
    return lax.optimization_barrier((value, *marks))[0]


def together(*values):
    return lax.optimization_barrier(values)


def local(
    tokens, out_grad, routes, attn_gain, w_query, w_key, w_value, w_out, moe_gain, w_router,
    w_gate, w_up, w_down,
):
    micros, _, features = tokens.shape
    count = lax.axis_size("expert")
    rank = lax.axis_index("expert")
    exp_dev = w_gate.shape[0]
    dp = lax.axis_size("dp")
    core = (lax.axis_index("dp") % 2).astype(jnp.int32)[None]
    seq_blocks = SEQ // BLOCK
    place = rank % seq_blocks
    cosine, sine = rotary_tables(place * BLOCK + jnp.arange(BLOCK, dtype=jnp.int32))
    place = place.astype(jnp.int32)[None]
    around = [(i, (i + 1) % count) for i in range(count)]
    upward = [(i, i + 1) for i in range(count - 1) if (i + 1) % seq_blocks]
    downward = [(b, a) for a, b in upward]
    ring = lambda a: lax.ppermute(a, "expert", around)
    later = lambda a: lax.ppermute(a, "expert", upward)
    earlier = lambda a: lax.ppermute(a, "expert", downward)
    add = lambda a, b: (a.astype(F32) + b.astype(F32)).astype(BF)
    every = lambda a, axis: lax.all_gather(a, axis, axis=0, tiled=True)
    swap = lambda a: lax.ppermute(a, "dp", [(i, i ^ 1) for i in range(dp)])
    same_core = [list(range(c, dp, 2)) for c in range(2)]
    across = lambda a, bit: lax.ppermute(a, "dp", [(i, i ^ bit) for i in range(dp)])
    x_place, y_place = lax.axis_index("dp") // 2 % 2, lax.axis_index("dp") // 4
    square = dp == 8

    places = jnp.stack([x_place, y_place]).astype(jnp.int32)

    share = lambda a: lax.psum_scatter(a, "dp", scatter_dimension=1, axis_index_groups=same_core, tiled=True)

    def fold_first(keep, got, tile=None):
        return list(fold(places, keep, got, tile)) if square else [add(keep, got)]

    def send_first(parts):
        if not square:
            return parts
        one, one_sent, two, two_sent = parts
        return [one, across(one_sent, 2), two, across(two_sent, 4)]

    def halve_first(keep, got, tile=None):
        return send_first(fold_first(keep, got, tile))

    def halve_second(parts):
        if not square:
            return parts
        one, one_sent = fold_again(places[1:], *parts[:2])
        two, two_sent = fold_again(places[:1], *parts[2:])
        return [one, across(one_sent, 4), two, across(two_sent, 2)]

    def halve_last(parts, axis, dtype):
        if not square:
            return share(parts[0]).astype(dtype)
        total = lambda a, b: (a.astype(F32) + b.astype(F32)).astype(dtype)
        return jnp.concatenate([total(*parts[:2]), total(*parts[2:])], axis=axis)

    beside = jnp.zeros((w_router.shape[0], LANES - EXPERTS - 2), BF)
    weights = every(
        jnp.concatenate(
            [w_query, w_out, w_key, w_value, w_router, attn_gain[:, None], moe_gain[:, None], beside], axis=1
        ),
        "dp",
    )
    behind = QD + features + 2 * KD

    members = jnp.any(routes[:, :, :, None] == jnp.arange(EXPERTS, dtype=jnp.int32), axis=2)
    before = jnp.tril(jnp.ones((BLOCK, BLOCK), F32), -1).astype(BF)
    slots = jnp.einsum("ts,mse->mte", before, members.astype(BF), preferred_element_type=F32)
    slots = jnp.where(members, slots, -1.0).astype(BF)
    dy_sent = jnp.concatenate([out_grad, slots, jnp.zeros((micros, BLOCK, LANES - EXPERTS), BF)], axis=2)

    dy_ring = [dy_sent]
    for _ in range(count - 2):
        dy_ring.append(ring(dy_ring[-1]))
    router_w = weights[:, behind:]
    gains = router_w[:, EXPERTS : EXPERTS + 2].T.astype(F32)
    gain_one, gain_two = gains[0:1], gains[1:2]
    x_whole = tokens.reshape(micros * BLOCK, features)
    normed, scale_one = norm_rows(x_whole, gain_one)
    normed = after(normed, dy_ring[-1])
    kv_own = project(normed, weights, QD + features, 2 * KD, KD, cosine, sine)
    dy_last = [ring(dy_ring[-1][0])]
    kv_own = list(kv_own)
    kv_own[0], dy_last[0] = together(kv_own[0], dy_last[0])
    kv_one = [kv_own[0]]
    for _ in range(seq_blocks - 1):
        kv_one.append(later(kv_one[-1]))
    dy_last.append(ring(after(dy_ring[-1][1], kv_one[-1])))

    kv_two = [after(kv_own[1], kv_one[-1])]
    kv_two.append(later(kv_two[-1]))
    queries = list(project(after(normed, kv_one[-1]), weights, 0, QD, QD, cosine, sine))
    kv_two[-1], queries[0] = together(kv_two[-1], queries[0])
    kv_two.append(later(kv_two[-1]))
    o_one, ob_one, lse_one = attend(place, queries[0], kv_one)
    kv_two[-1], dy_last[1], ob_one = together(kv_two[-1], dy_last[1], ob_one)
    dy_ring.append(dy_last)
    kv_two.append(later(kv_two[-1]))
    go_out = lambda m, ob: outward(ob, weights, tokens[m], gain_two, router_w, routes[m])
    mids = [list(go_out(0, ob_one))]
    sent = [every(mids[0][1], "expert")]
    kv_two[-1], mids[0][1] = together(kv_two[-1], mids[0][1])
    while len(kv_two) < seq_blocks:
        kv_two.append(later(kv_two[-1]))
    def in_order(m):
        whole = jnp.zeros((count * BLOCK, features + LANES), BF)
        for step, block in enumerate(dy_ring):
            whole = lax.dynamic_update_slice_in_dim(whole, block[m], (rank - step) % count * BLOCK, 0)
        return whole

    slot_rows, dy_slots = [], []
    for m in range(micros):
        dy_all = in_order(m)
        table = lax.dynamic_slice_in_dim(dy_all, features + rank * exp_dev, exp_dev, 1)
        slot_rows.append(table.astype(F32).T)
        dy_slots.append(dispatch(slot_rows[m], dy_all, features))
    kv_two[-1], *dy_slots = together(kv_two[-1], *dy_slots)
    o_two, ob_two, lse_two = attend(place, queries[1], kv_two)
    mids.append(list(go_out(1, ob_two)))
    sent.append(every(mids[1][1], "expert"))
    kvs = (kv_one, kv_two)
    heads = ((o_one, ob_one, lse_one), (o_two, ob_two, lse_two))

    own = rank.astype(jnp.int32)[None]
    experts = lambda m, x: expert_pass(own, x, dy_slots[m], w_gate, w_up, w_down)
    ring_block = lambda sums, j: lax.dynamic_slice_in_dim(sums, (rank - 1 - j) % count * BLOCK, BLOCK, 0)
    x_one = dispatch(slot_rows[0], sent[0], features + LANES)
    ys_one, dx_one, gdy_one, act_one, dg_one, du_one = experts(0, x_one)
    dx_one = combine(slot_rows[0], dx_one)
    dx_home = [lax.psum_scatter(dx_one, "expert", scatter_dimension=0, tiled=True)]
    mixture_one = combine(slot_rows[0], after(ys_one, dx_one))
    sent[1], mixture_one = together(sent[1], mixture_one)
    x_two = dispatch(slot_rows[1], sent[1], features + LANES)
    ys_two, dx_two, gdy_two, act_two, dg_two, du_two = experts(1, x_two)

    hidden = w_down.shape[1]
    (new_down,) = weight_pass(core, None, hidden, (act_one, act_two), (gdy_one, gdy_two))
    new_down, dx_home[0] = together(new_down, dx_home[0])
    down_grad = lax.psum_scatter(new_down, "dp", scatter_dimension=1, tiled=True)
    dx_two = combine(slot_rows[1], after(dx_two, new_down))
    dx_held = ring(ring_block(dx_two, 0))
    ups = weight_pass(
        core, features // dp, features, (x_one, x_two), (after(dg_one, dx_two), dg_two), (du_one, du_two)
    )
    dx_held, *ups = together(dx_held, *ups)
    for step in range(1, count - 2):
        dx_held = ring(add(dx_held, ring_block(dx_two, step)))
    got_gate, got_up = swap(ups[1]), swap(ups[3])

    def back_home(m, dx):
        mid, _, scale_two, gates = mids[m]
        return home_back(dx, gates, mid, scale_two, out_grad[m], router_w, gain_two, weights)

    def back_heads(m, dob):
        o, _, lse = heads[m]
        dq, *pieces = attend_back(place, queries[m], dob, o, lse, cosine, sine, kvs[m])
        return dq, pieces[::-1]

    first = list(back_home(0, after(dx_home[0], ups[0])))
    dq_one, far_one = back_heads(0, first[2])
    dx_held, got_gate, got_up, dq_one = together(dx_held, got_gate, got_up, dq_one)
    dx_held = ring(add(dx_held, ring_block(dx_two, count - 2)))
    up_half = add(ups[2], got_up)
    up_grad = share(up_half)
    dx_home.append(add(dx_held, ring_block(dx_two, count - 1)))
    held = ring(ring_block(after(mixture_one, dx_held), 0))
    back_one = earlier(far_one[0])
    second = list(back_home(1, after(dx_home[1], up_half, dq_one)))
    back_one, second[2] = together(back_one, second[2])
    back_one = earlier(add(back_one, far_one[1]))
    dq_two, far_two = back_heads(1, second[2])
    back_one, dq_two, far_two[0], held, down_grad = together(back_one, dq_two, far_two[0], held, down_grad)
    for piece in far_one[2:-1]:
        back_one = earlier(add(back_one, piece))
    back_two = earlier(far_two[0])
    gate_half = add(after(ups[0], dq_two), got_gate)
    gate_grad = share(gate_half)
    held = ring(add(held, ring_block(mixture_one, 1)))
    back_one = add(back_one, far_one[-1])

    def back_last(m, dq, dkv, dmid):
        return last_back(
            dq, dkv, cosine, sine, weights, weights, tokens[m], scale_one[m * BLOCK : (m + 1) * BLOCK], gain_one, dmid
        )

    back_two, back_one = together(back_two, back_one, gate_half)[:2]
    back_two = earlier(add(back_two, far_two[1]))
    grad_x_one, dkv_one, dgain_one = back_last(0, dq_one, back_one, first[0])
    back_two, dkv_one, held = together(back_two, dkv_one, held)
    for piece in far_two[2:-1]:
        back_two = earlier(add(back_two, piece))
    back_two = add(back_two, far_two[-1])
    grad_x_two, dkv_two, dgain_two = back_last(1, dq_two, back_two, second[0])
    gain_rows = jnp.concatenate([dgain_one + dgain_two, first[4] + second[4]], axis=0)
    gain_columns = jnp.pad(gain_rows.T, ((0, 0), (EXPERTS, LANES - EXPERTS - 2)))
    keep, send = dense_grads(
        core, features // dp, [normed] * micros, [dq_one, dq_two], [dkv_one, dkv_two], [k[1] for k in mids],
        [first[3], second[3]], [h[1] for h in heads], [first[1], second[1]], gain_columns,
    )
    for step in range(2, count - 1):
        held = ring(add(after(held, keep), ring_block(mixture_one, step)))
    got = swap(send)
    mixture_two = combine(slot_rows[1], after(ys_two, keep))
    got, mixture_two, up_grad = together(got, mixture_two, up_grad)
    dense_sums = halve_first(keep[None], got[None], 3 * LANES)
    held, mixture_two = together(held, mixture_two, dense_sums[0])[:2]
    mixtures = [add(held, ring_block(mixture_one, count - 1))]
    held = ring(ring_block(mixture_two, 0))
    held = ring(add(held, ring_block(mixture_two, 1)))
    held, *dense_sums = together(held, *dense_sums)
    dense_sums = halve_second(dense_sums)
    held = after(held, *dense_sums[::2])
    for step in range(2, count - 1):
        held = ring(add(held, ring_block(mixture_two, step)))
    held, gate_grad, *dense_sums = together(held, gate_grad, *dense_sums)
    mixtures.append(add(held, ring_block(mixture_two, count - 1)))
    dense_sum = halve_last(dense_sums, 2, BF)[0]
    gate_grad, up_grad, down_grad = gate_grad.astype(F32), up_grad.astype(F32), down_grad.astype(F32)
    dense = split_dense(lax.psum(dense_sum, "expert"))
    query, key, value, router, gain_columns, out = dense
    mixed = [(mids[m][0] + mixtures[m].astype(F32)).astype(BF) for m in range(micros)]
    return (
        jnp.stack(mixed),
        jnp.stack([grad_x_one, grad_x_two]),
        gain_columns[:, 0],
        query,
        key,
        value,
        out,
        gain_columns[:, 1],
        router,
        gate_grad,
        up_grad,
        down_grad,
    )


def solution(mesh):
    rows = P(None, ("dp", "expert"), None)
    return jax.shard_map(
        local,
        mesh=mesh,
        in_specs=(
            rows, rows, rows, P("dp"), P("dp", None), P("dp", None), P("dp", None), P("dp", None),
            P("dp"), P("dp", None),
            P("expert", None, None), P("expert", None, None), P("expert", None, None),
        ),
        out_specs=(
            rows, rows, P("dp"), P("dp", None), P("dp", None), P("dp", None), P("dp", None),
            P("dp"), P("dp", None),
            P("expert", "dp", None), P("expert", "dp", None), P("expert", "dp", None),
        ),
        check_vma=False,
    )
```

```python
from functools import partial

import jax
import jax.numpy as jnp
from jax import lax
from jax.experimental import pallas as pl
from jax.experimental.pallas import tpu as pltpu
from jax.sharding import PartitionSpec as P

HEADS = 24
KV_HEADS = 8
HEAD = 64
FF = 512
EXPERTS = 40
TOP = 8
BLOCK = 256
SEQ = 1024
CAP = 64
QD = 1536
KD = 512

EPSILON = 1e-06
ROPE_BASE = 10000.0
NEGATIVE = -1e30
LANES = 128
COLUMNS = 256
VMEM_LIMIT = 56 * 2**20
COST_SCALE = 0.1

BF = jnp.bfloat16
F32 = jnp.float32


def dense_dot(left, right):
    return jnp.dot(left, right, preferred_element_type=F32)


def left_dot(left, right):
    return lax.dot_general(left, right, (((0,), (0,)), ((), ())), preferred_element_type=F32)


def right_dot(left, right):
    return lax.dot_general(left, right, (((1,), (1,)), ((), ())), preferred_element_type=F32)


def rotary_tables(positions):
    half_size = HEAD // 2
    frequency = ROPE_BASE ** (-jnp.arange(half_size, dtype=F32) / half_size)
    angle = positions.astype(F32)[:, None] * frequency[None, :]
    cosine, sine = jnp.cos(angle), jnp.sin(angle)
    tiles = LANES // HEAD
    return (
        jnp.concatenate([cosine, cosine] * tiles, axis=1),
        jnp.concatenate([-sine, sine] * tiles, axis=1),
    )


def cost(flops, bytes_accessed, transcendentals):
    scale = lambda n: int(n * COST_SCALE)
    return pl.CostEstimate(
        flops=scale(flops), bytes_accessed=scale(bytes_accessed), transcendentals=scale(transcendentals)
    )


def params(limit=VMEM_LIMIT):
    return pltpu.CompilerParams(vmem_limit_bytes=limit)


def swap_halves(values):
    lane = lax.broadcasted_iota(jnp.int32, values.shape, 1)
    half = HEAD // 2
    return jnp.where(
        lane % HEAD < half,
        pltpu.roll(values, LANES - half, 1),
        pltpu.roll(values, half, 1),
    )


def turn(values, cosine, sine):
    return values * cosine + swap_halves(values) * sine


def norm_kernel(x_ref, gain_ref, normed_ref, scale_ref):
    rows = x_ref[...].astype(F32)
    scale = lax.rsqrt(jnp.mean(rows * rows, axis=1, keepdims=True) + EPSILON)
    scale_ref[...] = scale
    normed_ref[...] = (rows * scale * gain_ref[...]).astype(BF)


def norm_rows(x, gain):
    total, features = x.shape
    return pl.pallas_call(
        norm_kernel,
        grid=(total // BLOCK,),
        in_specs=[
            pl.BlockSpec((BLOCK, features), lambda i: (i, 0)),
            pl.BlockSpec((1, features), lambda i: (0, 0)),
        ],
        out_specs=[
            pl.BlockSpec((BLOCK, features), lambda i: (i, 0)),
            pl.BlockSpec((BLOCK, 1), lambda i: (i, 0)),
        ],
        out_shape=[
            jax.ShapeDtypeStruct((total, features), BF),
            jax.ShapeDtypeStruct((total, 1), F32),
        ],
        compiler_params=params(),
        cost_estimate=cost(flops=5 * total * features, bytes_accessed=4 * total * features, transcendentals=0),
        name="norm",
    )(x, gain)


def project_kernel(turned, normed_ref, w_ref, cosine_ref, sine_ref, *outs):
    tile = w_ref.shape[1]
    rows = dense_dot(normed_ref[...], w_ref[...])

    def write(turning):
        for start in range(0, tile, LANES):
            for m, out_ref in enumerate(outs):
                part = rows[m * BLOCK : (m + 1) * BLOCK, start : start + LANES]
                if turning:
                    part = turn(part, cosine_ref[...], sine_ref[...])
                out_ref[:, start : start + LANES] = part.astype(BF)

    pl.when(pl.program_id(0) < turned)(lambda: write(True))
    pl.when(pl.program_id(0) >= turned)(lambda: write(False))


def project(normed, weight, start, columns, turned_columns, cosine, sine):
    total, features = normed.shape
    tile = 2 * COLUMNS
    micros = total // BLOCK
    return pl.pallas_call(
        partial(project_kernel, turned_columns // tile),
        grid=(columns // tile,),
        in_specs=[
            pl.BlockSpec((total, features), lambda j: (0, 0)),
            pl.BlockSpec((features, tile), lambda j: (0, start // tile + j)),
            pl.BlockSpec((BLOCK, LANES), lambda j: (0, 0)),
            pl.BlockSpec((BLOCK, LANES), lambda j: (0, 0)),
        ],
        out_specs=[pl.BlockSpec((BLOCK, tile), lambda j: (0, j))] * micros,
        out_shape=[jax.ShapeDtypeStruct((BLOCK, columns), BF)] * micros,
        compiler_params=params(),
        cost_estimate=cost(
            flops=2 * total * features * columns,
            bytes_accessed=2 * (features * columns + total * (features + columns)),
            transcendentals=0,
        ),
        name="project",
    )(normed, weight, cosine, sine)


def outward_kernel(ob_ref, w_ref, x_ref, gain_ref, router_ref, routes_ref, mid_ref, sent_ref, scale_ref, gates_ref):
    j = pl.program_id(0)
    tile = w_ref.shape[1]
    features = mid_ref.shape[1]
    where = pl.ds(pl.multiple_of(j * tile, tile), tile)
    mid_ref[:, where] = x_ref[:, where].astype(F32) + dense_dot(ob_ref[...], w_ref[...])

    @pl.when(j == pl.num_programs(0) - 1)
    def _():
        mid = mid_ref[...]
        scale = lax.rsqrt(jnp.mean(mid * mid, axis=1, keepdims=True) + EPSILON)
        scale_ref[...] = scale
        normed = (mid * scale * gain_ref[...]).astype(BF)
        sent_ref[:, :features] = normed
        lane = lax.broadcasted_iota(jnp.int32, (BLOCK, LANES), 1)
        routes = routes_ref[...]
        member = lane == routes[:, 0:1]
        for k in range(1, TOP):
            member = jnp.logical_or(member, lane == routes[:, k : k + 1])
        logits = jnp.where(member, dense_dot(normed, router_ref[...]), NEGATIVE)
        weights = jnp.exp(logits - jnp.max(logits, axis=1, keepdims=True))
        weights = jnp.where(member, weights, 0.0)
        gates = weights / jnp.sum(weights, axis=1, keepdims=True)
        gates_ref[...] = gates
        high = gates.astype(BF).astype(F32)
        sent_ref[:, features:] = (high + pltpu.roll(gates - high, EXPERTS, 1)).astype(BF)


def outward(ob, w_qo, x, gain, router, routes):
    features = x.shape[1]
    tile = 2 * COLUMNS
    whole = lambda a: pl.BlockSpec(a.shape, lambda j: (0, 0))
    fixed = lambda *shape: pl.BlockSpec(shape, lambda j: (0, 0))
    return pl.pallas_call(
        outward_kernel,
        grid=(features // tile,),
        in_specs=[
            whole(ob),
            pl.BlockSpec((QD, tile), lambda j: (0, QD // tile + j)),
            whole(x), whole(gain), whole(router), whole(routes),
        ],
        out_specs=[fixed(BLOCK, features), fixed(BLOCK, features + LANES), fixed(BLOCK, 1), fixed(BLOCK, LANES)],
        out_shape=[
            jax.ShapeDtypeStruct((BLOCK, features), F32),
            jax.ShapeDtypeStruct((BLOCK, features + LANES), BF),
            jax.ShapeDtypeStruct((BLOCK, 1), F32),
            jax.ShapeDtypeStruct((BLOCK, LANES), F32),
        ],
        compiler_params=params(),
        cost_estimate=cost(
            flops=2 * BLOCK * features * QD, bytes_accessed=2 * features * QD + 14 * BLOCK * features, transcendentals=0
        ),
        name="outward",
    )(ob, w_qo, x, gain, router, routes)


def home_kernel(
    dx_ref, gates_ref, mid_ref, scale_ref, dy_ref, router_ref, gain_ref, w_ref,
    dmid_ref, da_ref, dob_ref, dlog_ref, dgain_ref,
):
    j = pl.program_id(0)
    features = mid_ref.shape[1]
    tile = w_ref.shape[0]

    @pl.when(j == 0)
    def _():
        table = dx_ref[:, features:].astype(F32)
        dgates = table + pltpu.roll(table, LANES - EXPERTS, 1)
        gates = gates_ref[...]
        dc = gates * (dgates - jnp.sum(gates * dgates, axis=1, keepdims=True))
        dlog = dc.astype(BF)
        dlog_ref[...] = dlog
        dnormed = dx_ref[:, :features].astype(F32) + right_dot(dlog, router_ref[...])
        mid = mid_ref[...]
        scale = scale_ref[...]
        dgain_ref[...] = jnp.sum(dnormed * mid * scale, axis=0, keepdims=True)
        scaled = dnormed * gain_ref[...]
        mean = jnp.mean(scaled * mid, axis=1, keepdims=True)
        dmid = dy_ref[...].astype(F32) + scale * scaled - mid * (scale * scale * scale * mean)
        dmid_ref[...] = dmid
        da_ref[...] = dmid.astype(BF)

    where = pl.ds(pl.multiple_of(j * tile, tile), tile)
    dob_ref[:, where] = right_dot(da_ref[...], w_ref[...]).astype(BF)


def home_back(dx, gates, mid, scale, dy, router, gain, w_qo):
    features = mid.shape[1]
    tile = 2 * COLUMNS
    whole = lambda a: pl.BlockSpec(a.shape, lambda j: (0, 0))
    fixed = lambda *shape: pl.BlockSpec(shape, lambda j: (0, 0))
    return pl.pallas_call(
        home_kernel,
        grid=(QD // tile,),
        in_specs=[
            whole(dx), whole(gates), whole(mid), whole(scale), whole(dy), whole(router), whole(gain),
            pl.BlockSpec((tile, features), lambda j: (j, 1)),
        ],
        out_specs=[
            fixed(BLOCK, features), fixed(BLOCK, features), fixed(BLOCK, QD), fixed(BLOCK, LANES), fixed(1, features),
        ],
        out_shape=[
            jax.ShapeDtypeStruct((BLOCK, features), F32),
            jax.ShapeDtypeStruct((BLOCK, features), BF),
            jax.ShapeDtypeStruct((BLOCK, QD), BF),
            jax.ShapeDtypeStruct((BLOCK, LANES), BF),
            jax.ShapeDtypeStruct((1, features), F32),
        ],
        compiler_params=params(),
        cost_estimate=cost(
            flops=2 * BLOCK * features * QD, bytes_accessed=2 * features * QD + 18 * BLOCK * features, transcendentals=0
        ),
        name="home_back",
    )(dx, gates, mid, scale, dy, router, gain, w_qo)


def last_kernel(
    dq_ref, dkv_ref, cosine_ref, sine_ref, wq_ref, wkv_ref, x_ref, scale_ref, gain_ref, dmid_ref,
    dx_ref, dkvb_ref, dgain_ref,
):
    j = pl.program_id(0)
    tile = wq_ref.shape[0]

    @pl.when(j == 0)
    def _():
        for start in range(0, KD, LANES):
            part = dkv_ref[0, :, start : start + LANES].astype(F32)
            dkvb_ref[:, start : start + LANES] = turn(part, cosine_ref[...], -sine_ref[...]).astype(BF)
        dkvb_ref[:, KD:] = dkv_ref[1]

    where = pl.ds(pl.multiple_of(j * tile, tile), tile)
    dx_ref[:, where] = right_dot(dq_ref[...], wq_ref[...]) + right_dot(dkvb_ref[...], wkv_ref[...])

    @pl.when(j == pl.num_programs(0) - 1)
    def _():
        dnormed = dx_ref[...]
        rows = x_ref[...].astype(F32)
        scale = scale_ref[...]
        dgain_ref[...] = jnp.sum(dnormed * rows * scale, axis=0, keepdims=True)
        scaled = dnormed * gain_ref[...]
        mean = jnp.mean(scaled * rows, axis=1, keepdims=True)
        dx_ref[...] = dmid_ref[...] + scale * scaled - rows * (scale * scale * scale * mean)


def last_back(dq, dkv, cosine, sine, w_q, w_kv, x, scale, gain, dmid):
    features = x.shape[1]
    tile = 2 * COLUMNS
    whole = lambda a: pl.BlockSpec(a.shape, lambda j: (0,) * a.ndim)
    fixed = lambda *shape: pl.BlockSpec(shape, lambda j: (0, 0))
    return pl.pallas_call(
        last_kernel,
        grid=(features // tile,),
        in_specs=[
            whole(dq), whole(dkv), whole(cosine), whole(sine),
            pl.BlockSpec((tile, QD), lambda j: (j, 0)),
            pl.BlockSpec((tile, 2 * KD), lambda j: (j, QD // KD)),
            whole(x), whole(scale), whole(gain), whole(dmid),
        ],
        out_specs=[fixed(BLOCK, features), fixed(BLOCK, 2 * KD), fixed(1, features)],
        out_shape=[
            jax.ShapeDtypeStruct((BLOCK, features), F32),
            jax.ShapeDtypeStruct((BLOCK, 2 * KD), BF),
            jax.ShapeDtypeStruct((1, features), F32),
        ],
        compiler_params=params(),
        cost_estimate=cost(
            flops=2 * BLOCK * features * (QD + 2 * KD),
            bytes_accessed=2 * features * (QD + 2 * KD) + 16 * BLOCK * features,
            transcendentals=0,
        ),
        name="last_back",
    )(dq, dkv, cosine, sine, w_q, w_kv, x, scale, gain, dmid)


def halves(core_ref, held_ref, step, keep_ref, send_ref):
    core = core_ref[0]
    for q in range(held_ref.shape[0] // (2 * step)):
        mine = pl.multiple_of((2 * q + core) * step, step)
        other = pl.multiple_of((2 * q + 1 - core) * step, step)
        keep_ref[q * step : (q + 1) * step, :] = held_ref[pl.ds(mine, step), :]
        send_ref[q * step : (q + 1) * step, :] = held_ref[pl.ds(other, step), :]


def dense_kernel(micros, step, core_ref, *refs):
    ins, (gains_ref, keep_ref, send_ref, held_ref) = refs[: 7 * micros], refs[7 * micros :]
    normed, dq, dkv, sent, dlog, ob, da = (ins[i * micros : (i + 1) * micros] for i in range(7))

    def total(lefts, rights):
        return sum(left_dot(left[...], right[...]) for left, right in zip(lefts, rights))

    start = 0
    for lefts, rights in ((normed, dq), (normed, dkv), (sent, dlog), (ob, da)):
        width = rights[0].shape[1]
        part = total(lefts, rights)
        if rights is dlog:
            part = part + gains_ref[...]
        held_ref[:, start : start + width] = part.astype(BF)
        start += width
    halves(core_ref, held_ref, step, keep_ref, send_ref)


def dense_grads(core, step, normed, dq, dkv, sent, dlog, ob, da, gains):
    groups = (normed, dq, dkv, sent, dlog, ob, da)
    micros = len(dq)
    tile = max(3 * LANES, 2 * step)
    lefts = (True, False, False, True, False, True, False)
    width = sum(group[0].shape[1] for group, left in zip(groups, lefts) if not left)
    specs = []
    for group, left in zip(groups, lefts):
        for m, a in enumerate(group):
            if left:
                block = m if a.shape[0] > BLOCK else 0
                specs.append(pl.BlockSpec((BLOCK, tile), lambda j, s, block=block: (block, j)))
            else:
                specs.append(pl.BlockSpec(a.shape, lambda j, s: (0, 0)))
    half = jax.ShapeDtypeStruct((QD // 2, width), BF)
    return pl.pallas_call(
        partial(dense_kernel, micros, step),
        grid_spec=pltpu.PrefetchScalarGridSpec(
            num_scalar_prefetch=1,
            grid=(QD // tile,),
            in_specs=[*specs, pl.BlockSpec((tile, gains.shape[1]), lambda j, s: (j, 0))],
            out_specs=[pl.BlockSpec((tile // 2, width), lambda j, s: (j, 0))] * 2,
            scratch_shapes=[pltpu.VMEM((tile, width), BF)],
        ),
        out_shape=[half, half],
        compiler_params=params(),
        cost_estimate=cost(
            flops=2 * micros * BLOCK * QD * width,
            bytes_accessed=2 * QD * width + 4 * micros * BLOCK * (QD + width),
            transcendentals=0,
        ),
        name="dense_grads",
    )(core, *[a for group in groups for a in group], gains)


PAIR = 2 * HEAD
GROUP = HEADS // KV_HEADS * PAIR


def spread(values):
    lane = lax.broadcasted_iota(jnp.int32, (BLOCK, LANES), 1)
    first = lane < HEAD
    zero = jnp.zeros((BLOCK, LANES), F32)
    one, two, three = (values[:, i * LANES : (i + 1) * LANES] for i in range(3))
    return jnp.concatenate(
        [
            jnp.where(first, one, zero),
            jnp.where(first, pltpu.roll(one, HEAD, 1), zero),
            jnp.where(first, two, zero),
            jnp.where(first, zero, two),
            jnp.where(first, zero, pltpu.roll(three, HEAD, 1)),
            jnp.where(first, zero, three),
        ],
        axis=0,
    )


def gather_heads(rows):
    lane = lax.broadcasted_iota(jnp.int32, (BLOCK, LANES), 1)
    first = lane < HEAD
    part = [rows[i * BLOCK : (i + 1) * BLOCK] for i in range(6)]
    return (
        jnp.where(first, part[0], pltpu.roll(part[1], HEAD, 1)),
        jnp.where(first, part[2], part[3]),
        jnp.where(first, pltpu.roll(part[4], HEAD, 1), part[5]),
    )


def attend_kernel(place_ref, q_ref, *refs):
    blocks = SEQ // BLOCK
    keys, values = refs[:blocks], refs[blocks : 2 * blocks]
    o_ref, ob_ref, lse_ref, max_ref, sum_ref, acc_ref = refs[2 * blocks :]
    query = spread(q_ref[...].astype(F32) * HEAD ** (-0.5)).astype(BF)
    for r in range(blocks):

        @pl.when(place_ref[0] >= r)
        def _():
            scores = right_dot(keys[r][...], query)
            top = jnp.max(scores, axis=0, keepdims=True)
            if r > 0:
                before = max_ref[...]
                top = jnp.maximum(top, before)
            weights = jnp.exp(scores - top)
            total = jnp.sum(weights, axis=0, keepdims=True)
            out = left_dot(values[r][...], weights.astype(BF))
            if r > 0:
                factor = jnp.exp(before - top)
                total = total + sum_ref[...] * factor
                out = out + acc_ref[...] * factor
            max_ref[...] = top
            sum_ref[...] = total
            acc_ref[...] = out

    lse_ref[0] = max_ref[...] + jnp.log(sum_ref[...])
    rows = jnp.transpose(acc_ref[...] / sum_ref[...])
    for i, part in enumerate(gather_heads(rows)):
        o_ref[:, i * LANES : (i + 1) * LANES] = part
        ob_ref[:, i * LANES : (i + 1) * LANES] = part.astype(BF)


def attend(place, query, kvs):
    pairs = KV_HEADS // 2
    rows = 6 * BLOCK
    return pl.pallas_call(
        attend_kernel,
        grid_spec=pltpu.PrefetchScalarGridSpec(
            num_scalar_prefetch=1,
            grid=(pairs,),
            in_specs=[
                pl.BlockSpec((BLOCK, GROUP), lambda p, s: (0, p)),
                *[pl.BlockSpec((BLOCK, PAIR), lambda p, s: (0, p)) for _ in kvs],
                *[pl.BlockSpec((BLOCK, PAIR), lambda p, s: (0, KV_HEADS // 2 + p)) for _ in kvs],
            ],
            out_specs=[
                pl.BlockSpec((BLOCK, GROUP), lambda p, s: (0, p)),
                pl.BlockSpec((BLOCK, GROUP), lambda p, s: (0, p)),
                pl.BlockSpec((1, 1, rows), lambda p, s: (p, 0, 0)),
            ],
            scratch_shapes=[
                pltpu.VMEM((1, rows), F32),
                pltpu.VMEM((1, rows), F32),
                pltpu.VMEM((PAIR, rows), F32),
            ],
        ),
        out_shape=[
            jax.ShapeDtypeStruct((BLOCK, QD), F32),
            jax.ShapeDtypeStruct((BLOCK, QD), BF),
            jax.ShapeDtypeStruct((pairs, 1, rows), F32),
        ],
        compiler_params=params(),
        cost_estimate=cost(
            flops=8 * SEQ * BLOCK * HEADS * PAIR, bytes_accessed=10 * BLOCK * QD, transcendentals=SEQ * BLOCK * HEADS
        ),
        name="attend",
    )(place, query, *kvs, *kvs)


def attend_back_kernel(place_ref, q_ref, dob_ref, o_ref, lse_ref, cosine_ref, sine_ref, *refs):
    blocks = SEQ // BLOCK
    keys, values = refs[:blocks], refs[blocks : 2 * blocks]
    dq_ref, outs, acc_ref = refs[2 * blocks], refs[2 * blocks + 1 : 3 * blocks + 1], refs[-1]
    query = spread(q_ref[...].astype(F32) * HEAD ** (-0.5)).astype(BF)
    grads = spread(dob_ref[...].astype(F32))
    delta = jnp.sum(jnp.transpose(grads * spread(o_ref[...])), axis=0, keepdims=True)
    grads = grads.astype(BF)
    for r in range(blocks):

        @pl.when(place_ref[0] >= r)
        def _():
            key = keys[r][...]
            weights = jnp.exp(right_dot(key, query) - lse_ref[0])
            dscores = (weights * (right_dot(values[r][...], grads) - delta)).astype(BF)
            outs[r][0] = dense_dot(dscores, query).astype(BF)
            outs[r][1] = dense_dot(weights.astype(BF), grads).astype(BF)
            part = left_dot(key, dscores)
            acc_ref[...] = part if r == 0 else acc_ref[...] + part

        @pl.when(place_ref[0] < r)
        def _():
            outs[r][...] = jnp.zeros(outs[r].shape, BF)

    rows = jnp.transpose(acc_ref[...]) * HEAD ** (-0.5)
    for i, part in enumerate(gather_heads(rows)):
        dq_ref[:, i * LANES : (i + 1) * LANES] = turn(part, cosine_ref[...], -sine_ref[...]).astype(BF)


def attend_back(place, query, dob, o, lse, cosine, sine, kvs):
    pairs = KV_HEADS // 2
    rows = 6 * BLOCK
    heads = pl.BlockSpec((BLOCK, GROUP), lambda p, s: (0, p))
    table = pl.BlockSpec((BLOCK, LANES), lambda p, s: (0, 0))
    return pl.pallas_call(
        attend_back_kernel,
        grid_spec=pltpu.PrefetchScalarGridSpec(
            num_scalar_prefetch=1,
            grid=(pairs,),
            in_specs=[
                heads, heads, heads,
                pl.BlockSpec((1, 1, rows), lambda p, s: (p, 0, 0)),
                table, table,
                *[pl.BlockSpec((BLOCK, PAIR), lambda p, s: (0, p)) for _ in kvs],
                *[pl.BlockSpec((BLOCK, PAIR), lambda p, s: (0, KV_HEADS // 2 + p)) for _ in kvs],
            ],
            out_specs=[heads, *[pl.BlockSpec((2, BLOCK, PAIR), lambda p, s: (0, 0, p)) for _ in kvs]],
            scratch_shapes=[pltpu.VMEM((PAIR, rows), F32)],
        ),
        out_shape=[
            jax.ShapeDtypeStruct((BLOCK, QD), BF),
            *[jax.ShapeDtypeStruct((2, BLOCK, KD), BF) for _ in kvs],
        ],
        compiler_params=params(),
        cost_estimate=cost(
            flops=20 * SEQ * BLOCK * HEADS * PAIR, bytes_accessed=14 * BLOCK * QD, transcendentals=SEQ * BLOCK * HEADS
        ),
        name="attend_back",
    )(place, query, dob, o, lse, cosine, sine, *kvs, *kvs)


def picks(slot_rows):
    slots = lax.broadcasted_iota(jnp.int32, (CAP, BLOCK), 0).astype(F32)
    one, zero = jnp.float32(1), jnp.float32(0)
    return [jnp.where(slots == slot_rows[e : e + 1, :], one, zero) for e in range(slot_rows.shape[0])]


def dispatch_kernel(slot_ref, rows_ref, out_ref):
    experts = slot_ref.shape[0]
    chosen = jnp.concatenate([p.astype(BF) for p in picks(slot_ref[...])], axis=0)
    width = out_ref.shape[2]
    for start in range(0, width, COLUMNS):
        size = min(COLUMNS, width - start)
        rows = dense_dot(chosen, rows_ref[:, start : start + size])
        out_ref[:, :, start : start + size] = rows.astype(BF).reshape(experts, CAP, size)


def dispatch(slot_rows, rows, features):
    experts, total = slot_rows.shape
    blocks = total // BLOCK
    return pl.pallas_call(
        dispatch_kernel,
        grid=(blocks,),
        in_specs=[
            pl.BlockSpec((experts, BLOCK), lambda b: (0, b)),
            pl.BlockSpec((BLOCK, features), lambda b: (b, 0)),
        ],
        out_specs=pl.BlockSpec((experts, CAP, features), lambda b: (0, b, 0)),
        out_shape=jax.ShapeDtypeStruct((experts, blocks * CAP, features), BF),
        compiler_params=params(),
        cost_estimate=cost(
            flops=2 * experts * CAP * total * features,
            bytes_accessed=2 * features * (total + experts * blocks * CAP),
            transcendentals=0,
        ),
        name="dispatch",
    )(slot_rows, rows)


def combine_kernel(slot_ref, slots_ref, out_ref):
    experts, features = slots_ref.shape[0], slots_ref.shape[2]
    chosen = jnp.concatenate([p.astype(BF) for p in picks(slot_ref[...])], axis=0)
    for start in range(0, features, COLUMNS):
        size = min(COLUMNS, features - start)
        held = slots_ref[:, :, start : start + size].reshape(experts * CAP, size)
        out_ref[:, start : start + size] = left_dot(chosen, held).astype(BF)


def combine(slot_rows, slots):
    experts, total = slot_rows.shape
    blocks = total // BLOCK
    features = slots.shape[2]
    return pl.pallas_call(
        combine_kernel,
        grid=(blocks,),
        in_specs=[
            pl.BlockSpec((experts, BLOCK), lambda b: (0, b)),
            pl.BlockSpec((experts, CAP, features), lambda b: (0, b, 0)),
        ],
        out_specs=pl.BlockSpec((BLOCK, features), lambda b: (b, 0)),
        out_shape=jax.ShapeDtypeStruct((total, features), BF),
        compiler_params=params(),
        cost_estimate=cost(
            flops=2 * experts * CAP * total * features,
            bytes_accessed=2 * features * (total + experts * blocks * CAP),
            transcendentals=0,
        ),
        name="combine",
    )(slot_rows, slots)


def expert_kernel(
    rank_ref, x_ref, dy_ref, wg_ref, wu_ref, wd_ref, ys_ref, dx_ref, gdy_ref, act_ref, dg_ref, du_ref
):
    features = dy_ref.shape[2]
    rows = x_ref[0, :, :features]
    pre = dense_dot(rows, wg_ref[0])
    up = dense_dot(rows, wu_ref[0])
    sigma = 1.0 / (1.0 + jnp.exp(-pre))
    silu = pre * sigma
    active = (silu * up).astype(BF)
    act_ref[0] = active
    column = rank_ref[0] * pl.num_programs(0) + pl.program_id(0)
    lane = lax.broadcasted_iota(jnp.int32, (rows.shape[0], LANES), 1)
    is_high, is_low = lane == column, lane == column + EXPERTS
    table = jnp.where(jnp.logical_or(is_high, is_low), x_ref[0, :, features:].astype(F32), 0.0)
    share = jnp.sum(table, axis=1, keepdims=True)
    result = dense_dot(active, wd_ref[0])
    grads = dy_ref[0].astype(F32)
    dots = jnp.sum(result * grads, axis=1, keepdims=True)
    high = dots.astype(BF).astype(F32)
    dx_ref[0, :, features:] = jnp.where(is_high, high, jnp.where(is_low, dots - high, 0.0)).astype(BF)
    ys_ref[0] = (result * share).astype(BF)
    gated = (grads * share).astype(BF)
    gdy_ref[0] = gated
    dact = right_dot(gated, wd_ref[0])
    dpre = (dact * up * sigma * (1.0 + pre * (1.0 - sigma))).astype(BF)
    dup = (dact * silu).astype(BF)
    dg_ref[0] = dpre
    du_ref[0] = dup
    dx_ref[0, :, :features] = (right_dot(dpre, wg_ref[0]) + right_dot(dup, wu_ref[0])).astype(BF)


def expert_pass(rank, x_slots, dy_slots, w_gate, w_up, w_down):
    experts, rows, features = dy_slots.shape
    hidden = w_gate.shape[2]
    one = lambda e, r: (e, 0, 0)
    longer = pl.BlockSpec((1, rows, features + LANES), one)
    wide = pl.BlockSpec((1, rows, features), one)
    narrow = pl.BlockSpec((1, rows, hidden), one)
    shape = lambda width: jax.ShapeDtypeStruct((experts, rows, width), BF)
    return pl.pallas_call(
        expert_kernel,
        grid_spec=pltpu.PrefetchScalarGridSpec(
            num_scalar_prefetch=1,
            grid=(experts,),
            in_specs=[
                longer, wide,
                pl.BlockSpec((1, features, hidden), one),
                pl.BlockSpec((1, features, hidden), one),
                pl.BlockSpec((1, hidden, features), one),
            ],
            out_specs=[wide, longer, wide, narrow, narrow, narrow],
        ),
        out_shape=[
            shape(features), shape(features + LANES), shape(features), shape(hidden), shape(hidden), shape(hidden)
        ],
        compiler_params=params(),
        cost_estimate=cost(
            flops=12 * experts * rows * features * hidden,
            bytes_accessed=6 * experts * features * hidden + 10 * experts * rows * features,
            transcendentals=experts * rows * hidden,
        ),
        name="experts",
    )(rank, x_slots, dy_slots, w_gate, w_up, w_down)


def weight_kernel(count, products, step, core_ref, *refs):
    lefts, rights = refs[:count], refs[count : count * (1 + products)]
    outs, held_ref = refs[count * (1 + products) : -1], refs[-1]
    for i in range(products):
        total = sum(left_dot(lefts[m][0], rights[i * count + m][0]) for m in range(count))
        if step is None:
            outs[i][0] = total.astype(BF)
        else:
            held_ref[...] = total.astype(BF)
            halves(core_ref, held_ref, step, outs[2 * i].at[0], outs[2 * i + 1].at[0])


def weight_pass(core, step, depth, lefts, *rights):
    experts, rows, width = rights[0][0].shape
    one = lambda e, s: (e, 0, 0)
    count, products = len(lefts), len(rights)
    part = depth if step is None else depth // 2
    copies = products if step is None else 2 * products
    half = jax.ShapeDtypeStruct((experts, part, width), BF)
    return pl.pallas_call(
        partial(weight_kernel, count, products, step),
        grid_spec=pltpu.PrefetchScalarGridSpec(
            num_scalar_prefetch=1,
            grid=(experts,),
            in_specs=[
                *[pl.BlockSpec((1, rows, depth), one) for _ in lefts],
                *[pl.BlockSpec((1, rows, width), one) for right in rights for _ in right],
            ],
            out_specs=[pl.BlockSpec((1, part, width), one)] * copies,
            scratch_shapes=[pltpu.VMEM((depth, width), BF)],
        ),
        out_shape=[half] * copies,
        compiler_params=params(),
        cost_estimate=cost(
            flops=2 * count * products * experts * rows * depth * width,
            bytes_accessed=2 * experts * (products * depth * width + count * rows * (depth + products * width)),
            transcendentals=0,
        ),
        name="expert_weights",
    )(core, *lefts, *[a for right in rights for a in right])


def split_kernel(sums_ref, query_ref, key_ref, value_ref, router_ref, gains_ref, out_ref):
    part = lambda start, width: sums_ref[:, start : start + width].astype(F32)
    small = QD + 2 * KD
    query_ref[...] = part(0, QD)
    key_ref[...] = part(QD, KD)
    value_ref[...] = part(QD + KD, KD)
    table = part(small, LANES)
    router_ref[...] = table[:, :EXPERTS]
    gains_ref[...] = table[:, EXPERTS : EXPERTS + 2]
    out_ref[...] = part(small + LANES, out_ref.shape[1])


def split_dense(sums):
    rows, width = sums.shape
    shape = lambda n: jax.ShapeDtypeStruct((rows, n), F32)
    widths = (QD, KD, KD, EXPERTS, 2, width - QD - 2 * KD - LANES)
    return pl.pallas_call(
        split_kernel,
        out_shape=[shape(n) for n in widths],
        compiler_params=params(),
        cost_estimate=cost(flops=0, bytes_accessed=6 * rows * width, transcendentals=0),
        name="split_dense",
    )(sums)


def fold_kernel(cut, step, place_ref, keep_ref, got_ref, *outs):
    x_place, y_place = place_ref[0], place_ref[1]

    def put(out_ref, slot, block):
        rows = pl.ds(pl.multiple_of(block * step, step), step)
        total = keep_ref[0, rows, :].astype(F32) + got_ref[0, rows, :].astype(F32)
        out_ref[0, slot * step : (slot + 1) * step, :] = total.astype(BF)

    first = pl.program_id(0) < cut

    @pl.when(first)
    def _():
        for y in range(2):
            put(outs[0], y, 2 * y + x_place)
            put(outs[1], y, 2 * y + 1 - x_place)

    @pl.when(jnp.logical_not(first))
    def _():
        for x in range(2):
            put(outs[2], x, 2 * y_place + x)
            put(outs[3], x, 2 * (1 - y_place) + x)


def fold(places, keep, got, tile=None):
    some, rows, width = keep.shape
    step = rows // 4
    count = some if tile is None else width // tile
    cut = (count + 1) // 2
    size = width if tile is None else tile
    place = (lambda i: (i, 0, 0)) if tile is None else (lambda i: (0, 0, i))
    block = lambda high, index: pl.BlockSpec((1, high, size), index)
    whole = block(rows, lambda i, s: place(i))
    one = block(2 * step, lambda i, s: place(jnp.minimum(i, cut - 1)))
    two = block(2 * step, lambda i, s: place(jnp.maximum(i - cut, 0)))
    shape = lambda n: jax.ShapeDtypeStruct(
        (n, 2 * step, width) if tile is None else (some, 2 * step, n * tile), BF
    )
    return pl.pallas_call(
        partial(fold_kernel, cut, step),
        grid_spec=pltpu.PrefetchScalarGridSpec(
            num_scalar_prefetch=1,
            grid=(count,),
            in_specs=[whole, whole],
            out_specs=[one, one, two, two],
        ),
        out_shape=[shape(cut), shape(cut), shape(count - cut), shape(count - cut)],
        compiler_params=params(),
        cost_estimate=cost(
            flops=some * rows * width, bytes_accessed=6 * some * rows * width, transcendentals=0
        ),
        name="fold",
    )(places, keep, got)


def fold_again_kernel(step, place_ref, keep_ref, got_ref, stay_ref, go_ref):
    for out_ref, half in ((stay_ref, place_ref[0]), (go_ref, 1 - place_ref[0])):
        rows = pl.ds(pl.multiple_of(half * step, step), step)
        total = keep_ref[0, rows, :].astype(F32) + got_ref[0, rows, :].astype(F32)
        out_ref[0] = total.astype(BF)


def fold_again(place, keep, got):
    some, rows, width = keep.shape
    step = rows // 2
    tile = width
    while tile * rows > 2**19 and tile % 2 == 0 and tile // 2 % LANES == 0:
        tile //= 2
    index = lambda i, j, s: (i, 0, j)
    return pl.pallas_call(
        partial(fold_again_kernel, step),
        grid_spec=pltpu.PrefetchScalarGridSpec(
            num_scalar_prefetch=1,
            grid=(some, width // tile),
            in_specs=[pl.BlockSpec((1, rows, tile), index)] * 2,
            out_specs=[pl.BlockSpec((1, step, tile), index)] * 2,
        ),
        out_shape=[jax.ShapeDtypeStruct((some, step, width), BF)] * 2,
        compiler_params=params(),
        cost_estimate=cost(
            flops=some * rows * width, bytes_accessed=6 * some * rows * width, transcendentals=0
        ),
        name="fold_again",
    )(place, keep, got)


def after(value, *marks):
    return lax.optimization_barrier((value, *marks))[0]


def together(*values):
    return lax.optimization_barrier(values)


def local(
    tokens, out_grad, routes, attn_gain, w_query, w_key, w_value, w_out, moe_gain, w_router,
    w_gate, w_up, w_down,
):
    micros, _, features = tokens.shape
    count = lax.axis_size("expert")
    rank = lax.axis_index("expert")
    exp_dev = w_gate.shape[0]
    dp = lax.axis_size("dp")
    core = (lax.axis_index("dp") % 2).astype(jnp.int32)[None]
    seq_blocks = SEQ // BLOCK
    place = rank % seq_blocks
    cosine, sine = rotary_tables(place * BLOCK + jnp.arange(BLOCK, dtype=jnp.int32))
    place = place.astype(jnp.int32)[None]
    around = [(i, (i + 1) % count) for i in range(count)]
    upward = [(i, i + 1) for i in range(count - 1) if (i + 1) % seq_blocks]
    downward = [(b, a) for a, b in upward]
    ring = lambda a: lax.ppermute(a, "expert", around)
    later = lambda a: lax.ppermute(a, "expert", upward)
    earlier = lambda a: lax.ppermute(a, "expert", downward)
    add = lambda a, b: (a.astype(F32) + b.astype(F32)).astype(BF)
    every = lambda a, axis: lax.all_gather(a, axis, axis=0, tiled=True)
    swap = lambda a: lax.ppermute(a, "dp", [(i, i ^ 1) for i in range(dp)])
    same_core = [list(range(c, dp, 2)) for c in range(2)]
    across = lambda a, bit: lax.ppermute(a, "dp", [(i, i ^ bit) for i in range(dp)])
    x_place, y_place = lax.axis_index("dp") // 2 % 2, lax.axis_index("dp") // 4
    square = dp == 8

    places = jnp.stack([x_place, y_place]).astype(jnp.int32)

    share = lambda a: lax.psum_scatter(a, "dp", scatter_dimension=1, axis_index_groups=same_core, tiled=True)

    def fold_first(keep, got, tile=None):
        return list(fold(places, keep, got, tile)) if square else [add(keep, got)]

    def send_first(parts):
        if not square:
            return parts
        one, one_sent, two, two_sent = parts
        return [one, across(one_sent, 2), two, across(two_sent, 4)]

    def halve_first(keep, got, tile=None):
        return send_first(fold_first(keep, got, tile))

    def fold_second(parts):
        if not square:
            return parts
        return [*fold_again(places[1:], *parts[:2]), *fold_again(places[:1], *parts[2:])]

    def send_second(parts):
        if not square:
            return parts
        one, one_sent, two, two_sent = parts
        return [one, across(one_sent, 4), two, across(two_sent, 2)]

    def halve_second(parts):
        return send_second(fold_second(parts))

    def halve_last(parts, axis, dtype):
        if not square:
            return share(parts[0]).astype(dtype)
        total = lambda a, b: (a.astype(F32) + b.astype(F32)).astype(dtype)
        return jnp.concatenate([total(*parts[:2]), total(*parts[2:])], axis=axis)

    beside = jnp.zeros((w_router.shape[0], LANES - EXPERTS - 2), BF)
    weights = every(
        jnp.concatenate(
            [w_query, w_out, w_key, w_value, w_router, attn_gain[:, None], moe_gain[:, None], beside], axis=1
        ),
        "dp",
    )
    behind = QD + features + 2 * KD

    members = jnp.any(routes[:, :, :, None] == jnp.arange(EXPERTS, dtype=jnp.int32), axis=2)
    before = jnp.tril(jnp.ones((BLOCK, BLOCK), F32), -1).astype(BF)
    slots = jnp.einsum("ts,mse->mte", before, members.astype(BF), preferred_element_type=F32)
    slots = jnp.where(members, slots, -1.0).astype(BF)
    dy_sent = jnp.concatenate([out_grad, slots, jnp.zeros((micros, BLOCK, LANES - EXPERTS), BF)], axis=2)

    dy_ring = [dy_sent]
    for _ in range(count - 2):
        dy_ring.append(ring(dy_ring[-1]))
    router_w = weights[:, behind:]
    gains = router_w[:, EXPERTS : EXPERTS + 2].T.astype(F32)
    gain_one, gain_two = gains[0:1], gains[1:2]
    x_whole = tokens.reshape(micros * BLOCK, features)
    normed, scale_one = norm_rows(x_whole, gain_one)
    normed = after(normed, dy_ring[-1])
    kv_own = project(normed, weights, QD + features, 2 * KD, KD, cosine, sine)
    dy_last = [ring(dy_ring[-1][0])]
    kv_own = list(kv_own)
    kv_own[0], dy_last[0] = together(kv_own[0], dy_last[0])
    kv_one = [kv_own[0]]
    for _ in range(seq_blocks - 1):
        kv_one.append(later(kv_one[-1]))
    dy_last.append(ring(after(dy_ring[-1][1], kv_one[-1])))

    kv_two = [after(kv_own[1], kv_one[-1])]
    kv_two.append(later(kv_two[-1]))
    queries = list(project(after(normed, kv_one[-1]), weights, 0, QD, QD, cosine, sine))
    kv_two[-1], queries[0] = together(kv_two[-1], queries[0])
    kv_two.append(later(kv_two[-1]))
    o_one, ob_one, lse_one = attend(place, queries[0], kv_one)
    kv_two[-1], dy_last[1], ob_one = together(kv_two[-1], dy_last[1], ob_one)
    dy_ring.append(dy_last)
    kv_two.append(later(kv_two[-1]))
    go_out = lambda m, ob: outward(ob, weights, tokens[m], gain_two, router_w, routes[m])
    mids = [list(go_out(0, ob_one))]
    sent = [every(mids[0][1], "expert")]
    kv_two[-1], mids[0][1] = together(kv_two[-1], mids[0][1])
    while len(kv_two) < seq_blocks:
        kv_two.append(later(kv_two[-1]))
    def in_order(m):
        whole = jnp.zeros((count * BLOCK, features + LANES), BF)
        for step, block in enumerate(dy_ring):
            whole = lax.dynamic_update_slice_in_dim(whole, block[m], (rank - step) % count * BLOCK, 0)
        return whole

    slot_rows, dy_slots = [], []
    for m in range(micros):
        dy_all = in_order(m)
        table = lax.dynamic_slice_in_dim(dy_all, features + rank * exp_dev, exp_dev, 1)
        slot_rows.append(table.astype(F32).T)
        dy_slots.append(dispatch(slot_rows[m], dy_all, features))
    kv_two[-1], *dy_slots = together(kv_two[-1], *dy_slots)
    o_two, ob_two, lse_two = attend(place, queries[1], kv_two)
    mids.append(list(go_out(1, ob_two)))
    sent.append(every(mids[1][1], "expert"))
    kvs = (kv_one, kv_two)
    heads = ((o_one, ob_one, lse_one), (o_two, ob_two, lse_two))

    own = rank.astype(jnp.int32)[None]
    experts = lambda m, x: expert_pass(own, x, dy_slots[m], w_gate, w_up, w_down)
    ring_block = lambda sums, j: lax.dynamic_slice_in_dim(sums, (rank - 1 - j) % count * BLOCK, BLOCK, 0)
    x_one = dispatch(slot_rows[0], sent[0], features + LANES)
    ys_one, dx_one, gdy_one, act_one, dg_one, du_one = experts(0, x_one)
    dx_one = combine(slot_rows[0], dx_one)
    dx_home = [lax.psum_scatter(dx_one, "expert", scatter_dimension=0, tiled=True)]
    mixture_one = combine(slot_rows[0], after(ys_one, dx_one))
    sent[1], mixture_one = together(sent[1], mixture_one)
    x_two = dispatch(slot_rows[1], sent[1], features + LANES)
    ys_two, dx_two, gdy_two, act_two, dg_two, du_two = experts(1, x_two)

    hidden = w_down.shape[1]
    (new_down,) = weight_pass(core, None, hidden, (act_one, act_two), (gdy_one, gdy_two))
    new_down, dx_home[0] = together(new_down, dx_home[0])
    down_grad = lax.psum_scatter(new_down, "dp", scatter_dimension=1, tiled=True)
    dx_two = combine(slot_rows[1], after(dx_two, new_down))
    dx_held = ring(ring_block(dx_two, 0))
    ups = weight_pass(
        core, features // dp, features, (x_one, x_two), (after(dg_one, dx_two), dg_two), (du_one, du_two)
    )
    dx_held, *ups = together(dx_held, *ups)
    for step in range(1, count - 2):
        dx_held = ring(add(dx_held, ring_block(dx_two, step)))
    got_gate, got_up = swap(ups[1]), swap(ups[3])

    def back_home(m, dx):
        mid, _, scale_two, gates = mids[m]
        return home_back(dx, gates, mid, scale_two, out_grad[m], router_w, gain_two, weights)

    def back_heads(m, dob):
        o, _, lse = heads[m]
        dq, *pieces = attend_back(place, queries[m], dob, o, lse, cosine, sine, kvs[m])
        return dq, pieces[::-1]

    first = list(back_home(0, after(dx_home[0], ups[0])))
    dq_one, far_one = back_heads(0, first[2])
    dx_held, got_gate, got_up, dq_one = together(dx_held, got_gate, got_up, dq_one)
    dx_held = ring(add(dx_held, ring_block(dx_two, count - 2)))
    up_half = add(ups[2], got_up)
    dx_held, up_half = together(dx_held, up_half)
    up_grad = share(up_half)
    dx_home.append(add(dx_held, ring_block(dx_two, count - 1)))
    held = ring(ring_block(after(mixture_one, dx_held), 0))
    back_one = earlier(far_one[0])
    second = list(back_home(1, after(dx_home[1], up_half, dq_one)))
    back_one, second[2] = together(back_one, second[2])
    back_one = earlier(add(back_one, far_one[1]))
    dq_two, far_two = back_heads(1, second[2])
    back_one, dq_two, far_two[0], held, down_grad = together(back_one, dq_two, far_two[0], held, down_grad)
    for piece in far_one[2:-1]:
        back_one = earlier(add(back_one, piece))
    back_two = earlier(far_two[0])
    gate_parts = fold_first(after(ups[0], dq_two), got_gate)
    back_two, back_one, *gate_parts = together(back_two, back_one, *gate_parts)
    gate_sums = send_first(gate_parts)
    back_one = add(back_one, far_one[-1])
    back_two = earlier(add(back_two, far_two[1]))

    def back_last(m, dq, dkv, dmid):
        return last_back(
            dq, dkv, cosine, sine, weights, weights, tokens[m], scale_one[m * BLOCK : (m + 1) * BLOCK], gain_one, dmid
        )

    grad_x_one, dkv_one, dgain_one = back_last(0, dq_one, back_one, first[0])
    back_two, dkv_one = together(back_two, dkv_one)
    for piece in far_two[2:-1]:
        back_two = earlier(add(back_two, piece))
    mixture_two = combine(slot_rows[1], after(ys_two, dkv_one))
    back_two, mixture_two = together(back_two, mixture_two)
    back_two = add(back_two, far_two[-1])
    grad_x_two, dkv_two, dgain_two = back_last(1, dq_two, back_two, second[0])
    held = ring(add(after(held, mixture_two), ring_block(mixture_one, 1)))

    gain_rows = jnp.concatenate([dgain_one + dgain_two, first[4] + second[4]], axis=0)
    gain_columns = jnp.pad(gain_rows.T, ((0, 0), (EXPERTS, LANES - EXPERTS - 2)))
    keep, send = dense_grads(
        core, features // dp, [normed] * micros, [dq_one, dq_two], [dkv_one, dkv_two], [k[1] for k in mids],
        [first[3], second[3]], [h[1] for h in heads], [first[1], second[1]], gain_columns,
    )
    held, keep, send, *gate_sums = together(held, keep, send, *gate_sums)
    for step in range(2, count - 1):
        held = ring(add(held, ring_block(mixture_one, step)))
    got = swap(send)
    got, up_grad = together(got, up_grad)
    dense_sums = halve_first(keep[None], got[None], 3 * LANES)
    held = together(held, dense_sums[0])[0]
    mixtures = [add(held, ring_block(mixture_one, count - 1))]
    held = ring(ring_block(mixture_two, 0))
    held = ring(add(held, ring_block(mixture_two, 1)))
    gate_parts = fold_second([after(a, dense_sums[0]) for a in gate_sums])
    each = len(gate_parts)
    held, *rest = together(held, *gate_parts, *dense_sums)
    gate_parts, dense_sums = rest[:each], halve_second(rest[each:])
    held = after(held, *dense_sums[::2])
    for step in range(2, count - 1):
        held = ring(add(held, ring_block(mixture_two, step)))
    held, *dense_sums = together(held, *dense_sums)
    mixtures.append(add(held, ring_block(mixture_two, count - 1)))
    dense_sum = halve_last(dense_sums, 2, BF)[0]
    gate_sums = send_second(together(*gate_parts, dense_sum)[:-1])
    gate_grad = halve_last(gate_sums, 0, F32)
    up_grad, down_grad = up_grad.astype(F32), down_grad.astype(F32)
    dense = split_dense(lax.psum(dense_sum, "expert"))
    query, key, value, router, gain_columns, out = dense
    mixed = [(mids[m][0] + mixtures[m].astype(F32)).astype(BF) for m in range(micros)]
    return (
        jnp.stack(mixed),
        jnp.stack([grad_x_one, grad_x_two]),
        gain_columns[:, 0],
        query,
        key,
        value,
        out,
        gain_columns[:, 1],
        router,
        gate_grad,
        up_grad,
        down_grad,
    )


def solution(mesh):
    rows = P(None, ("dp", "expert"), None)
    return jax.shard_map(
        local,
        mesh=mesh,
        in_specs=(
            rows, rows, rows, P("dp"), P("dp", None), P("dp", None), P("dp", None), P("dp", None),
            P("dp"), P("dp", None),
            P("expert", None, None), P("expert", None, None), P("expert", None, None),
        ),
        out_specs=(
            rows, rows, P("dp"), P("dp", None), P("dp", None), P("dp", None), P("dp", None),
            P("dp"), P("dp", None),
            P("expert", "dp", None), P("expert", "dp", None), P("expert", "dp", None),
        ),
        check_vma=False,
    )
```

```python
from functools import partial

import jax
import jax.numpy as jnp
from jax import lax
from jax.experimental import pallas as pl
from jax.experimental.pallas import tpu as pltpu
from jax.sharding import PartitionSpec as P

HEADS = 24
KV_HEADS = 8
HEAD = 64
FF = 512
EXPERTS = 40
TOP = 8
BLOCK = 256
SEQ = 1024
CAP = 64
QD = 1536
KD = 512

EPSILON = 1e-06
ROPE_BASE = 10000.0
NEGATIVE = -1e30
LANES = 128
COLUMNS = 256
VMEM_LIMIT = 56 * 2**20
COST_SCALE = 0.1

BF = jnp.bfloat16
F32 = jnp.float32


def dense_dot(left, right):
    return jnp.dot(left, right, preferred_element_type=F32)


def left_dot(left, right):
    return lax.dot_general(left, right, (((0,), (0,)), ((), ())), preferred_element_type=F32)


def right_dot(left, right):
    return lax.dot_general(left, right, (((1,), (1,)), ((), ())), preferred_element_type=F32)


def rotary_tables(positions):
    half_size = HEAD // 2
    frequency = ROPE_BASE ** (-jnp.arange(half_size, dtype=F32) / half_size)
    angle = positions.astype(F32)[:, None] * frequency[None, :]
    cosine, sine = jnp.cos(angle), jnp.sin(angle)
    tiles = LANES // HEAD
    return (
        jnp.concatenate([cosine, cosine] * tiles, axis=1),
        jnp.concatenate([-sine, sine] * tiles, axis=1),
    )


def cost(flops, bytes_accessed, transcendentals):
    scale = lambda n: int(n * COST_SCALE)
    return pl.CostEstimate(
        flops=scale(flops), bytes_accessed=scale(bytes_accessed), transcendentals=scale(transcendentals)
    )


def params(limit=VMEM_LIMIT):
    return pltpu.CompilerParams(vmem_limit_bytes=limit)


def swap_halves(values):
    lane = lax.broadcasted_iota(jnp.int32, values.shape, 1)
    half = HEAD // 2
    return jnp.where(
        lane % HEAD < half,
        pltpu.roll(values, LANES - half, 1),
        pltpu.roll(values, half, 1),
    )


def turn(values, cosine, sine):
    return values * cosine + swap_halves(values) * sine


def norm_kernel(x_ref, gain_ref, normed_ref, scale_ref):
    rows = x_ref[...].astype(F32)
    scale = lax.rsqrt(jnp.mean(rows * rows, axis=1, keepdims=True) + EPSILON)
    scale_ref[...] = scale
    normed_ref[...] = (rows * scale * gain_ref[...]).astype(BF)


def norm_rows(x, gain):
    total, features = x.shape
    return pl.pallas_call(
        norm_kernel,
        grid=(total // BLOCK,),
        in_specs=[
            pl.BlockSpec((BLOCK, features), lambda i: (i, 0)),
            pl.BlockSpec((1, features), lambda i: (0, 0)),
        ],
        out_specs=[
            pl.BlockSpec((BLOCK, features), lambda i: (i, 0)),
            pl.BlockSpec((BLOCK, 1), lambda i: (i, 0)),
        ],
        out_shape=[
            jax.ShapeDtypeStruct((total, features), BF),
            jax.ShapeDtypeStruct((total, 1), F32),
        ],
        compiler_params=params(),
        cost_estimate=cost(flops=5 * total * features, bytes_accessed=4 * total * features, transcendentals=0),
        name="norm",
    )(x, gain)


def project_kernel(turned, normed_ref, w_ref, cosine_ref, sine_ref, *outs):
    tile = w_ref.shape[1]
    rows = dense_dot(normed_ref[...], w_ref[...])

    def write(turning):
        for start in range(0, tile, LANES):
            for m, out_ref in enumerate(outs):
                part = rows[m * BLOCK : (m + 1) * BLOCK, start : start + LANES]
                if turning:
                    part = turn(part, cosine_ref[...], sine_ref[...])
                out_ref[:, start : start + LANES] = part.astype(BF)

    pl.when(pl.program_id(0) < turned)(lambda: write(True))
    pl.when(pl.program_id(0) >= turned)(lambda: write(False))


def project(normed, weight, start, columns, turned_columns, cosine, sine):
    total, features = normed.shape
    tile = 2 * COLUMNS
    micros = total // BLOCK
    return pl.pallas_call(
        partial(project_kernel, turned_columns // tile),
        grid=(columns // tile,),
        in_specs=[
            pl.BlockSpec((total, features), lambda j: (0, 0)),
            pl.BlockSpec((features, tile), lambda j: (0, start // tile + j)),
            pl.BlockSpec((BLOCK, LANES), lambda j: (0, 0)),
            pl.BlockSpec((BLOCK, LANES), lambda j: (0, 0)),
        ],
        out_specs=[pl.BlockSpec((BLOCK, tile), lambda j: (0, j))] * micros,
        out_shape=[jax.ShapeDtypeStruct((BLOCK, columns), BF)] * micros,
        compiler_params=params(),
        cost_estimate=cost(
            flops=2 * total * features * columns,
            bytes_accessed=2 * (features * columns + total * (features + columns)),
            transcendentals=0,
        ),
        name="project",
    )(normed, weight, cosine, sine)


def outward_kernel(ob_ref, w_ref, x_ref, gain_ref, router_ref, routes_ref, mid_ref, sent_ref, scale_ref, gates_ref):
    j = pl.program_id(0)
    tile = w_ref.shape[1]
    features = mid_ref.shape[1]
    where = pl.ds(pl.multiple_of(j * tile, tile), tile)
    mid_ref[:, where] = x_ref[:, where].astype(F32) + dense_dot(ob_ref[...], w_ref[...])

    @pl.when(j == pl.num_programs(0) - 1)
    def _():
        mid = mid_ref[...]
        scale = lax.rsqrt(jnp.mean(mid * mid, axis=1, keepdims=True) + EPSILON)
        scale_ref[...] = scale
        normed = (mid * scale * gain_ref[...]).astype(BF)
        sent_ref[:, :features] = normed
        lane = lax.broadcasted_iota(jnp.int32, (BLOCK, LANES), 1)
        routes = routes_ref[...]
        member = lane == routes[:, 0:1]
        for k in range(1, TOP):
            member = jnp.logical_or(member, lane == routes[:, k : k + 1])
        logits = jnp.where(member, dense_dot(normed, router_ref[...]), NEGATIVE)
        weights = jnp.exp(logits - jnp.max(logits, axis=1, keepdims=True))
        weights = jnp.where(member, weights, 0.0)
        gates = weights / jnp.sum(weights, axis=1, keepdims=True)
        gates_ref[...] = gates
        high = gates.astype(BF).astype(F32)
        sent_ref[:, features:] = (high + pltpu.roll(gates - high, EXPERTS, 1)).astype(BF)


def outward(ob, w_qo, x, gain, router, routes):
    features = x.shape[1]
    tile = 2 * COLUMNS
    whole = lambda a: pl.BlockSpec(a.shape, lambda j: (0, 0))
    fixed = lambda *shape: pl.BlockSpec(shape, lambda j: (0, 0))
    return pl.pallas_call(
        outward_kernel,
        grid=(features // tile,),
        in_specs=[
            whole(ob),
            pl.BlockSpec((QD, tile), lambda j: (0, QD // tile + j)),
            whole(x), whole(gain), whole(router), whole(routes),
        ],
        out_specs=[fixed(BLOCK, features), fixed(BLOCK, features + LANES), fixed(BLOCK, 1), fixed(BLOCK, LANES)],
        out_shape=[
            jax.ShapeDtypeStruct((BLOCK, features), F32),
            jax.ShapeDtypeStruct((BLOCK, features + LANES), BF),
            jax.ShapeDtypeStruct((BLOCK, 1), F32),
            jax.ShapeDtypeStruct((BLOCK, LANES), F32),
        ],
        compiler_params=params(),
        cost_estimate=cost(
            flops=2 * BLOCK * features * QD, bytes_accessed=2 * features * QD + 14 * BLOCK * features, transcendentals=0
        ),
        name="outward",
    )(ob, w_qo, x, gain, router, routes)


def home_kernel(
    dx_ref, gates_ref, mid_ref, scale_ref, dy_ref, router_ref, gain_ref, w_ref,
    dmid_ref, da_ref, dob_ref, dlog_ref, dgain_ref,
):
    j = pl.program_id(0)
    features = mid_ref.shape[1]
    tile = w_ref.shape[0]

    @pl.when(j == 0)
    def _():
        table = dx_ref[:, features:].astype(F32)
        dgates = table + pltpu.roll(table, LANES - EXPERTS, 1)
        gates = gates_ref[...]
        dc = gates * (dgates - jnp.sum(gates * dgates, axis=1, keepdims=True))
        dlog = dc.astype(BF)
        dlog_ref[...] = dlog
        dnormed = dx_ref[:, :features].astype(F32) + right_dot(dlog, router_ref[...])
        mid = mid_ref[...]
        scale = scale_ref[...]
        dgain_ref[...] = jnp.sum(dnormed * mid * scale, axis=0, keepdims=True)
        scaled = dnormed * gain_ref[...]
        mean = jnp.mean(scaled * mid, axis=1, keepdims=True)
        dmid = dy_ref[...].astype(F32) + scale * scaled - mid * (scale * scale * scale * mean)
        dmid_ref[...] = dmid
        da_ref[...] = dmid.astype(BF)

    where = pl.ds(pl.multiple_of(j * tile, tile), tile)
    dob_ref[:, where] = right_dot(da_ref[...], w_ref[...]).astype(BF)


def home_back(dx, gates, mid, scale, dy, router, gain, w_qo):
    features = mid.shape[1]
    tile = 2 * COLUMNS
    whole = lambda a: pl.BlockSpec(a.shape, lambda j: (0, 0))
    fixed = lambda *shape: pl.BlockSpec(shape, lambda j: (0, 0))
    return pl.pallas_call(
        home_kernel,
        grid=(QD // tile,),
        in_specs=[
            whole(dx), whole(gates), whole(mid), whole(scale), whole(dy), whole(router), whole(gain),
            pl.BlockSpec((tile, features), lambda j: (j, 1)),
        ],
        out_specs=[
            fixed(BLOCK, features), fixed(BLOCK, features), fixed(BLOCK, QD), fixed(BLOCK, LANES), fixed(1, features),
        ],
        out_shape=[
            jax.ShapeDtypeStruct((BLOCK, features), F32),
            jax.ShapeDtypeStruct((BLOCK, features), BF),
            jax.ShapeDtypeStruct((BLOCK, QD), BF),
            jax.ShapeDtypeStruct((BLOCK, LANES), BF),
            jax.ShapeDtypeStruct((1, features), F32),
        ],
        compiler_params=params(),
        cost_estimate=cost(
            flops=2 * BLOCK * features * QD, bytes_accessed=2 * features * QD + 18 * BLOCK * features, transcendentals=0
        ),
        name="home_back",
    )(dx, gates, mid, scale, dy, router, gain, w_qo)


def last_kernel(
    dq_ref, dkv_ref, cosine_ref, sine_ref, wq_ref, wkv_ref, x_ref, scale_ref, gain_ref, dmid_ref,
    dx_ref, dkvb_ref, dgain_ref,
):
    j = pl.program_id(0)
    tile = wq_ref.shape[0]

    @pl.when(j == 0)
    def _():
        for start in range(0, KD, LANES):
            part = dkv_ref[0, :, start : start + LANES].astype(F32)
            dkvb_ref[:, start : start + LANES] = turn(part, cosine_ref[...], -sine_ref[...]).astype(BF)
        dkvb_ref[:, KD:] = dkv_ref[1]

    where = pl.ds(pl.multiple_of(j * tile, tile), tile)
    dx_ref[:, where] = right_dot(dq_ref[...], wq_ref[...]) + right_dot(dkvb_ref[...], wkv_ref[...])

    @pl.when(j == pl.num_programs(0) - 1)
    def _():
        dnormed = dx_ref[...]
        rows = x_ref[...].astype(F32)
        scale = scale_ref[...]
        dgain_ref[...] = jnp.sum(dnormed * rows * scale, axis=0, keepdims=True)
        scaled = dnormed * gain_ref[...]
        mean = jnp.mean(scaled * rows, axis=1, keepdims=True)
        dx_ref[...] = dmid_ref[...] + scale * scaled - rows * (scale * scale * scale * mean)


def last_back(dq, dkv, cosine, sine, w_q, w_kv, x, scale, gain, dmid):
    features = x.shape[1]
    tile = 2 * COLUMNS
    whole = lambda a: pl.BlockSpec(a.shape, lambda j: (0,) * a.ndim)
    fixed = lambda *shape: pl.BlockSpec(shape, lambda j: (0, 0))
    return pl.pallas_call(
        last_kernel,
        grid=(features // tile,),
        in_specs=[
            whole(dq), whole(dkv), whole(cosine), whole(sine),
            pl.BlockSpec((tile, QD), lambda j: (j, 0)),
            pl.BlockSpec((tile, 2 * KD), lambda j: (j, QD // KD)),
            whole(x), whole(scale), whole(gain), whole(dmid),
        ],
        out_specs=[fixed(BLOCK, features), fixed(BLOCK, 2 * KD), fixed(1, features)],
        out_shape=[
            jax.ShapeDtypeStruct((BLOCK, features), F32),
            jax.ShapeDtypeStruct((BLOCK, 2 * KD), BF),
            jax.ShapeDtypeStruct((1, features), F32),
        ],
        compiler_params=params(),
        cost_estimate=cost(
            flops=2 * BLOCK * features * (QD + 2 * KD),
            bytes_accessed=2 * features * (QD + 2 * KD) + 16 * BLOCK * features,
            transcendentals=0,
        ),
        name="last_back",
    )(dq, dkv, cosine, sine, w_q, w_kv, x, scale, gain, dmid)


def halves(core_ref, held_ref, step, keep_ref, send_ref):
    core = core_ref[0]
    for q in range(held_ref.shape[0] // (2 * step)):
        mine = pl.multiple_of((2 * q + core) * step, step)
        other = pl.multiple_of((2 * q + 1 - core) * step, step)
        keep_ref[q * step : (q + 1) * step, :] = held_ref[pl.ds(mine, step), :]
        send_ref[q * step : (q + 1) * step, :] = held_ref[pl.ds(other, step), :]


def dense_kernel(micros, step, core_ref, *refs):
    ins, (gains_ref, keep_ref, send_ref, held_ref) = refs[: 7 * micros], refs[7 * micros :]
    normed, dq, dkv, sent, dlog, ob, da = (ins[i * micros : (i + 1) * micros] for i in range(7))

    def total(lefts, rights):
        return sum(left_dot(left[...], right[...]) for left, right in zip(lefts, rights))

    start = 0
    for lefts, rights in ((normed, dq), (normed, dkv), (sent, dlog), (ob, da)):
        width = rights[0].shape[1]
        part = total(lefts, rights)
        if rights is dlog:
            part = part + gains_ref[...]
        held_ref[:, start : start + width] = part.astype(BF)
        start += width
    halves(core_ref, held_ref, step, keep_ref, send_ref)


def dense_grads(core, step, normed, dq, dkv, sent, dlog, ob, da, gains):
    groups = (normed, dq, dkv, sent, dlog, ob, da)
    micros = len(dq)
    tile = max(3 * LANES, 2 * step)
    lefts = (True, False, False, True, False, True, False)
    width = sum(group[0].shape[1] for group, left in zip(groups, lefts) if not left)
    specs = []
    for group, left in zip(groups, lefts):
        for m, a in enumerate(group):
            if left:
                block = m if a.shape[0] > BLOCK else 0
                specs.append(pl.BlockSpec((BLOCK, tile), lambda j, s, block=block: (block, j)))
            else:
                specs.append(pl.BlockSpec(a.shape, lambda j, s: (0, 0)))
    half = jax.ShapeDtypeStruct((QD // 2, width), BF)
    return pl.pallas_call(
        partial(dense_kernel, micros, step),
        grid_spec=pltpu.PrefetchScalarGridSpec(
            num_scalar_prefetch=1,
            grid=(QD // tile,),
            in_specs=[*specs, pl.BlockSpec((tile, gains.shape[1]), lambda j, s: (j, 0))],
            out_specs=[pl.BlockSpec((tile // 2, width), lambda j, s: (j, 0))] * 2,
            scratch_shapes=[pltpu.VMEM((tile, width), BF)],
        ),
        out_shape=[half, half],
        compiler_params=params(),
        cost_estimate=cost(
            flops=2 * micros * BLOCK * QD * width,
            bytes_accessed=2 * QD * width + 4 * micros * BLOCK * (QD + width),
            transcendentals=0,
        ),
        name="dense_grads",
    )(core, *[a for group in groups for a in group], gains)


PAIR = 2 * HEAD
GROUP = HEADS // KV_HEADS * PAIR


def spread(values):
    lane = lax.broadcasted_iota(jnp.int32, (BLOCK, LANES), 1)
    first = lane < HEAD
    zero = jnp.zeros((BLOCK, LANES), F32)
    one, two, three = (values[:, i * LANES : (i + 1) * LANES] for i in range(3))
    return jnp.concatenate(
        [
            jnp.where(first, one, zero),
            jnp.where(first, pltpu.roll(one, HEAD, 1), zero),
            jnp.where(first, two, zero),
            jnp.where(first, zero, two),
            jnp.where(first, zero, pltpu.roll(three, HEAD, 1)),
            jnp.where(first, zero, three),
        ],
        axis=0,
    )


def gather_heads(rows):
    lane = lax.broadcasted_iota(jnp.int32, (BLOCK, LANES), 1)
    first = lane < HEAD
    part = [rows[i * BLOCK : (i + 1) * BLOCK] for i in range(6)]
    return (
        jnp.where(first, part[0], pltpu.roll(part[1], HEAD, 1)),
        jnp.where(first, part[2], part[3]),
        jnp.where(first, pltpu.roll(part[4], HEAD, 1), part[5]),
    )


def attend_kernel(place_ref, q_ref, *refs):
    blocks = SEQ // BLOCK
    keys, values = refs[:blocks], refs[blocks : 2 * blocks]
    o_ref, ob_ref, lse_ref, max_ref, sum_ref, acc_ref = refs[2 * blocks :]
    query = spread(q_ref[...].astype(F32) * HEAD ** (-0.5)).astype(BF)
    for r in range(blocks):

        @pl.when(place_ref[0] >= r)
        def _():
            scores = right_dot(keys[r][...], query)
            top = jnp.max(scores, axis=0, keepdims=True)
            if r > 0:
                before = max_ref[...]
                top = jnp.maximum(top, before)
            weights = jnp.exp(scores - top)
            total = jnp.sum(weights, axis=0, keepdims=True)
            out = left_dot(values[r][...], weights.astype(BF))
            if r > 0:
                factor = jnp.exp(before - top)
                total = total + sum_ref[...] * factor
                out = out + acc_ref[...] * factor
            max_ref[...] = top
            sum_ref[...] = total
            acc_ref[...] = out

    lse_ref[0] = max_ref[...] + jnp.log(sum_ref[...])
    rows = jnp.transpose(acc_ref[...] / sum_ref[...])
    for i, part in enumerate(gather_heads(rows)):
        o_ref[:, i * LANES : (i + 1) * LANES] = part
        ob_ref[:, i * LANES : (i + 1) * LANES] = part.astype(BF)


def attend(place, query, kvs):
    pairs = KV_HEADS // 2
    rows = 6 * BLOCK
    return pl.pallas_call(
        attend_kernel,
        grid_spec=pltpu.PrefetchScalarGridSpec(
            num_scalar_prefetch=1,
            grid=(pairs,),
            in_specs=[
                pl.BlockSpec((BLOCK, GROUP), lambda p, s: (0, p)),
                *[pl.BlockSpec((BLOCK, PAIR), lambda p, s: (0, p)) for _ in kvs],
                *[pl.BlockSpec((BLOCK, PAIR), lambda p, s: (0, KV_HEADS // 2 + p)) for _ in kvs],
            ],
            out_specs=[
                pl.BlockSpec((BLOCK, GROUP), lambda p, s: (0, p)),
                pl.BlockSpec((BLOCK, GROUP), lambda p, s: (0, p)),
                pl.BlockSpec((1, 1, rows), lambda p, s: (p, 0, 0)),
            ],
            scratch_shapes=[
                pltpu.VMEM((1, rows), F32),
                pltpu.VMEM((1, rows), F32),
                pltpu.VMEM((PAIR, rows), F32),
            ],
        ),
        out_shape=[
            jax.ShapeDtypeStruct((BLOCK, QD), F32),
            jax.ShapeDtypeStruct((BLOCK, QD), BF),
            jax.ShapeDtypeStruct((pairs, 1, rows), F32),
        ],
        compiler_params=params(),
        cost_estimate=cost(
            flops=8 * SEQ * BLOCK * HEADS * PAIR, bytes_accessed=10 * BLOCK * QD, transcendentals=SEQ * BLOCK * HEADS
        ),
        name="attend",
    )(place, query, *kvs, *kvs)


def attend_back_kernel(place_ref, q_ref, dob_ref, o_ref, lse_ref, cosine_ref, sine_ref, *refs):
    blocks = SEQ // BLOCK
    keys, values = refs[:blocks], refs[blocks : 2 * blocks]
    dq_ref, outs, acc_ref = refs[2 * blocks], refs[2 * blocks + 1 : 3 * blocks + 1], refs[-1]
    query = spread(q_ref[...].astype(F32) * HEAD ** (-0.5)).astype(BF)
    grads = spread(dob_ref[...].astype(F32))
    delta = jnp.sum(jnp.transpose(grads * spread(o_ref[...])), axis=0, keepdims=True)
    grads = grads.astype(BF)
    for r in range(blocks):

        @pl.when(place_ref[0] >= r)
        def _():
            key = keys[r][...]
            weights = jnp.exp(right_dot(key, query) - lse_ref[0])
            dscores = (weights * (right_dot(values[r][...], grads) - delta)).astype(BF)
            outs[r][0] = dense_dot(dscores, query).astype(BF)
            outs[r][1] = dense_dot(weights.astype(BF), grads).astype(BF)
            part = left_dot(key, dscores)
            acc_ref[...] = part if r == 0 else acc_ref[...] + part

        @pl.when(place_ref[0] < r)
        def _():
            outs[r][...] = jnp.zeros(outs[r].shape, BF)

    rows = jnp.transpose(acc_ref[...]) * HEAD ** (-0.5)
    for i, part in enumerate(gather_heads(rows)):
        dq_ref[:, i * LANES : (i + 1) * LANES] = turn(part, cosine_ref[...], -sine_ref[...]).astype(BF)


def attend_back(place, query, dob, o, lse, cosine, sine, kvs):
    pairs = KV_HEADS // 2
    rows = 6 * BLOCK
    heads = pl.BlockSpec((BLOCK, GROUP), lambda p, s: (0, p))
    table = pl.BlockSpec((BLOCK, LANES), lambda p, s: (0, 0))
    return pl.pallas_call(
        attend_back_kernel,
        grid_spec=pltpu.PrefetchScalarGridSpec(
            num_scalar_prefetch=1,
            grid=(pairs,),
            in_specs=[
                heads, heads, heads,
                pl.BlockSpec((1, 1, rows), lambda p, s: (p, 0, 0)),
                table, table,
                *[pl.BlockSpec((BLOCK, PAIR), lambda p, s: (0, p)) for _ in kvs],
                *[pl.BlockSpec((BLOCK, PAIR), lambda p, s: (0, KV_HEADS // 2 + p)) for _ in kvs],
            ],
            out_specs=[heads, *[pl.BlockSpec((2, BLOCK, PAIR), lambda p, s: (0, 0, p)) for _ in kvs]],
            scratch_shapes=[pltpu.VMEM((PAIR, rows), F32)],
        ),
        out_shape=[
            jax.ShapeDtypeStruct((BLOCK, QD), BF),
            *[jax.ShapeDtypeStruct((2, BLOCK, KD), BF) for _ in kvs],
        ],
        compiler_params=params(),
        cost_estimate=cost(
            flops=20 * SEQ * BLOCK * HEADS * PAIR, bytes_accessed=14 * BLOCK * QD, transcendentals=SEQ * BLOCK * HEADS
        ),
        name="attend_back",
    )(place, query, dob, o, lse, cosine, sine, *kvs, *kvs)


def picks(slot_rows):
    slots = lax.broadcasted_iota(jnp.int32, (CAP, BLOCK), 0).astype(F32)
    one, zero = jnp.float32(1), jnp.float32(0)
    return [jnp.where(slots == slot_rows[e : e + 1, :], one, zero) for e in range(slot_rows.shape[0])]


def dispatch_kernel(slot_ref, rows_ref, out_ref):
    experts = slot_ref.shape[0]
    chosen = jnp.concatenate([p.astype(BF) for p in picks(slot_ref[...])], axis=0)
    width = out_ref.shape[2]
    for start in range(0, width, COLUMNS):
        size = min(COLUMNS, width - start)
        rows = dense_dot(chosen, rows_ref[:, start : start + size])
        out_ref[:, :, start : start + size] = rows.astype(BF).reshape(experts, CAP, size)


def dispatch(slot_rows, rows, features):
    experts, total = slot_rows.shape
    blocks = total // BLOCK
    return pl.pallas_call(
        dispatch_kernel,
        grid=(blocks,),
        in_specs=[
            pl.BlockSpec((experts, BLOCK), lambda b: (0, b)),
            pl.BlockSpec((BLOCK, features), lambda b: (b, 0)),
        ],
        out_specs=pl.BlockSpec((experts, CAP, features), lambda b: (0, b, 0)),
        out_shape=jax.ShapeDtypeStruct((experts, blocks * CAP, features), BF),
        compiler_params=params(),
        cost_estimate=cost(
            flops=2 * experts * CAP * total * features,
            bytes_accessed=2 * features * (total + experts * blocks * CAP),
            transcendentals=0,
        ),
        name="dispatch",
    )(slot_rows, rows)


def combine_kernel(slot_ref, slots_ref, out_ref):
    experts, features = slots_ref.shape[0], slots_ref.shape[2]
    chosen = jnp.concatenate([p.astype(BF) for p in picks(slot_ref[...])], axis=0)
    for start in range(0, features, COLUMNS):
        size = min(COLUMNS, features - start)
        held = slots_ref[:, :, start : start + size].reshape(experts * CAP, size)
        out_ref[:, start : start + size] = left_dot(chosen, held).astype(BF)


def combine(slot_rows, slots):
    experts, total = slot_rows.shape
    blocks = total // BLOCK
    features = slots.shape[2]
    return pl.pallas_call(
        combine_kernel,
        grid=(blocks,),
        in_specs=[
            pl.BlockSpec((experts, BLOCK), lambda b: (0, b)),
            pl.BlockSpec((experts, CAP, features), lambda b: (0, b, 0)),
        ],
        out_specs=pl.BlockSpec((BLOCK, features), lambda b: (b, 0)),
        out_shape=jax.ShapeDtypeStruct((total, features), BF),
        compiler_params=params(),
        cost_estimate=cost(
            flops=2 * experts * CAP * total * features,
            bytes_accessed=2 * features * (total + experts * blocks * CAP),
            transcendentals=0,
        ),
        name="combine",
    )(slot_rows, slots)


def expert_kernel(
    rank_ref, x_ref, dy_ref, wg_ref, wu_ref, wd_ref, ys_ref, dx_ref, gdy_ref, act_ref, dg_ref, du_ref
):
    features = dy_ref.shape[2]
    rows = x_ref[0, :, :features]
    pre = dense_dot(rows, wg_ref[0])
    up = dense_dot(rows, wu_ref[0])
    sigma = 1.0 / (1.0 + jnp.exp(-pre))
    silu = pre * sigma
    active = (silu * up).astype(BF)
    act_ref[0] = active
    column = rank_ref[0] * pl.num_programs(0) + pl.program_id(0)
    lane = lax.broadcasted_iota(jnp.int32, (rows.shape[0], LANES), 1)
    is_high, is_low = lane == column, lane == column + EXPERTS
    table = jnp.where(jnp.logical_or(is_high, is_low), x_ref[0, :, features:].astype(F32), 0.0)
    share = jnp.sum(table, axis=1, keepdims=True)
    result = dense_dot(active, wd_ref[0])
    grads = dy_ref[0].astype(F32)
    dots = jnp.sum(result * grads, axis=1, keepdims=True)
    high = dots.astype(BF).astype(F32)
    dx_ref[0, :, features:] = jnp.where(is_high, high, jnp.where(is_low, dots - high, 0.0)).astype(BF)
    ys_ref[0] = (result * share).astype(BF)
    gated = (grads * share).astype(BF)
    gdy_ref[0] = gated
    dact = right_dot(gated, wd_ref[0])
    dpre = (dact * up * sigma * (1.0 + pre * (1.0 - sigma))).astype(BF)
    dup = (dact * silu).astype(BF)
    dg_ref[0] = dpre
    du_ref[0] = dup
    dx_ref[0, :, :features] = (right_dot(dpre, wg_ref[0]) + right_dot(dup, wu_ref[0])).astype(BF)


def expert_pass(rank, x_slots, dy_slots, w_gate, w_up, w_down):
    experts, rows, features = dy_slots.shape
    hidden = w_gate.shape[2]
    one = lambda e, r: (e, 0, 0)
    longer = pl.BlockSpec((1, rows, features + LANES), one)
    wide = pl.BlockSpec((1, rows, features), one)
    narrow = pl.BlockSpec((1, rows, hidden), one)
    shape = lambda width: jax.ShapeDtypeStruct((experts, rows, width), BF)
    return pl.pallas_call(
        expert_kernel,
        grid_spec=pltpu.PrefetchScalarGridSpec(
            num_scalar_prefetch=1,
            grid=(experts,),
            in_specs=[
                longer, wide,
                pl.BlockSpec((1, features, hidden), one),
                pl.BlockSpec((1, features, hidden), one),
                pl.BlockSpec((1, hidden, features), one),
            ],
            out_specs=[wide, longer, wide, narrow, narrow, narrow],
        ),
        out_shape=[
            shape(features), shape(features + LANES), shape(features), shape(hidden), shape(hidden), shape(hidden)
        ],
        compiler_params=params(),
        cost_estimate=cost(
            flops=12 * experts * rows * features * hidden,
            bytes_accessed=6 * experts * features * hidden + 10 * experts * rows * features,
            transcendentals=experts * rows * hidden,
        ),
        name="experts",
    )(rank, x_slots, dy_slots, w_gate, w_up, w_down)


def weight_kernel(count, products, step, core_ref, *refs):
    lefts, rights = refs[:count], refs[count : count * (1 + products)]
    outs, held_ref = refs[count * (1 + products) : -1], refs[-1]
    for i in range(products):
        total = sum(left_dot(lefts[m][0], rights[i * count + m][0]) for m in range(count))
        if step is None:
            outs[i][0] = total.astype(BF)
        else:
            held_ref[...] = total.astype(BF)
            halves(core_ref, held_ref, step, outs[2 * i].at[0], outs[2 * i + 1].at[0])


def weight_pass(core, step, depth, lefts, *rights):
    experts, rows, width = rights[0][0].shape
    one = lambda e, s: (e, 0, 0)
    count, products = len(lefts), len(rights)
    part = depth if step is None else depth // 2
    copies = products if step is None else 2 * products
    half = jax.ShapeDtypeStruct((experts, part, width), BF)
    return pl.pallas_call(
        partial(weight_kernel, count, products, step),
        grid_spec=pltpu.PrefetchScalarGridSpec(
            num_scalar_prefetch=1,
            grid=(experts,),
            in_specs=[
                *[pl.BlockSpec((1, rows, depth), one) for _ in lefts],
                *[pl.BlockSpec((1, rows, width), one) for right in rights for _ in right],
            ],
            out_specs=[pl.BlockSpec((1, part, width), one)] * copies,
            scratch_shapes=[pltpu.VMEM((depth, width), BF)],
        ),
        out_shape=[half] * copies,
        compiler_params=params(),
        cost_estimate=cost(
            flops=2 * count * products * experts * rows * depth * width,
            bytes_accessed=2 * experts * (products * depth * width + count * rows * (depth + products * width)),
            transcendentals=0,
        ),
        name="expert_weights",
    )(core, *lefts, *[a for right in rights for a in right])


def split_kernel(sums_ref, query_ref, key_ref, value_ref, router_ref, gains_ref, out_ref):
    part = lambda start, width: sums_ref[:, start : start + width].astype(F32)
    small = QD + 2 * KD
    query_ref[...] = part(0, QD)
    key_ref[...] = part(QD, KD)
    value_ref[...] = part(QD + KD, KD)
    table = part(small, LANES)
    router_ref[...] = table[:, :EXPERTS]
    gains_ref[...] = table[:, EXPERTS : EXPERTS + 2]
    out_ref[...] = part(small + LANES, out_ref.shape[1])


def split_dense(sums):
    rows, width = sums.shape
    shape = lambda n: jax.ShapeDtypeStruct((rows, n), F32)
    widths = (QD, KD, KD, EXPERTS, 2, width - QD - 2 * KD - LANES)
    return pl.pallas_call(
        split_kernel,
        out_shape=[shape(n) for n in widths],
        compiler_params=params(),
        cost_estimate=cost(flops=0, bytes_accessed=6 * rows * width, transcendentals=0),
        name="split_dense",
    )(sums)


def fold_kernel(cut, step, place_ref, keep_ref, got_ref, *outs):
    x_place, y_place = place_ref[0], place_ref[1]

    def put(out_ref, slot, block):
        rows = pl.ds(pl.multiple_of(block * step, step), step)
        out_ref[0, slot * step : (slot + 1) * step, :] = keep_ref[0, rows, :] + got_ref[0, rows, :]

    first = pl.program_id(0) < cut

    @pl.when(first)
    def _():
        for y in range(2):
            put(outs[0], y, 2 * y + x_place)
            put(outs[1], y, 2 * y + 1 - x_place)

    @pl.when(jnp.logical_not(first))
    def _():
        for x in range(2):
            put(outs[2], x, 2 * y_place + x)
            put(outs[3], x, 2 * (1 - y_place) + x)


def fold(places, keep, got, tile=None):
    some, rows, width = keep.shape
    step = rows // 4
    count = some if tile is None else width // tile
    cut = (count + 1) // 2
    size = width if tile is None else tile
    place = (lambda i: (i, 0, 0)) if tile is None else (lambda i: (0, 0, i))
    block = lambda high, index: pl.BlockSpec((1, high, size), index)
    whole = block(rows, lambda i, s: place(i))
    one = block(2 * step, lambda i, s: place(jnp.minimum(i, cut - 1)))
    two = block(2 * step, lambda i, s: place(jnp.maximum(i - cut, 0)))
    shape = lambda n: jax.ShapeDtypeStruct(
        (n, 2 * step, width) if tile is None else (some, 2 * step, n * tile), BF
    )
    return pl.pallas_call(
        partial(fold_kernel, cut, step),
        grid_spec=pltpu.PrefetchScalarGridSpec(
            num_scalar_prefetch=1,
            grid=(count,),
            in_specs=[whole, whole],
            out_specs=[one, one, two, two],
        ),
        out_shape=[shape(cut), shape(cut), shape(count - cut), shape(count - cut)],
        compiler_params=params(),
        cost_estimate=cost(
            flops=some * rows * width, bytes_accessed=6 * some * rows * width, transcendentals=0
        ),
        name="fold",
    )(places, keep, got)


def fold_again_kernel(step, place_ref, keep_ref, got_ref, stay_ref, go_ref):
    for out_ref, half in ((stay_ref, place_ref[0]), (go_ref, 1 - place_ref[0])):
        rows = pl.ds(pl.multiple_of(half * step, step), step)
        out_ref[0] = keep_ref[0, rows, :] + got_ref[0, rows, :]


def fold_again(place, keep, got):
    some, rows, width = keep.shape
    step = rows // 2
    tile = width
    while tile * rows > 2**19 and tile % 2 == 0 and tile // 2 % LANES == 0:
        tile //= 2
    index = lambda i, j, s: (i, 0, j)
    return pl.pallas_call(
        partial(fold_again_kernel, step),
        grid_spec=pltpu.PrefetchScalarGridSpec(
            num_scalar_prefetch=1,
            grid=(some, width // tile),
            in_specs=[pl.BlockSpec((1, rows, tile), index)] * 2,
            out_specs=[pl.BlockSpec((1, step, tile), index)] * 2,
        ),
        out_shape=[jax.ShapeDtypeStruct((some, step, width), BF)] * 2,
        compiler_params=params(),
        cost_estimate=cost(
            flops=some * rows * width, bytes_accessed=6 * some * rows * width, transcendentals=0
        ),
        name="fold_again",
    )(place, keep, got)


def after(value, *marks):
    return lax.optimization_barrier((value, *marks))[0]


def together(*values):
    return lax.optimization_barrier(values)


def local(
    tokens, out_grad, routes, attn_gain, w_query, w_key, w_value, w_out, moe_gain, w_router,
    w_gate, w_up, w_down,
):
    micros, _, features = tokens.shape
    count = lax.axis_size("expert")
    rank = lax.axis_index("expert")
    exp_dev = w_gate.shape[0]
    dp = lax.axis_size("dp")
    core = (lax.axis_index("dp") % 2).astype(jnp.int32)[None]
    seq_blocks = SEQ // BLOCK
    place = rank % seq_blocks
    cosine, sine = rotary_tables(place * BLOCK + jnp.arange(BLOCK, dtype=jnp.int32))
    place = place.astype(jnp.int32)[None]
    around = [(i, (i + 1) % count) for i in range(count)]
    upward = [(i, i + 1) for i in range(count - 1) if (i + 1) % seq_blocks]
    downward = [(b, a) for a, b in upward]
    ring = lambda a: lax.ppermute(a, "expert", around)
    later = lambda a: lax.ppermute(a, "expert", upward)
    earlier = lambda a: lax.ppermute(a, "expert", downward)
    add = lambda a, b: (a.astype(F32) + b.astype(F32)).astype(BF)
    every = lambda a, axis: lax.all_gather(a, axis, axis=0, tiled=True)
    swap = lambda a: lax.ppermute(a, "dp", [(i, i ^ 1) for i in range(dp)])
    same_core = [list(range(c, dp, 2)) for c in range(2)]
    across = lambda a, bit: lax.ppermute(a, "dp", [(i, i ^ bit) for i in range(dp)])
    x_place, y_place = lax.axis_index("dp") // 2 % 2, lax.axis_index("dp") // 4
    square = dp == 8

    places = jnp.stack([x_place, y_place]).astype(jnp.int32)

    share = lambda a: lax.psum_scatter(a, "dp", scatter_dimension=1, axis_index_groups=same_core, tiled=True)

    def fold_first(keep, got, tile=None):
        return list(fold(places, keep, got, tile)) if square else [add(keep, got)]

    def send_first(parts):
        if not square:
            return parts
        one, one_sent, two, two_sent = parts
        return [one, across(one_sent, 2), two, across(two_sent, 4)]

    def halve_first(keep, got, tile=None):
        return send_first(fold_first(keep, got, tile))

    def fold_second(parts):
        if not square:
            return parts
        return [*fold_again(places[1:], *parts[:2]), *fold_again(places[:1], *parts[2:])]

    def send_second(parts):
        if not square:
            return parts
        one, one_sent, two, two_sent = parts
        return [one, across(one_sent, 4), two, across(two_sent, 2)]

    def halve_second(parts):
        return send_second(fold_second(parts))

    def halve_last(parts, axis, dtype):
        if not square:
            return share(parts[0]).astype(dtype)
        total = lambda a, b: (a.astype(F32) + b.astype(F32)).astype(dtype)
        return jnp.concatenate([total(*parts[:2]), total(*parts[2:])], axis=axis)

    beside = jnp.zeros((w_router.shape[0], LANES - EXPERTS - 2), BF)
    weights = every(
        jnp.concatenate(
            [w_query, w_out, w_key, w_value, w_router, attn_gain[:, None], moe_gain[:, None], beside], axis=1
        ),
        "dp",
    )
    behind = QD + features + 2 * KD

    members = jnp.any(routes[:, :, :, None] == jnp.arange(EXPERTS, dtype=jnp.int32), axis=2)
    before = jnp.tril(jnp.ones((BLOCK, BLOCK), F32), -1).astype(BF)
    slots = jnp.einsum("ts,mse->mte", before, members.astype(BF), preferred_element_type=F32)
    slots = jnp.where(members, slots, -1.0).astype(BF)
    dy_sent = jnp.concatenate([out_grad, slots, jnp.zeros((micros, BLOCK, LANES - EXPERTS), BF)], axis=2)

    dy_ring = [dy_sent]
    for _ in range(count - 2):
        dy_ring.append(ring(dy_ring[-1]))
    router_w = weights[:, behind:]
    gains = router_w[:, EXPERTS : EXPERTS + 2].T.astype(F32)
    gain_one, gain_two = gains[0:1], gains[1:2]
    x_whole = tokens.reshape(micros * BLOCK, features)
    normed, scale_one = norm_rows(x_whole, gain_one)
    normed = after(normed, dy_ring[-1])
    kv_own = project(normed, weights, QD + features, 2 * KD, KD, cosine, sine)
    dy_last = [ring(dy_ring[-1][0])]
    kv_own = list(kv_own)
    kv_own[0], dy_last[0] = together(kv_own[0], dy_last[0])
    kv_one = [kv_own[0]]
    for _ in range(seq_blocks - 1):
        kv_one.append(later(kv_one[-1]))
    dy_last.append(ring(after(dy_ring[-1][1], kv_one[-1])))

    kv_two = [after(kv_own[1], kv_one[-1])]
    kv_two.append(later(kv_two[-1]))
    queries = list(project(after(normed, kv_one[-1]), weights, 0, QD, QD, cosine, sine))
    kv_two[-1], queries[0] = together(kv_two[-1], queries[0])
    kv_two.append(later(kv_two[-1]))
    o_one, ob_one, lse_one = attend(place, queries[0], kv_one)
    kv_two[-1], dy_last[1], ob_one = together(kv_two[-1], dy_last[1], ob_one)
    dy_ring.append(dy_last)
    kv_two.append(later(kv_two[-1]))
    go_out = lambda m, ob: outward(ob, weights, tokens[m], gain_two, router_w, routes[m])
    mids = [list(go_out(0, ob_one))]
    sent = [every(mids[0][1], "expert")]
    kv_two[-1], mids[0][1] = together(kv_two[-1], mids[0][1])
    while len(kv_two) < seq_blocks:
        kv_two.append(later(kv_two[-1]))
    def in_order(m):
        whole = jnp.zeros((count * BLOCK, features + LANES), BF)
        for step, block in enumerate(dy_ring):
            whole = lax.dynamic_update_slice_in_dim(whole, block[m], (rank - step) % count * BLOCK, 0)
        return whole

    slot_rows, dy_slots = [], []
    for m in range(micros):
        dy_all = in_order(m)
        table = lax.dynamic_slice_in_dim(dy_all, features + rank * exp_dev, exp_dev, 1)
        slot_rows.append(table.astype(F32).T)
        dy_slots.append(dispatch(slot_rows[m], dy_all, features))
    kv_two[-1], *dy_slots = together(kv_two[-1], *dy_slots)
    o_two, ob_two, lse_two = attend(place, queries[1], kv_two)
    mids.append(list(go_out(1, ob_two)))
    sent.append(every(mids[1][1], "expert"))
    kvs = (kv_one, kv_two)
    heads = ((o_one, ob_one, lse_one), (o_two, ob_two, lse_two))

    own = rank.astype(jnp.int32)[None]
    experts = lambda m, x: expert_pass(own, x, dy_slots[m], w_gate, w_up, w_down)
    ring_block = lambda sums, j: lax.dynamic_slice_in_dim(sums, (rank - 1 - j) % count * BLOCK, BLOCK, 0)
    x_one = dispatch(slot_rows[0], sent[0], features + LANES)
    ys_one, dx_one, gdy_one, act_one, dg_one, du_one = experts(0, x_one)
    dx_one = combine(slot_rows[0], dx_one)
    dx_home = [lax.psum_scatter(dx_one, "expert", scatter_dimension=0, tiled=True)]
    mixture_one = combine(slot_rows[0], after(ys_one, dx_one))
    sent[1], mixture_one = together(sent[1], mixture_one)
    x_two = dispatch(slot_rows[1], sent[1], features + LANES)
    ys_two, dx_two, gdy_two, act_two, dg_two, du_two = experts(1, x_two)

    hidden = w_down.shape[1]
    (new_down,) = weight_pass(core, None, hidden, (act_one, act_two), (gdy_one, gdy_two))
    new_down, dx_home[0] = together(new_down, dx_home[0])
    down_grad = lax.psum_scatter(new_down, "dp", scatter_dimension=1, tiled=True)
    dx_two = combine(slot_rows[1], after(dx_two, new_down))
    dx_held = ring(ring_block(dx_two, 0))
    ups = weight_pass(
        core, features // dp, features, (x_one, x_two), (after(dg_one, dx_two), dg_two), (du_one, du_two)
    )
    dx_held, *ups = together(dx_held, *ups)
    for step in range(1, count - 2):
        dx_held = ring(add(dx_held, ring_block(dx_two, step)))
    got_gate, got_up = swap(ups[1]), swap(ups[3])

    def back_home(m, dx):
        mid, _, scale_two, gates = mids[m]
        return home_back(dx, gates, mid, scale_two, out_grad[m], router_w, gain_two, weights)

    def back_heads(m, dob):
        o, _, lse = heads[m]
        dq, *pieces = attend_back(place, queries[m], dob, o, lse, cosine, sine, kvs[m])
        return dq, pieces[::-1]

    first = list(back_home(0, after(dx_home[0], ups[0])))
    dq_one, far_one = back_heads(0, first[2])
    dx_held, got_gate, got_up, dq_one = together(dx_held, got_gate, got_up, dq_one)
    dx_held = ring(add(dx_held, ring_block(dx_two, count - 2)))
    up_half = add(ups[2], got_up)
    dx_held, up_half = together(dx_held, up_half)
    up_grad = share(up_half)
    dx_home.append(add(dx_held, ring_block(dx_two, count - 1)))
    held = ring(ring_block(after(mixture_one, dx_held), 0))
    back_one = earlier(far_one[0])
    second = list(back_home(1, after(dx_home[1], up_half, dq_one)))
    back_one, second[2] = together(back_one, second[2])
    back_one = earlier(add(back_one, far_one[1]))
    dq_two, far_two = back_heads(1, second[2])
    back_one, dq_two, far_two[0], held, down_grad = together(back_one, dq_two, far_two[0], held, down_grad)
    for piece in far_one[2:-1]:
        back_one = earlier(add(back_one, piece))
    back_two = earlier(far_two[0])
    gate_parts = fold_first(after(ups[0], dq_two), got_gate)
    back_two, back_one, *gate_parts = together(back_two, back_one, *gate_parts)
    gate_sums = send_first(gate_parts)
    back_one = add(back_one, far_one[-1])
    back_two = earlier(add(back_two, far_two[1]))

    def back_last(m, dq, dkv, dmid):
        return last_back(
            dq, dkv, cosine, sine, weights, weights, tokens[m], scale_one[m * BLOCK : (m + 1) * BLOCK], gain_one, dmid
        )

    grad_x_one, dkv_one, dgain_one = back_last(0, dq_one, back_one, first[0])
    back_two, dkv_one = together(back_two, dkv_one)
    for piece in far_two[2:-1]:
        back_two = earlier(add(back_two, piece))
    mixture_two = combine(slot_rows[1], after(ys_two, dkv_one))
    back_two, mixture_two = together(back_two, mixture_two)
    back_two = add(back_two, far_two[-1])
    grad_x_two, dkv_two, dgain_two = back_last(1, dq_two, back_two, second[0])
    held = ring(add(after(held, mixture_two), ring_block(mixture_one, 1)))

    gain_rows = jnp.concatenate([dgain_one + dgain_two, first[4] + second[4]], axis=0)
    gain_columns = jnp.pad(gain_rows.T, ((0, 0), (EXPERTS, LANES - EXPERTS - 2)))
    keep, send = dense_grads(
        core, features // dp, [normed] * micros, [dq_one, dq_two], [dkv_one, dkv_two], [k[1] for k in mids],
        [first[3], second[3]], [h[1] for h in heads], [first[1], second[1]], gain_columns,
    )
    held, keep, send, *gate_sums = together(held, keep, send, *gate_sums)
    for step in range(2, count - 1):
        held = ring(add(held, ring_block(mixture_one, step)))
    got = swap(send)
    got, up_grad = together(got, up_grad)
    dense_sums = halve_first(keep[None], got[None], 3 * LANES)
    held = together(held, dense_sums[0])[0]
    mixtures = [add(held, ring_block(mixture_one, count - 1))]
    held = ring(ring_block(mixture_two, 0))
    held = ring(add(held, ring_block(mixture_two, 1)))
    gate_parts = fold_second([after(a, dense_sums[0]) for a in gate_sums])
    each = len(gate_parts)
    held, *rest = together(held, *gate_parts, *dense_sums)
    gate_parts, dense_sums = rest[:each], halve_second(rest[each:])
    held = after(held, *dense_sums[::2])
    for step in range(2, count - 1):
        held = ring(add(held, ring_block(mixture_two, step)))
    held, *dense_sums = together(held, *dense_sums)
    mixtures.append(add(held, ring_block(mixture_two, count - 1)))
    dense_sum = halve_last(dense_sums, 2, BF)[0]
    gate_sums = send_second(together(*gate_parts, dense_sum)[:-1])
    gate_grad = halve_last(gate_sums, 0, F32)
    up_grad, down_grad = up_grad.astype(F32), down_grad.astype(F32)
    dense = split_dense(lax.psum(dense_sum, "expert"))
    query, key, value, router, gain_columns, out = dense
    mixed = [(mids[m][0] + mixtures[m].astype(F32)).astype(BF) for m in range(micros)]
    return (
        jnp.stack(mixed),
        jnp.stack([grad_x_one, grad_x_two]),
        gain_columns[:, 0],
        query,
        key,
        value,
        out,
        gain_columns[:, 1],
        router,
        gate_grad,
        up_grad,
        down_grad,
    )


def solution(mesh):
    rows = P(None, ("dp", "expert"), None)
    return jax.shard_map(
        local,
        mesh=mesh,
        in_specs=(
            rows, rows, rows, P("dp"), P("dp", None), P("dp", None), P("dp", None), P("dp", None),
            P("dp"), P("dp", None),
            P("expert", None, None), P("expert", None, None), P("expert", None, None),
        ),
        out_specs=(
            rows, rows, P("dp"), P("dp", None), P("dp", None), P("dp", None), P("dp", None),
            P("dp"), P("dp", None),
            P("expert", "dp", None), P("expert", "dp", None), P("expert", "dp", None),
        ),
        check_vma=False,
    )
```
